32 devices in a mesh: section: 2 (over x), dp: 16 (over z, y, core).
Axes of the slice: x: 2, y: 2, z: 4, core: 2. Of those that a mesh axis runs over, the one named last changes fastest.
Arguments:
- inputs: bfloat16 [2, 4096, 1024], P(None, 'dp'), may hold values from -6 to 6
- teacher: float32 [2, 4096, 1024], P(None, 'dp'), may hold values from -6 to 6
- lengths: int32 [2, 16, 4], P(None, 'dp'), may hold values from 1 to 128, 256 in all within a row
- attn_query: bfloat16 [2, 1024, 2048], P('section', 'dp'), may hold values from -0.1875 to 0.1875
- attn_key: bfloat16 [2, 1024, 1024], P('section', 'dp'), may hold values from -0.1875 to 0.1875
- attn_value: bfloat16 [2, 1024, 1024], P('section', 'dp'), may hold values from -0.1875 to 0.1875
- attn_out: bfloat16 [2, 2048, 1024], P('section', 'dp'), may hold values from -0.75 to 0.75
- ffn_gate: bfloat16 [2, 1024, 3072], P('section', 'dp'), may hold values from -0.1875 to 0.1875
- ffn_up: bfloat16 [2, 1024, 3072], P('section', 'dp'), may hold values from -0.1875 to 0.1875
- ffn_down: bfloat16 [2, 3072, 1024], P('section', 'dp'), may hold values from -0.109375 to 0.109375
- norm_attn: bfloat16 [2, 1024], P('section', 'dp'), may hold values from 0.5 to 1.5
- norm_ffn: bfloat16 [2, 1024], P('section', 'dp'), may hold values from 0.5 to 1.5
- norm_query: bfloat16 [2, 128], P('section', 'dp'), may hold values from 0.5 to 1.5
- norm_key: bfloat16 [2, 128], P('section', 'dp'), may hold values from 0.5 to 1.5
Outputs:
- output: bfloat16 [2, 4096, 1024], P('section', 'dp')
- loss: float32 [], replicated
- input_grad: bfloat16 [2, 4096, 1024], P('section', 'dp')
- grad_query: float32 [2, 1024, 2048], P('section', 'dp')
- grad_key: float32 [2, 1024, 1024], P('section', 'dp')
- grad_value: float32 [2, 1024, 1024], P('section', 'dp')
- grad_out: float32 [2, 2048, 1024], P('section', 'dp')
- grad_gate: float32 [2, 1024, 3072], P('section', 'dp')
- grad_up: float32 [2, 1024, 3072], P('section', 'dp')
- grad_down: float32 [2, 3072, 1024], P('section', 'dp')
- grad_norm_attn: float32 [2, 1024], P('section', 'dp')
- grad_norm_ffn: float32 [2, 1024], P('section', 'dp')
- grad_norm_query: float32 [2, 128], P('section', 'dp')
- grad_norm_key: float32 [2, 128], P('section', 'dp')
The draws below stay inside these ranges and needn't reach their ends.
Inputs may be any that keep to these rules, and one draw needn't show every extreme that they name: In each micro-batch the 4 lengths of one index of dp sum to 256, and the largest of them is 128.
All inputs are finite; a program needn't handle non-finite values.
Results may differ from the reference program's by a relative error of at most 0.017.
Values may be sent and summed in bfloat16 or wider, within the bound.
No kernel may reach another device: no remote copies, remote signals or barrier semaphores. Data moves between devices by JAX's collectives and lax.ppermute only.
A program may use at most 256 MiB of HBM per device.

```python
import math
import jax
import jax.numpy as jnp
import numpy as np
from jax import lax

D = 1024
QUERY_HEADS = 16
KEY_VALUE_HEADS = 8
HEAD_SIZE = 128
FF = 3072
TOKENS_PER_SHARD = 256
SEQ_DEV = 4
MB = 2
QW = 2048
KW = 1024
TOKENS = 4096
SEQ_MOST = 128
N_SECTION = 2
N_DP = 16


def block_scale(own_key, shape, pieces, least, high):
    loudness, own = 1.0, jax.random.fold_in(own_key, 6)
    for position, shards_of in pieces:
        heights = jnp.exp(jax.random.uniform(jax.random.fold_in(own, position), (shards_of,), jnp.float32, least / len(pieces), high / len(pieces)))
        loudness = loudness * jnp.repeat(heights, shape[position] // shards_of).reshape([-1 if axis == position else 1 for axis in range(len(shape))])
    return loudness


def length_profile(amount, total, reach, skew):
    loads = [(1 << 20) // math.isqrt(standing ** skew) + 1 for standing in range(2, amount + 1)]
    spare, counts = total - reach - (amount - 1), [1] * (amount - 1)
    while spare > 0:
        movable = [i for i in range(amount - 1) if counts[i] < reach]
        pool, budget = sum([loads[i] for i in movable]), spare
        for i in movable:
            addition = min(reach - counts[i], max(1, budget * loads[i] // pool), spare)
            counts[i] = counts[i] + addition
            spare = spare - addition
    return np.array([reach] + counts)


def ragged(key, count, total, reach, lean):
    if count == 2:
        one = jax.random.randint(key, (), max(1, total - reach), min(reach, total - 1) + 1)
        return jnp.stack([one, total - one])
    sizes = jnp.asarray(length_profile(count, total, reach, lean), jnp.int32)
    pairs = (count - 1) // 2
    giver, receiver = sizes[1:1 + 2 * pairs:2], sizes[2:2 + 2 * pairs:2]
    slack = jnp.minimum(giver - 1, reach - receiver)
    moved = jax.random.randint(jax.random.fold_in(key, 1), (pairs,), 0, 1 << 20) % (slack + 1)
    sizes = sizes.at[1:1 + 2 * pairs:2].set(giver - moved).at[2:2 + 2 * pairs:2].set(receiver + moved)
    return sizes[jax.random.permutation(jax.random.fold_in(key, 2), count)]


def noise(key, extent, scale, bound, split=(), kind=jnp.bfloat16):
    gain = block_scale(key, extent, split, -0.22, 0.18) if split else 1.0
    result = jax.random.normal(key, extent, jnp.float32) * scale * gain
    return jnp.minimum(jnp.maximum(result, -bound), bound).astype(kind)


def setup_inputs(seed: int = 0) -> dict:
    key_list = jax.random.split(jax.random.key(seed), 15)
    return {
        "inputs": noise(key_list[0], (MB, TOKENS, D), 1.0, 6.0, ((1, 16),)),
        "teacher": noise(key_list[1], (MB, TOKENS, D), 1.0, 6.0, ((1, 16),), jnp.float32),
        "lengths": jax.vmap(lambda own: ragged(own, SEQ_DEV, TOKENS_PER_SHARD, SEQ_MOST, 2))(jax.random.split(key_list[2], MB * N_DP)).reshape((MB, N_DP, SEQ_DEV)).astype(jnp.int32),
        "attn_query": noise(key_list[3], (N_SECTION, D, QW), D ** -0.5, 0.1875, ((0, 2), (1, 16))),
        "attn_key": noise(key_list[4], (N_SECTION, D, KW), D ** -0.5, 0.1875, ((0, 2), (1, 16))),
        "attn_value": noise(key_list[5], (N_SECTION, D, KW), D ** -0.5, 0.1875, ((0, 2), (1, 16))),
        "attn_out": noise(key_list[6], (N_SECTION, QW, D), (QW // 32) ** -0.5, 0.75, ((0, 2), (1, 16))),
        "ffn_gate": noise(key_list[7], (N_SECTION, D, FF), D ** -0.5, 0.1875, ((0, 2), (1, 16))),
        "ffn_up": noise(key_list[8], (N_SECTION, D, FF), D ** -0.5, 0.1875, ((0, 2), (1, 16))),
        "ffn_down": noise(key_list[9], (N_SECTION, FF, D), FF ** -0.5, 0.109375, ((0, 2), (1, 16))),
        "norm_attn": jnp.clip(1.0 + 0.1 * jax.random.normal(key_list[10], (N_SECTION, D), jnp.float32), 0.5, 1.5).astype(jnp.bfloat16),
        "norm_ffn": jnp.clip(1.0 + 0.1 * jax.random.normal(key_list[11], (N_SECTION, D), jnp.float32), 0.5, 1.5).astype(jnp.bfloat16),
        "norm_query": jnp.clip(1.0 + 0.1 * jax.random.normal(key_list[12], (N_SECTION, HEAD_SIZE), jnp.float32), 0.5, 1.5).astype(jnp.bfloat16),
        "norm_key": jnp.clip(1.0 + 0.1 * jax.random.normal(key_list[13], (N_SECTION, HEAD_SIZE), jnp.float32), 0.5, 1.5).astype(jnp.bfloat16),
    }


EPS = 1e-06
THETA = 1000000.0
NEGATIVE = -1e+30
HIGH = lax.Precision.HIGHEST

@jax.custom_vjp
def reduced_precision(v):
    return lax.optimization_barrier(v.astype(jnp.bfloat16)).astype(jnp.float32)

@jax.custom_vjp
def reduced_backward(v):
    return v

def low_keep(v):
    return (reduced_precision(v), None)

def low_pass(kept, grad):
    return (grad,)

def back_keep(v):
    return (v, None)

def back_low(kept, grad):
    return (reduced_precision(grad),)
reduced_precision.defvjp(low_keep, low_pass)
reduced_backward.defvjp(back_keep, back_low)

def layout(lengths_row):
    ends = jnp.cumsum(lengths_row).astype(jnp.int32)
    places = jnp.arange(TOKENS_PER_SHARD, dtype=jnp.int32)
    passed = (ends[None, :] <= places[:, None]).astype(jnp.int32)
    segment_index = lax.optimization_barrier(jnp.sum(passed, axis=1)).astype(jnp.int32)
    start = lax.optimization_barrier(jnp.sum(passed * lengths_row[None, :], axis=1)).astype(jnp.int32)
    return (segment_index, (places - start).astype(jnp.int32))

def rotary_tables(place):
    half = HEAD_SIZE // 2
    freqs = THETA ** (-(jnp.arange(half, dtype=jnp.float32) * 2.0 / HEAD_SIZE))
    angles = place.astype(jnp.float32)[:, None] * freqs[None, :]
    return (jnp.cos(angles), jnp.sin(angles))

def projection_step(values, weight):
    return jnp.dot(values, weight, precision=HIGH, preferred_element_type=jnp.float32)

def rms_scale(values):
    return values * lax.rsqrt(lax.optimization_barrier(jnp.mean(values * values, axis=-1, keepdims=True)) + EPS)

def rotate(values, cosine_table, sine_table):
    half = values.shape[-1] // 2
    first = values[..., :half]
    second = values[..., half:]
    turn_cos = cosine_table[:, None, :]
    turn_sin = sine_table[:, None, :]
    return jnp.concatenate([first * turn_cos - second * turn_sin, second * turn_cos + first * turn_sin], axis=-1)

def attention_block(parts):
    query_rows, key, value_rows, segment_index = parts
    group_count = QUERY_HEADS // KEY_VALUE_HEADS
    grouped_heads = query_rows.reshape(TOKENS_PER_SHARD, KEY_VALUE_HEADS, group_count, HEAD_SIZE)
    scores = reduced_backward(jnp.einsum('qhgd,khd->hgqk', grouped_heads, key, precision=HIGH) * HEAD_SIZE ** (-0.5))
    places = jnp.arange(TOKENS_PER_SHARD, dtype=jnp.int32)
    allowed = (segment_index[:, None] == segment_index[None, :]) & (places[:, None] >= places[None, :])
    weights = reduced_precision(jax.nn.softmax(jnp.where(allowed[None, None], scores, NEGATIVE), axis=-1))
    mixed_output = jnp.einsum('hgqk,khd->qhgd', weights, value_rows, precision=HIGH)
    return mixed_output.reshape(TOKENS_PER_SHARD, QUERY_HEADS * HEAD_SIZE)

def layer(hidden, params, cosine_table, sine_table, segment_index):
    w_query, key_weight, value_weight, w_out, w_gate, w_up, w_down, gain_attn, gain_ffn, gain_query, key_norm_scale = params
    token_rows = hidden.shape[0]
    normalized_rows = reduced_precision(rms_scale(hidden) * gain_attn)
    query_rows = reduced_backward(projection_step(normalized_rows, w_query)).reshape(token_rows, QUERY_HEADS, HEAD_SIZE)
    key = reduced_backward(projection_step(normalized_rows, key_weight)).reshape(token_rows, KEY_VALUE_HEADS, HEAD_SIZE)
    value_rows = reduced_precision(reduced_backward(projection_step(normalized_rows, value_weight))).reshape(token_rows, KEY_VALUE_HEADS, HEAD_SIZE)
    query_rows = reduced_precision(rotate(rms_scale(query_rows) * gain_query, cosine_table, sine_table))
    key = reduced_precision(rotate(rms_scale(key) * key_norm_scale, cosine_table, sine_table))
    block_list = token_rows // TOKENS_PER_SHARD
    mixed_output = lax.map(jax.checkpoint(attention_block), (query_rows.reshape(block_list, TOKENS_PER_SHARD, QUERY_HEADS, HEAD_SIZE), key.reshape(block_list, TOKENS_PER_SHARD, KEY_VALUE_HEADS, HEAD_SIZE), value_rows.reshape(block_list, TOKENS_PER_SHARD, KEY_VALUE_HEADS, HEAD_SIZE), segment_index.reshape(block_list, TOKENS_PER_SHARD)))
    mixed_output = reduced_precision(reduced_backward(mixed_output.reshape(token_rows, QUERY_HEADS * HEAD_SIZE)))
    middle = hidden + reduced_backward(projection_step(mixed_output, w_out))
    normed_ffn = reduced_precision(rms_scale(middle) * gain_ffn)
    gate = reduced_backward(projection_step(normed_ffn, w_gate))
    up_part = reduced_backward(projection_step(normed_ffn, w_up))
    inner = reduced_precision(jax.nn.silu(gate) * up_part)
    return middle + reduced_backward(projection_step(inner, w_down))

def reference(inputs, teacher, lengths, attn_query, attn_key, attn_value, attn_out, ffn_gate, ffn_up, ffn_down, norm_attn, norm_ffn, norm_query, norm_key):
    token_rows = MB * TOKENS
    segment_index, place = jax.vmap(layout)(lengths.reshape(MB * N_DP, SEQ_DEV))
    segment_index = segment_index.reshape(token_rows)
    place = place.reshape(token_rows)
    cosine_table, sine_table = rotary_tables(place)
    keep = (segment_index < SEQ_DEV - 1).astype(jnp.float32)
    target = teacher.reshape(token_rows, D).astype(jnp.float32)
    start = inputs.reshape(token_rows, D).astype(jnp.float32)
    params = tuple((weight.astype(jnp.float32) for weight in (attn_query, attn_key, attn_value, attn_out, ffn_gate, ffn_up, ffn_down, norm_attn, norm_ffn, norm_query, norm_key)))

    def forward(first, *weights):
        hidden = first
        for section_index in range(N_SECTION):
            hidden = reduced_precision(layer(hidden, [weight[section_index] for weight in weights], cosine_table, sine_table, segment_index))
            if section_index + 1 < N_SECTION:
                hidden = reduced_backward(hidden)
        diff = hidden - target
        return (0.5 * jnp.sum(keep[:, None] * diff * diff), hidden)
    half, pull, final = jax.vjp(forward, start, *params, has_aux=True)
    grads = pull(jnp.ones_like(half))
    total = jnp.sum(keep)
    loss = 2.0 * half / (total * D)
    output = final.astype(jnp.bfloat16).reshape(MB, TOKENS, D)
    input_grad = grads[0].astype(jnp.bfloat16).reshape(MB, TOKENS, D)
    return (output, loss, input_grad, grads[1], grads[2], grads[3], grads[4], grads[5], grads[6], grads[7], grads[8], grads[9], grads[10], grads[11])
```

```python
import jax
import jax.numpy as jnp
from jax import lax
from jax.sharding import PartitionSpec as P

QUERY_HEADS = 16
KEY_VALUE_HEADS = 8
HEAD_SIZE = 128
TOKENS_PER_SHARD = 256


EPS = 1e-06
THETA = 1000000.0
NEGATIVE = -1e30
CONTRACT_ROWS = (((0,), (0,)), ((), ()))
CONTRACT_COLS = (((1,), (1,)), ((), ()))


def one_way(value, source):
    return lax.ppermute(value, "section", [(source, 1 - source)])


def chip_at(place, chips):
    place = lax.rem(place + 2 * chips, chips)
    return jnp.where(place < chips // 2, 2 * place, 2 * (chips - 1 - place) + 1)


def ring_place(chip, chips):
    return jnp.where(chip % 2 == 0, chip // 2, chips - 1 - chip // 2)


def ring_routes(devices):
    chips = devices // 2
    order = list(range(0, chips, 2)) + list(range(chips - 1, 0, -2))
    right, left = [], []
    for place in range(chips):
        here, there = order[place], order[(place + 1) % chips]
        for core in range(2):
            right.append((2 * here + core, 2 * there + core))
            left.append((2 * there + core, 2 * here + core))
    return right, left, [(device, device ^ 1) for device in range(devices)]


def gather_ring(shard, after=None):
    devices = lax.axis_size("dp")
    chips = devices // 2
    right, left, pair = ring_routes(devices)
    index = lax.axis_index("dp")
    core = index % 2
    place = ring_place(index // 2, chips)
    rows = shard.shape[0]
    half = rows // 2
    if after is not None:
        shard, after = lax.optimization_barrier((shard, after))
    whole = jnp.zeros((devices,) + shard.shape, shard.dtype)

    def put(whole, piece, owner, offset):
        return lax.dynamic_update_slice(whole, piece[None], (owner, offset, 0))

    whole = put(whole, shard, index, 0)
    whole = put(whole, lax.ppermute(shard, "dp", pair), index + 1 - 2 * core, 0)
    forward, behind = shard[:half], shard[half:]
    marks = []
    for step in range(1, chips):
        forward = lax.ppermute(forward, "dp", right)
        behind = lax.ppermute(behind, "dp", left)
        marks.append((forward, behind))
        forward_pair = lax.ppermute(forward, "dp", pair)
        behind_pair = lax.ppermute(behind, "dp", pair)
        owner = 2 * chip_at(place - step, chips)
        whole = put(whole, forward, owner + core, 0)
        whole = put(whole, forward_pair, owner + 1 - core, 0)
        owner = 2 * chip_at(place + step, chips)
        whole = put(whole, behind, owner + core, half)
        whole = put(whole, behind_pair, owner + 1 - core, half)
    return whole, marks


def scatter_ring(parts):
    devices = lax.axis_size("dp")
    chips = devices // 2
    right, left, pair = ring_routes(devices)
    index = lax.axis_index("dp")
    core = index % 2
    place = ring_place(index // 2, chips)
    half = parts.shape[1] // 2
    grouped = parts.reshape((chips, 2) + parts.shape[1:])
    mine = lax.dynamic_index_in_dim(grouped, core, 1, keepdims=False)
    theirs = lax.dynamic_index_in_dim(grouped, 1 - core, 1, keepdims=False)
    sums = []
    for low, high in ((0, half), (half, 2 * half)):
        got = lax.ppermute(theirs[:, low:high], "dp", pair)
        sums.append(
            (mine[:, low:high].astype(jnp.float32) + got.astype(jnp.float32)).astype(jnp.bfloat16)
        )

    def own(total, where):
        return lax.dynamic_index_in_dim(total, chip_at(where, chips), 0, keepdims=False)

    forward = own(sums[0], place - 1)
    behind = own(sums[1], place + 1)
    for step in range(1, chips):
        forward = lax.ppermute(forward, "dp", right).astype(jnp.float32)
        behind = lax.ppermute(behind, "dp", left).astype(jnp.float32)
        forward = forward + own(sums[0], place - step - 1).astype(jnp.float32)
        behind = behind + own(sums[1], place + step + 1).astype(jnp.float32)
        if step + 1 < chips:
            forward = forward.astype(jnp.bfloat16)
            behind = behind.astype(jnp.bfloat16)
    return jnp.concatenate([forward, behind], axis=0)


def packed(shard, width):
    pieces = shard.shape[-1] // width
    return [shard[:, width * i : width * (i + 1)] for i in range(pieces)]


def packed_grad(grad, devices, width):
    rows, columns = grad.shape
    pieces = columns // width
    grad = grad.astype(jnp.bfloat16).reshape(devices, rows // devices, pieces, width)
    return grad.transpose(0, 2, 1, 3).reshape(devices, pieces * rows // devices, width)


def unpacked(whole, low, pieces, rows):
    devices, width = whole.shape[0], whole.shape[-1]
    part = whole[:, low : low + pieces * rows].reshape(devices, pieces, rows, width)
    return part.transpose(0, 2, 1, 3).reshape(devices * rows, pieces * width)


def beside(grad, low, pieces, rows):
    return jnp.concatenate(
        [grad[low + rows * i : low + rows * (i + 1)] for i in range(pieces)], axis=1
    )


def layout(lengths_row):
    ends = jnp.cumsum(lengths_row)
    places = jnp.arange(TOKENS_PER_SHARD, dtype=jnp.int32)
    passed = (ends[None, :] <= places[:, None]).astype(jnp.int32)
    segment_index = jnp.sum(passed, axis=1)
    start = jnp.sum(passed * lengths_row[None, :], axis=1)
    return (segment_index, places - start)


def rotary_tables(place):
    half = HEAD_SIZE // 2
    freqs = THETA ** (-(jnp.arange(half, dtype=jnp.float32) * 2.0 / HEAD_SIZE))
    angles = place.astype(jnp.float32)[:, None] * freqs[None, :]
    return (jnp.cos(angles), jnp.sin(angles))


def squared_partial_sums(values):
    factor = lax.rsqrt(jnp.mean(values * values, axis=-1, keepdims=True) + EPS)
    return (values * factor, factor)


def norm_back(grad, scaled, factor, gain):
    pulled = grad * gain
    return factor * (pulled - scaled * jnp.mean(pulled * scaled, axis=-1, keepdims=True))


def rotate(values, cosine_table, sine_table):
    half = values.shape[-1] // 2
    first = values[..., :half]
    second = values[..., half:]
    turn_cos = cosine_table[:, None, :]
    turn_sin = sine_table[:, None, :]
    return jnp.concatenate(
        [first * turn_cos - second * turn_sin, second * turn_cos + first * turn_sin], axis=-1
    )


def inverse_rotation(grad, cosine_table, sine_table):
    half = grad.shape[-1] // 2
    first = grad[..., :half]
    second = grad[..., half:]
    turn_cos = cosine_table[:, None, :]
    turn_sin = sine_table[:, None, :]
    return jnp.concatenate(
        [first * turn_cos + second * turn_sin, second * turn_cos - first * turn_sin], axis=-1
    )


def product(left, right):
    return jnp.dot(left, right, preferred_element_type=jnp.float32)


def outer_rows(left, right):
    return lax.dot_general(left, right, CONTRACT_ROWS, preferred_element_type=jnp.float32)


def times_transpose(left, right):
    return lax.dot_general(left, right, CONTRACT_COLS, preferred_element_type=jnp.float32)


def block_scores(grouped_heads, key, allowed):
    scores = jnp.einsum(
        "bqhgd,bkhd->bhgqk", grouped_heads, key, preferred_element_type=jnp.float32
    ) * HEAD_SIZE ** (-0.5)
    return jnp.where(allowed[:, None, None], scores, NEGATIVE)


def attend(grouped_heads, key, value_rows, allowed):
    scores = block_scores(grouped_heads, key, allowed)
    top = jnp.max(scores, axis=-1, keepdims=True)
    raised = jnp.exp(scores - top)
    total = jnp.sum(raised, axis=-1, keepdims=True)
    weights = (raised / total).astype(jnp.bfloat16)
    mixed_output = jnp.einsum(
        "bhgqk,bkhd->bqhgd", weights, value_rows, preferred_element_type=jnp.float32
    )
    return (mixed_output, top + jnp.log(total))


def attend_back(grouped_heads, key, value_rows, allowed, log_total, mixed_gradient):
    weights = jnp.exp(block_scores(grouped_heads, key, allowed) - log_total)
    value_gradient = jnp.einsum(
        "bhgqk,bqhgd->bkhd",
        weights.astype(jnp.bfloat16),
        mixed_gradient,
        preferred_element_type=jnp.float32,
    )
    d_weights = jnp.einsum(
        "bqhgd,bkhd->bhgqk", mixed_gradient, value_rows, preferred_element_type=jnp.float32
    )
    d_scores = (
        weights * (d_weights - jnp.sum(d_weights * weights, axis=-1, keepdims=True))
    ).astype(jnp.bfloat16)
    scale = HEAD_SIZE ** (-0.5)
    d_query = (
        jnp.einsum("bhgqk,bkhd->bqhgd", d_scores, key, preferred_element_type=jnp.float32) * scale
    )
    key_gradient = (
        jnp.einsum("bhgqk,bqhgd->bkhd", d_scores, grouped_heads, preferred_element_type=jnp.float32)
        * scale
    )
    return (d_query, key_gradient, value_gradient)


def attention_rows(hidden_in, tables, attn_weights, gains):
    cosine_table, sine_table, allowed = tables
    full_query, full_key, full_value, full_out = attn_weights
    gain_attn, gain_query, key_norm_scale, _ = gains
    token_rows = hidden_in.shape[0]
    group_count = QUERY_HEADS // KEY_VALUE_HEADS
    block_list = token_rows // TOKENS_PER_SHARD
    hidden = hidden_in.astype(jnp.float32)
    scaled, factor = squared_partial_sums(hidden)
    normalized_rows = (scaled * gain_attn).astype(jnp.bfloat16)
    query_pre = product(normalized_rows, full_query)
    unrotated_key = product(normalized_rows, full_key)
    reduced_value = product(normalized_rows, full_value).astype(jnp.bfloat16)
    reduced_query = rotate(
        squared_partial_sums(query_pre.reshape(token_rows, QUERY_HEADS, HEAD_SIZE))[0] * gain_query,
        cosine_table,
        sine_table,
    ).astype(jnp.bfloat16)
    reduced_key = rotate(
        squared_partial_sums(unrotated_key.reshape(token_rows, KEY_VALUE_HEADS, HEAD_SIZE))[0]
        * key_norm_scale,
        cosine_table,
        sine_table,
    ).astype(jnp.bfloat16)
    reduced_query = reduced_query.reshape(
        block_list, TOKENS_PER_SHARD, KEY_VALUE_HEADS, group_count, HEAD_SIZE
    )
    reduced_key = reduced_key.reshape(block_list, TOKENS_PER_SHARD, KEY_VALUE_HEADS, HEAD_SIZE)
    reduced_value = reduced_value.reshape(block_list, TOKENS_PER_SHARD, KEY_VALUE_HEADS, HEAD_SIZE)
    mixed_output, log_total = attend(reduced_query, reduced_key, reduced_value, allowed)
    mixed_low = mixed_output.reshape(token_rows, QUERY_HEADS * HEAD_SIZE).astype(jnp.bfloat16)
    middle = hidden + product(mixed_low, full_out)
    kept = (
        hidden,
        normalized_rows,
        query_pre,
        unrotated_key,
        reduced_query,
        reduced_key,
        reduced_value,
        log_total,
        mixed_low,
    )
    return middle, kept


def feed_forward(middle, ffn_weights, gains):
    full_gate, full_up, full_down = ffn_weights
    gain_ffn = gains[3]
    scaled_ffn, factor_ffn = squared_partial_sums(middle)
    normed_ffn = (scaled_ffn * gain_ffn).astype(jnp.bfloat16)
    gate = product(normed_ffn, full_gate)
    up_part = product(normed_ffn, full_up)
    inner = (jax.nn.silu(gate) * up_part).astype(jnp.bfloat16)
    result = middle + product(inner, full_down)
    return result, (middle, normed_ffn, gate, up_part, inner)


def feed_forward_back(kept, d_result, ffn_weights, gains):
    middle, normed_ffn, gate, up_part, inner = kept
    full_gate, full_up, full_down = ffn_weights
    gain_ffn = gains[3]
    d_branch = d_result.astype(jnp.bfloat16)
    d_inner = times_transpose(d_branch, full_down)
    sigma = jax.nn.sigmoid(gate)
    d_gate = (d_inner * up_part * sigma * (1.0 + gate * (1.0 - sigma))).astype(jnp.bfloat16)
    d_up = (d_inner * gate * sigma).astype(jnp.bfloat16)
    d_normed_ffn = times_transpose(d_gate, full_gate) + times_transpose(d_up, full_up)
    scaled_ffn, factor_ffn = squared_partial_sums(middle)
    grad_gain_ffn = jnp.sum(d_normed_ffn * scaled_ffn, axis=0)
    d_middle = d_result + norm_back(d_normed_ffn, scaled_ffn, factor_ffn, gain_ffn)
    return d_middle, (d_branch, d_gate, d_up, grad_gain_ffn)


def attention_back(kept, d_middle, tables, attn_weights, gains):
    (
        hidden,
        normalized_rows,
        query_pre,
        unrotated_key,
        reduced_query,
        reduced_key,
        reduced_value,
        log_total,
        mixed_low,
    ) = kept
    cosine_table, sine_table, allowed = tables
    full_query, full_key, full_value, full_out = attn_weights
    gain_attn, gain_query, key_norm_scale, _ = gains
    token_rows = hidden.shape[0]
    d_attn = d_middle.astype(jnp.bfloat16)
    mixed_gradient = times_transpose(d_attn, full_out).astype(jnp.bfloat16)
    d_query, key_gradient, value_gradient = attend_back(
        reduced_query,
        reduced_key,
        reduced_value,
        allowed,
        log_total,
        mixed_gradient.reshape(reduced_query.shape),
    )
    reduced_value_gradient = value_gradient.reshape(token_rows, KEY_VALUE_HEADS * HEAD_SIZE).astype(
        jnp.bfloat16
    )
    query_scaled, query_factor = squared_partial_sums(
        query_pre.reshape(token_rows, QUERY_HEADS, HEAD_SIZE)
    )
    d_query_normed = inverse_rotation(
        d_query.reshape(token_rows, QUERY_HEADS, HEAD_SIZE), cosine_table, sine_table
    )
    grad_gain_query = jnp.sum(d_query_normed * query_scaled, axis=(0, 1))
    d_query_pre = (
        norm_back(d_query_normed, query_scaled, query_factor, gain_query)
        .reshape(token_rows, QUERY_HEADS * HEAD_SIZE)
        .astype(jnp.bfloat16)
    )
    scaled_key_rows, key_multiplier = squared_partial_sums(
        unrotated_key.reshape(token_rows, KEY_VALUE_HEADS, HEAD_SIZE)
    )
    normed_key_gradient = inverse_rotation(
        key_gradient.reshape(token_rows, KEY_VALUE_HEADS, HEAD_SIZE), cosine_table, sine_table
    )
    grad_gain_key = jnp.sum(normed_key_gradient * scaled_key_rows, axis=(0, 1))
    d_key_pre = (
        norm_back(normed_key_gradient, scaled_key_rows, key_multiplier, key_norm_scale)
        .reshape(token_rows, KEY_VALUE_HEADS * HEAD_SIZE)
        .astype(jnp.bfloat16)
    )
    d_normed = (
        times_transpose(d_query_pre, full_query)
        + times_transpose(d_key_pre, full_key)
        + times_transpose(reduced_value_gradient, full_value)
    )
    scaled, factor = squared_partial_sums(hidden)
    grad_gain_attn = jnp.sum(d_normed * scaled, axis=0)
    d_hidden = d_middle + norm_back(d_normed, scaled, factor, gain_attn)
    return d_hidden, (
        d_attn,
        d_query_pre,
        d_key_pre,
        reduced_value_gradient,
        grad_gain_attn,
        grad_gain_query,
        grad_gain_key,
    )


def local(
    inputs,
    teacher,
    lengths,
    attn_query,
    attn_key,
    attn_value,
    attn_out,
    ffn_gate,
    ffn_up,
    ffn_down,
    norm_attn,
    norm_ffn,
    norm_query,
    norm_key,
):
    section = lax.axis_index("section")
    index = lax.axis_index("dp")
    devices = lax.axis_size("dp")
    batches, _, model = inputs.shape
    slots = lengths.shape[2]
    token_rows = batches * TOKENS_PER_SHARD
    rows = attn_query.shape[1]
    forward_rows = ffn_down.shape[1]

    gain_sizes = (norm_attn.shape[1], norm_query.shape[1], norm_key.shape[1], norm_ffn.shape[1])
    gain_shard = jnp.concatenate([norm_attn[0], norm_query[0], norm_key[0], norm_ffn[0]])
    gain_whole = lax.all_gather(gain_shard.astype(jnp.float32), "dp", axis=0)
    gains, low = [], 0
    for size in gain_sizes:
        gains.append(gain_whole[:, low : low + size].reshape(devices * size))
        low += size

    half_down = forward_rows // 2
    half_out = attn_out.shape[1] // 2
    attn_shard = jnp.concatenate(
        packed(attn_query[0], model)
        + [attn_out[0]]
        + packed(attn_key[0], model)
        + packed(attn_value[0], model),
        axis=0,
    )
    ffn_shard = jnp.concatenate(
        packed(ffn_gate[0], model) + [ffn_down[0]] + packed(ffn_up[0], model), axis=0
    )
    attn_whole, marks = gather_ring(attn_shard)
    ffn_whole, _ = gather_ring(ffn_shard, marks[-2])
    attn_weights = (
        unpacked(attn_whole, 0, 2, rows),
        unpacked(attn_whole, 4 * rows, 1, rows),
        unpacked(attn_whole, 5 * rows, 1, rows),
        unpacked(attn_whole, 2 * rows, 1, 2 * rows),
    )
    ffn_weights = (
        unpacked(ffn_whole, 0, 3, rows),
        unpacked(ffn_whole, 3 * rows + forward_rows, 3, rows),
        unpacked(ffn_whole, 3 * rows, 1, forward_rows),
    )

    segments, places = jax.vmap(layout)(lengths[:, 0, :])
    keep = (segments < slots - 1).astype(jnp.float32).reshape(token_rows)
    order = jnp.arange(TOKENS_PER_SHARD, dtype=jnp.int32)
    causal = order[:, None] >= order[None, :]
    allowed = (segments[:, :, None] == segments[:, None, :]) & causal[None]
    cosine_table, sine_table = rotary_tables(places.reshape(token_rows))
    tables = (cosine_table, sine_table, allowed)

    first = inputs.reshape(token_rows, model)
    middle, _ = attention_rows(first, tables, attn_weights, gains)
    result, _ = feed_forward(middle, ffn_weights, gains)
    carried = one_way(result.astype(jnp.bfloat16), 0)
    hidden_in = jnp.where(section == 0, first, carried)
    middle, attn_kept = attention_rows(hidden_in, tables, attn_weights, gains)
    result, ffn_kept = feed_forward(middle, ffn_weights, gains)
    result_low = result.astype(jnp.bfloat16)

    diff = result_low.astype(jnp.float32) - teacher.reshape(token_rows, model)
    cotangent = keep[:, None] * diff
    squares = jnp.sum(cotangent * diff)

    d_middle, _ = feed_forward_back(ffn_kept, cotangent, ffn_weights, gains)
    d_hidden, _ = attention_back(attn_kept, d_middle, tables, attn_weights, gains)
    incoming = one_way(d_hidden.astype(jnp.bfloat16), 1)
    d_result = jnp.where(section == 1, cotangent, incoming.astype(jnp.float32))
    d_middle, ffn_terms = feed_forward_back(ffn_kept, d_result, ffn_weights, gains)
    d_branch, d_gate, d_up, grad_gain_ffn = ffn_terms
    _, normed_ffn, _, _, inner = ffn_kept
    ffn_parts = jnp.concatenate(
        [
            packed_grad(outer_rows(normed_ffn, d_gate), devices, model),
            packed_grad(outer_rows(inner, d_branch), devices, model),
            packed_grad(outer_rows(normed_ffn, d_up), devices, model),
        ],
        axis=1,
    )
    ffn_grad = scatter_ring(ffn_parts)
    d_hidden, attn_terms = attention_back(attn_kept, d_middle, tables, attn_weights, gains)
    d_attn, d_query, d_key, d_value, grad_gain_attn, grad_gain_query, grad_gain_key = attn_terms
    normalized_rows, mixed_low = attn_kept[1], attn_kept[8]
    attn_parts = jnp.concatenate(
        [
            packed_grad(outer_rows(normalized_rows, d_query), devices, model),
            packed_grad(outer_rows(mixed_low, d_attn), devices, model),
            packed_grad(outer_rows(normalized_rows, d_key), devices, model),
            packed_grad(outer_rows(normalized_rows, d_value), devices, model),
        ],
        axis=1,
    )
    attn_grad = scatter_ring(attn_parts)

    grad_gate = beside(ffn_grad, 0, 3, rows)
    grad_down = ffn_grad[3 * rows : 3 * rows + forward_rows]
    grad_up = beside(ffn_grad, 3 * rows + forward_rows, 3, rows)
    grad_query = beside(attn_grad, 0, 2, rows)
    grad_out = attn_grad[2 * rows : 4 * rows]
    grad_key = attn_grad[4 * rows : 5 * rows]
    grad_value = attn_grad[5 * rows :]

    small = jnp.concatenate(
        [
            grad_gain_attn,
            grad_gain_query,
            grad_gain_key,
            grad_gain_ffn,
            jnp.stack([squares, jnp.sum(keep)]),
        ]
    )
    small_sum = jnp.sum(lax.all_gather(small, "dp", axis=0), axis=0)
    totals = small_sum[-2:]
    totals = jnp.where(section == 1, totals, one_way(totals, 1))
    loss = totals[0] / (totals[1] * model)
    gain_grads, low = [], 0
    for size in gain_sizes:
        gain_grads.append(lax.dynamic_slice(small_sum, (low + index * size,), (size,))[None])
        low += devices * size
    grad_gain_attn, grad_gain_query, grad_gain_key, grad_gain_ffn = gain_grads

    half = batches // 2
    finals = result_low.reshape(batches, TOKENS_PER_SHARD, model)
    grads = d_hidden.astype(jnp.bfloat16).reshape(batches, TOKENS_PER_SHARD, model)
    output = jnp.where(section == 0, one_way(finals[:half], 1), finals[half:])
    input_grad = jnp.where(section == 0, grads[:half], one_way(grads[half:], 0))
    return (
        output,
        loss,
        input_grad,
        grad_query[None],
        grad_key[None],
        grad_value[None],
        grad_out[None],
        grad_gate[None],
        grad_up[None],
        grad_down[None],
        grad_gain_attn,
        grad_gain_ffn,
        grad_gain_query,
        grad_gain_key,
    )


def solution(mesh):
    placed = (
        P(None, "dp", None),
        P(None, "dp", None),
        P(None, "dp", None),
        P("section", "dp", None),
        P("section", "dp", None),
        P("section", "dp", None),
        P("section", "dp", None),
        P("section", "dp", None),
        P("section", "dp", None),
        P("section", "dp", None),
        P("section", "dp"),
        P("section", "dp"),
        P("section", "dp"),
        P("section", "dp"),
    )
    return jax.shard_map(
        local,
        mesh=mesh,
        in_specs=placed,
        out_specs=(
            P("section", "dp", None),
            P(),
            P("section", "dp", None),
            P("section", "dp", None),
            P("section", "dp", None),
            P("section", "dp", None),
            P("section", "dp", None),
            P("section", "dp", None),
            P("section", "dp", None),
            P("section", "dp", None),
            P("section", "dp"),
            P("section", "dp"),
            P("section", "dp"),
            P("section", "dp"),
        ),
        check_vma=False,
    )
```

```python
import functools

import jax
import jax.numpy as jnp
from jax import lax
from jax.experimental import pallas as pl
from jax.experimental.pallas import tpu as pltpu
from jax.sharding import PartitionSpec as P

QUERY_HEADS = 16
KEY_VALUE_HEADS = 8
HEAD_SIZE = 128
TOKENS_PER_SHARD = 256


EPS = 1e-06
THETA = 1000000.0
NEGATIVE = -1e30
CONTRACT_ROWS = (((0,), (0,)), ((), ()))
CONTRACT_COLS = (((1,), (1,)), ((), ()))
RING_LEAD = 1


def one_way(value, source):
    return lax.ppermute(value, "section", [(source, 1 - source)])


def chip_at(place, chips):
    place = lax.rem(place + 2 * chips, chips)
    return jnp.where(place < chips // 2, 2 * place, 2 * (chips - 1 - place) + 1)


def ring_place(chip, chips):
    return jnp.where(chip % 2 == 0, chip // 2, chips - 1 - chip // 2)


def ring_routes(devices):
    chips = devices // 2
    order = list(range(0, chips, 2)) + list(range(chips - 1, 0, -2))
    right, left = [], []
    for place in range(chips):
        here, there = order[place], order[(place + 1) % chips]
        for core in range(2):
            right.append((2 * here + core, 2 * there + core))
            left.append((2 * there + core, 2 * here + core))
    return right, left, [(device, device ^ 1) for device in range(devices)]


def spread(value):
    devices = lax.axis_size("dp")
    index = lax.axis_index("dp")
    step = 1
    while step < devices:
        other = lax.ppermute(value, "dp", [(low, low ^ step) for low in range(devices)])
        later = (index // step) % 2 == 1
        value = jnp.where(
            later,
            jnp.concatenate([other, value], axis=0),
            jnp.concatenate([value, other], axis=0),
        )
        step *= 2
    return value


def summed(value):
    devices = lax.axis_size("dp")
    step = 1
    while step < devices:
        value = value + lax.ppermute(value, "dp", [(low, low ^ step) for low in range(devices)])
        step *= 2
    return value


def blank(shape, dtype):
    return pl.pallas_call(
        lambda ref: None,
        out_specs=pl.BlockSpec(memory_space=pl.ANY),
        out_shape=jax.ShapeDtypeStruct(shape, dtype),
    )()


def gather_ring(shard, after=None):
    devices = lax.axis_size("dp")
    chips = devices // 2
    right, left, pair = ring_routes(devices)
    index = lax.axis_index("dp")
    core = index % 2
    place = ring_place(index // 2, chips)
    half = shard.shape[0] // 2
    if after is not None:
        shard, after = lax.optimization_barrier((shard, after))
    whole = blank((devices,) + shard.shape, shard.dtype)

    def put(whole, piece, owner, offset):
        return lax.dynamic_update_slice(whole, piece[None], (owner, offset, 0))

    forward, behind = shard[:half], shard[half:]
    marks = []
    other = lax.ppermute(shard, "dp", pair)
    whole = put(whole, shard, index, 0)
    whole = put(whole, other, index + 1 - 2 * core, 0)
    for step in range(1, chips):
        forward = lax.ppermute(forward, "dp", right)
        behind = lax.ppermute(behind, "dp", left)
        marks.append((forward, behind))
        forward_pair = lax.ppermute(forward, "dp", pair)
        behind_pair = lax.ppermute(behind, "dp", pair)
        owner = 2 * chip_at(place - step, chips)
        whole = put(whole, forward, owner + core, 0)
        whole = put(whole, forward_pair, owner + 1 - core, 0)
        owner = 2 * chip_at(place + step, chips)
        whole = put(whole, behind, owner + core, half)
        whole = put(whole, behind_pair, owner + 1 - core, half)
    return whole, marks


def scatter_ring(forward_parts, behind_parts):
    devices = lax.axis_size("dp")
    chips = devices // 2
    right, left, pair = ring_routes(devices)
    sums = []
    for mine, theirs in (forward_parts, behind_parts):
        got = lax.ppermute(theirs, "dp", pair)
        sums.append((mine, got))

    def own(which, place):
        mine, got = sums[which]
        return mine[place].astype(jnp.float32) + got[place].astype(jnp.float32)

    forward = own(0, chips - 1)
    behind = own(1, 1)
    for step in range(1, chips):
        forward = lax.ppermute(forward.astype(jnp.bfloat16), "dp", right).astype(jnp.float32)
        behind = lax.ppermute(behind.astype(jnp.bfloat16), "dp", left).astype(jnp.float32)
        forward = forward + own(0, chips - 1 - step)
        behind = behind + own(1, (step + 1) % chips)
    return jnp.concatenate([forward, behind], axis=0)


def packed(shard, width):
    pieces = shard.shape[-1] // width
    return [shard[:, width * i : width * (i + 1)] for i in range(pieces)]


def beside(grad, low, pieces, rows):
    return jnp.concatenate(
        [grad[low + rows * i : low + rows * (i + 1)] for i in range(pieces)], axis=1
    )


def layout(lengths_row):
    ends = jnp.cumsum(lengths_row)
    places = jnp.arange(TOKENS_PER_SHARD, dtype=jnp.int32)
    passed = (ends[None, :] <= places[:, None]).astype(jnp.int32)
    segment_index = jnp.sum(passed, axis=1)
    start = jnp.sum(passed * lengths_row[None, :], axis=1)
    return (segment_index, places - start)


def rotary_tables(place):
    half = HEAD_SIZE // 2
    freqs = THETA ** (-(jnp.arange(half, dtype=jnp.float32) * 2.0 / HEAD_SIZE))
    angles = place.astype(jnp.float32)[:, None] * freqs[None, :]
    return (jnp.cos(angles), jnp.sin(angles))


def wide_call(body, grid, in_specs, out_specs, out_shape, scratch=(), flops=0, moved=0, prefetch=0, vmem=48):
    return pl.pallas_call(
        body,
        grid_spec=pltpu.PrefetchScalarGridSpec(
            num_scalar_prefetch=prefetch,
            grid=grid,
            in_specs=in_specs,
            out_specs=out_specs,
            scratch_shapes=list(scratch),
        ),
        out_shape=out_shape,
        compiler_params=pltpu.CompilerParams(vmem_limit_bytes=vmem << 20),
        cost_estimate=pl.CostEstimate(
            flops=int(flops), bytes_accessed=int(moved), transcendentals=0
        ),
    )


def whole_spec(shape):
    return pl.BlockSpec(shape, lambda *_: (0,) * len(shape))


def dot_plain(left, right):
    return jnp.dot(left, right, preferred_element_type=jnp.float32)


def dot_columns(left, right):
    return lax.dot_general(left, right, CONTRACT_COLS, preferred_element_type=jnp.float32)


def dot_rows(left, right):
    return lax.dot_general(left, right, CONTRACT_ROWS, preferred_element_type=jnp.float32)


def unit_rows(values):
    factor = lax.rsqrt(jnp.mean(values * values, axis=-1, keepdims=True) + EPS)
    return values * factor, factor


def norm_pull(grad, scaled, factor, gain):
    pulled = grad * gain
    return factor * (pulled - scaled * jnp.mean(pulled * scaled, axis=-1, keepdims=True))


def square(ref):
    value = ref[...]
    return value.reshape(value.shape[0] * value.shape[1], value.shape[2])


def qkv_kernel(h_ref, gain_ref, gain_q_ref, gain_k_ref, cos_ref, sin_ref, w_ref, xa_ref, qkv_ref, pre_ref):
    step = pl.program_id(0)

    @pl.when(step == 0)
    def _():
        scaled, _ = unit_rows(h_ref[...].astype(jnp.float32))
        xa_ref[...] = (scaled * gain_ref[...]).astype(jnp.bfloat16)

    pre = dot_plain(xa_ref[...], square(w_ref))

    @pl.when(step < 3)
    def _():
        pre_ref[...] = pre.astype(jnp.bfloat16)
        gain = jnp.where(step < 2, gain_q_ref[...], gain_k_ref[...])
        cosine, sine = cos_ref[...], sin_ref[...]
        for head in range(pre.shape[1] // HEAD_SIZE):
            part = slice(head * HEAD_SIZE, (head + 1) * HEAD_SIZE)
            scaled, _ = unit_rows(pre[:, part])
            scaled = scaled * gain
            turned = scaled * cosine + pltpu.roll(scaled, HEAD_SIZE // 2, 1) * sine
            qkv_ref[:, part] = turned.astype(jnp.bfloat16)

    @pl.when(step == 3)
    def _():
        qkv_ref[...] = pre.astype(jnp.bfloat16)


def project_qkv(hidden, gains, tables, whole):
    devices, rows, model = whole.shape
    rows = rows // 6
    tokens = hidden.shape[0]
    cosine, sine = tables[:2]
    return wide_call(
        qkv_kernel,
        (4,),
        [
            whole_spec((tokens, model)),
            whole_spec((1, model)),
            whole_spec((1, HEAD_SIZE)),
            whole_spec((1, HEAD_SIZE)),
            whole_spec((tokens, HEAD_SIZE)),
            whole_spec((tokens, HEAD_SIZE)),
            pl.BlockSpec((devices, rows, model), lambda j: (0, j + 2 * (j // 2), 0)),
        ],
        [
            whole_spec((tokens, model)),
            pl.BlockSpec((tokens, model), lambda j: (0, j)),
            pl.BlockSpec((tokens, model), lambda j: (0, jnp.minimum(j, 2))),
        ],
        [
            jax.ShapeDtypeStruct((tokens, model), jnp.bfloat16),
            jax.ShapeDtypeStruct((tokens, 4 * model), jnp.bfloat16),
            jax.ShapeDtypeStruct((tokens, 3 * model), jnp.bfloat16),
        ],
        flops=2 * tokens * model * 4 * model,
        moved=8 * model * model + 18 * tokens * model,
    )(hidden, gains[0], gains[1], gains[2], cosine, sine, whole)


HEADS_PER_STEP = 4


def attend_kernel(q_ref, k_ref, v_ref, row_ref, column_ref, o_ref):
    tokens = k_ref.shape[0]
    causal = lax.broadcasted_iota(jnp.int32, (tokens, tokens), 0) >= lax.broadcasted_iota(
        jnp.int32, (tokens, tokens), 1
    )
    allowed = (row_ref[...] == column_ref[0]) & causal
    for head in range(2 * HEADS_PER_STEP):
        part = slice(head * HEAD_SIZE, (head + 1) * HEAD_SIZE)
        shared = slice(head // 2 * HEAD_SIZE, (head // 2 + 1) * HEAD_SIZE)
        scores = dot_columns(q_ref[:, part], k_ref[:, shared]) * HEAD_SIZE ** (-0.5)
        scores = jnp.where(allowed, scores, NEGATIVE)
        raised = jnp.exp(scores - jnp.max(scores, axis=-1, keepdims=True))
        weights = raised * (1.0 / jnp.sum(raised, axis=-1, keepdims=True))
        mixed = dot_plain(weights.astype(jnp.bfloat16), v_ref[:, shared])
        o_ref[:, part] = mixed.astype(jnp.bfloat16)


def attend(qkv, tables):
    row_segments, column_segments = tables[2:]
    tokens = qkv.shape[0]
    blocks = tokens // TOKENS_PER_SHARD
    groups = KEY_VALUE_HEADS // HEADS_PER_STEP
    wide = HEADS_PER_STEP * HEAD_SIZE
    return wide_call(
        attend_kernel,
        (blocks, groups),
        [
            pl.BlockSpec((TOKENS_PER_SHARD, 2 * wide), lambda b, g: (b, g)),
            pl.BlockSpec((TOKENS_PER_SHARD, wide), lambda b, g: (b, 2 * groups + g)),
            pl.BlockSpec((TOKENS_PER_SHARD, wide), lambda b, g: (b, 3 * groups + g)),
            pl.BlockSpec((TOKENS_PER_SHARD, 1), lambda b, g: (b, 0)),
            pl.BlockSpec((1, 1, TOKENS_PER_SHARD), lambda b, g: (b, 0, 0)),
        ],
        pl.BlockSpec((TOKENS_PER_SHARD, 2 * wide), lambda b, g: (b, g)),
        jax.ShapeDtypeStruct((tokens, QUERY_HEADS * HEAD_SIZE), jnp.bfloat16),
        flops=16 * tokens * TOKENS_PER_SHARD * QUERY_HEADS * HEAD_SIZE,
        moved=12 * tokens * 1024,
    )(qkv, qkv, qkv, row_segments, column_segments)


def out_kernel(o_ref, w_ref, h_ref, gain_ref, hm_ref, xf_ref, total):
    step = pl.program_id(0)
    term = dot_plain(o_ref[...], square(w_ref))

    @pl.when(step == 0)
    def _():
        total[...] = h_ref[...].astype(jnp.float32) + term

    @pl.when(step > 0)
    def _():
        total[...] += term

    @pl.when(step == pl.num_programs(0) - 1)
    def _():
        middle = total[...]
        hm_ref[...] = middle
        scaled, _ = unit_rows(middle)
        xf_ref[...] = (scaled * gain_ref[...]).astype(jnp.bfloat16)


def project_out(mixed, whole, hidden, gains):
    devices, rows, model = whole.shape
    rows = rows // 6
    tokens, wide = mixed.shape
    return wide_call(
        out_kernel,
        (4,),
        [
            pl.BlockSpec((tokens, wide // 4), lambda c: (0, c)),
            pl.BlockSpec((devices // 4, 2 * rows, model), lambda c: (c, 1, 0)),
            whole_spec((tokens, model)),
            whole_spec((1, model)),
        ],
        [whole_spec((tokens, model)), whole_spec((tokens, model))],
        [
            jax.ShapeDtypeStruct((tokens, model), jnp.float32),
            jax.ShapeDtypeStruct((tokens, model), jnp.bfloat16),
        ],
        scratch=[pltpu.VMEM((tokens, model), jnp.float32)],
        flops=2 * tokens * wide * model,
        moved=2 * wide * model + 12 * tokens * model,
    )(mixed, whole, hidden, gains[3])


def ffn_kernel(chunk, xf_ref, hm_ref, gate_ref, up_ref, down_ref, *rest):
    outs, (inner, total) = rest[:-2], rest[-2:]
    step = pl.program_id(0)
    model = xf_ref.shape[1]

    @pl.when(step < 3)
    def _():
        xf = xf_ref[...]
        gate = dot_plain(xf, square(gate_ref))
        up = dot_plain(xf, square(up_ref))
        mixed = (gate * jax.nn.sigmoid(gate) * up).astype(jnp.bfloat16)
        inner[:, pl.ds(pl.multiple_of(step * model, model), model)] = mixed
        if len(outs) > 1:
            outs[1][...] = gate.astype(jnp.bfloat16)
            outs[2][...] = up.astype(jnp.bfloat16)
            outs[3][...] = mixed

    @pl.when(step >= 3)
    def _():
        place = pl.multiple_of((step - 3) * chunk, 128)
        term = dot_plain(inner[:, pl.ds(place, chunk)], square(down_ref))

        @pl.when(step == 3)
        def _():
            total[...] = hm_ref[...] + term

        @pl.when(step > 3)
        def _():
            total[...] += term

        @pl.when(step == pl.num_programs(0) - 1)
        def _():
            outs[0][...] = total[...].astype(jnp.bfloat16)


def feed_forward(normed, middle, whole, keep):
    devices, rows, model = whole.shape
    rows = rows // 9
    tokens = normed.shape[0]
    width = 3 * model
    chunk = width // 4
    column = pl.BlockSpec((tokens, model), lambda i: (0, jnp.minimum(i, 2)))
    shapes = [jax.ShapeDtypeStruct((tokens, model), jnp.bfloat16)]
    specs = [whole_spec((tokens, model))]
    if keep:
        shapes += [jax.ShapeDtypeStruct((tokens, width), jnp.bfloat16)] * 3
        specs += [column] * 3
    return wide_call(
        functools.partial(ffn_kernel, chunk),
        (7,),
        [
            whole_spec((tokens, model)),
            whole_spec((tokens, model)),
            pl.BlockSpec((devices, rows, model), lambda i: (0, jnp.minimum(i, 2), 0)),
            pl.BlockSpec((devices, rows, model), lambda i: (0, 6 + jnp.minimum(i, 2), 0)),
            pl.BlockSpec(
                (devices // 4, 3 * rows, model), lambda i: (jnp.maximum(i - 3, 0), 1, 0)
            ),
        ],
        specs,
        shapes,
        scratch=[
            pltpu.VMEM((tokens, width), jnp.bfloat16),
            pltpu.VMEM((tokens, model), jnp.float32),
        ],
        flops=6 * tokens * width * model,
        moved=6 * width * model + 8 * tokens * model + (6 * tokens * width if keep else 0),
    )(normed, middle, whole, whole, whole)


def ffn_back_kernel(
    chunk, dy_ref, hm_ref, gain_ref, g_ref, u_ref, gate_ref, up_ref, down_ref,
    dh_ref, low_ref, dg_ref, du_ref, dgain_ref, dg_all, du_all, low_dy, total,
):
    step = pl.program_id(0)
    model = hm_ref.shape[1]

    @pl.when(step == 0)
    def _():
        low_dy[...] = dy_ref[...].astype(jnp.bfloat16)

    @pl.when(step < 4)
    def _():
        d_inner = dot_columns(low_dy[...], square(down_ref))
        gate = g_ref[...].astype(jnp.float32)
        sigma = jax.nn.sigmoid(gate)
        silu = gate * sigma
        d_gate = (
            d_inner * u_ref[...].astype(jnp.float32) * (sigma + silu * (1.0 - sigma))
        ).astype(jnp.bfloat16)
        d_up = (d_inner * silu).astype(jnp.bfloat16)
        place = pl.multiple_of(step * chunk, 128)
        dg_all[:, pl.ds(place, chunk)] = d_gate
        du_all[:, pl.ds(place, chunk)] = d_up
        dg_ref[...] = d_gate
        du_ref[...] = d_up

    @pl.when(step >= 4)
    def _():
        place = pl.ds(pl.multiple_of((step - 4) * model, 128), model)
        term = dot_columns(dg_all[:, place], square(gate_ref)) + dot_columns(
            du_all[:, place], square(up_ref)
        )

        @pl.when(step == 4)
        def _():
            total[...] = term

        @pl.when(step > 4)
        def _():
            total[...] += term

        @pl.when(step == pl.num_programs(0) - 1)
        def _():
            grad = total[...]
            scaled, factor = unit_rows(hm_ref[...])
            dgain_ref[...] = jnp.sum(grad * scaled, axis=0, keepdims=True)
            d_hidden = dy_ref[...] + norm_pull(grad, scaled, factor, gain_ref[...])
            dh_ref[...] = d_hidden
            low_ref[...] = d_hidden.astype(jnp.bfloat16)


def feed_forward_back(d_result, middle, gains, gate, up, whole):
    devices, rows, model = whole.shape
    rows = rows // 9
    tokens = middle.shape[0]
    width = 3 * model
    chunk = width // 4
    column = pl.BlockSpec((tokens, chunk), lambda i: (0, jnp.minimum(i, 3)))
    full = whole_spec((tokens, model))
    return wide_call(
        functools.partial(ffn_back_kernel, chunk),
        (7,),
        [
            full,
            full,
            whole_spec((1, model)),
            column,
            column,
            pl.BlockSpec((devices, rows, model), lambda i: (0, jnp.maximum(i - 4, 0), 0)),
            pl.BlockSpec((devices, rows, model), lambda i: (0, 6 + jnp.maximum(i - 4, 0), 0)),
            pl.BlockSpec((devices // 4, 3 * rows, model), lambda i: (jnp.minimum(i, 3), 1, 0)),
        ],
        [full, full, column, column, whole_spec((1, model))],
        [
            jax.ShapeDtypeStruct((tokens, model), jnp.float32),
            jax.ShapeDtypeStruct((tokens, model), jnp.bfloat16),
            jax.ShapeDtypeStruct((tokens, width), jnp.bfloat16),
            jax.ShapeDtypeStruct((tokens, width), jnp.bfloat16),
            jax.ShapeDtypeStruct((1, model), jnp.float32),
        ],
        scratch=[
            pltpu.VMEM((tokens, width), jnp.bfloat16),
            pltpu.VMEM((tokens, width), jnp.bfloat16),
            pltpu.VMEM((tokens, model), jnp.bfloat16),
            pltpu.VMEM((tokens, model), jnp.float32),
        ],
        flops=6 * tokens * width * model,
        moved=6 * width * model + 14 * tokens * model + 8 * tokens * width,
        vmem=56,
    )(d_result, middle, gains[3], gate, up, whole, whole, whole)


def out_back_kernel(d_ref, w_ref, o_ref):
    o_ref[...] = dot_columns(d_ref[...], square(w_ref)).astype(jnp.bfloat16)


def project_out_back(low, whole):
    devices, rows, model = whole.shape
    rows = rows // 6
    tokens = low.shape[0]
    wide = QUERY_HEADS * HEAD_SIZE
    return wide_call(
        out_back_kernel,
        (4,),
        [
            whole_spec((tokens, model)),
            pl.BlockSpec((devices // 4, 2 * rows, model), lambda c: (c, 1, 0)),
        ],
        pl.BlockSpec((tokens, wide // 4), lambda c: (0, c)),
        jax.ShapeDtypeStruct((tokens, wide), jnp.bfloat16),
        flops=2 * tokens * wide * model,
        moved=2 * wide * model + 6 * tokens * model,
    )(low, whole)


BACK_HEADS = 4


def attend_back_kernel(
    q_ref, k_ref, v_ref, do_ref, pre_q_ref, pre_k_ref, row_ref, column_ref, cos_ref, sin_ref,
    gain_q_ref, gain_k_ref, dq_ref, dk_ref, dv_ref, dgain_q_ref, dgain_k_ref,
):
    tokens = k_ref.shape[0]
    first = (pl.program_id(0) == 0) & (pl.program_id(1) == 0)

    @pl.when(first)
    def _():
        dgain_q_ref[...] = jnp.zeros_like(dgain_q_ref)
        dgain_k_ref[...] = jnp.zeros_like(dgain_k_ref)

    causal = lax.broadcasted_iota(jnp.int32, (tokens, tokens), 0) <= lax.broadcasted_iota(
        jnp.int32, (tokens, tokens), 1
    )
    allowed = (row_ref[...] == column_ref[0]) & causal
    cosine, sine = cos_ref[...], sin_ref[...]
    scale = HEAD_SIZE ** (-0.5)

    def through_norm(grad, pre, gain, dgain_ref):
        grad = grad * cosine - pltpu.roll(grad, HEAD_SIZE // 2, 1) * sine
        scaled, factor = unit_rows(pre.astype(jnp.float32))
        dgain_ref[...] += jnp.sum(grad * scaled, axis=0, keepdims=True)
        return norm_pull(grad, scaled, factor, gain).astype(jnp.bfloat16)

    for shared in range(BACK_HEADS):
        lone = slice(shared * HEAD_SIZE, (shared + 1) * HEAD_SIZE)
        key, value = k_ref[:, lone], v_ref[:, lone]
        d_key = d_value = None
        for head in range(2 * shared, 2 * shared + 2):
            part = slice(head * HEAD_SIZE, (head + 1) * HEAD_SIZE)
            query, d_mixed = q_ref[:, part], do_ref[:, part]
            scores = dot_columns(key, query) * scale
            scores = jnp.where(allowed, scores, NEGATIVE)
            raised = jnp.exp(scores - jnp.max(scores, axis=0, keepdims=True))
            weights = raised * (1.0 / jnp.sum(raised, axis=0, keepdims=True))
            value_term = dot_plain(weights.astype(jnp.bfloat16), d_mixed)
            d_weights = dot_columns(value, d_mixed)
            pulled = jnp.sum(d_weights * weights, axis=0, keepdims=True)
            d_scores = (weights * (d_weights - pulled)).astype(jnp.bfloat16)
            d_query = dot_rows(d_scores, key) * scale
            key_term = dot_plain(d_scores, query)
            d_key = key_term if d_key is None else d_key + key_term
            d_value = value_term if d_value is None else d_value + value_term
            dq_ref[:, part] = through_norm(d_query, pre_q_ref[:, part], gain_q_ref[...], dgain_q_ref)
        dk_ref[:, lone] = through_norm(
            d_key * scale, pre_k_ref[:, lone], gain_k_ref[...], dgain_k_ref
        )
        dv_ref[:, lone] = d_value.astype(jnp.bfloat16)


def attend_back(qkv, pre, d_mixed, tables, gains):
    cosine, sine, row_segments, column_segments = tables
    tokens = qkv.shape[0]
    blocks = tokens // TOKENS_PER_SHARD
    groups = KEY_VALUE_HEADS // BACK_HEADS
    wide = BACK_HEADS * HEAD_SIZE
    model = KEY_VALUE_HEADS * HEAD_SIZE
    pair = pl.BlockSpec((TOKENS_PER_SHARD, 2 * wide), lambda b, g: (b, g))
    lone = pl.BlockSpec((TOKENS_PER_SHARD, wide), lambda b, g: (b, g))
    table = pl.BlockSpec((TOKENS_PER_SHARD, HEAD_SIZE), lambda b, g: (b, 0))
    return wide_call(
        attend_back_kernel,
        (blocks, groups),
        [
            pair,
            pl.BlockSpec((TOKENS_PER_SHARD, wide), lambda b, g: (b, 2 * groups + g)),
            pl.BlockSpec((TOKENS_PER_SHARD, wide), lambda b, g: (b, 3 * groups + g)),
            pair,
            pair,
            pl.BlockSpec((TOKENS_PER_SHARD, wide), lambda b, g: (b, 2 * groups + g)),
            pl.BlockSpec((TOKENS_PER_SHARD, 1), lambda b, g: (b, 0)),
            pl.BlockSpec((1, 1, TOKENS_PER_SHARD), lambda b, g: (b, 0, 0)),
            table,
            table,
            whole_spec((1, HEAD_SIZE)),
            whole_spec((1, HEAD_SIZE)),
        ],
        [pair, lone, lone, whole_spec((1, HEAD_SIZE)), whole_spec((1, HEAD_SIZE))],
        [
            jax.ShapeDtypeStruct((tokens, 2 * model), jnp.bfloat16),
            jax.ShapeDtypeStruct((tokens, model), jnp.bfloat16),
            jax.ShapeDtypeStruct((tokens, model), jnp.bfloat16),
            jax.ShapeDtypeStruct((1, HEAD_SIZE), jnp.float32),
            jax.ShapeDtypeStruct((1, HEAD_SIZE), jnp.float32),
        ],
        flops=32 * tokens * TOKENS_PER_SHARD * QUERY_HEADS * HEAD_SIZE,
        moved=30 * tokens * 1024,
    )(
        qkv, qkv, qkv, d_mixed, pre, pre, row_segments, column_segments, cosine, sine,
        gains[1], gains[2],
    )


def qkv_back_kernel(dq_ref, dk_ref, dv_ref, w_ref, h_ref, dh_ref, gain_ref, dx_ref, dgain_ref, total):
    step = pl.program_id(0)
    model = h_ref.shape[1]

    def add(part):
        term = dot_columns(part, square(w_ref))

        @pl.when(step == 0)
        def _():
            total[...] = term

        @pl.when(step > 0)
        def _():
            total[...] += term

    @pl.when(step < 2)
    def _():
        add(dq_ref[:, pl.ds(pl.multiple_of(step * model, 128), model)])

    @pl.when(step == 2)
    def _():
        add(dk_ref[...])

    @pl.when(step == 3)
    def _():
        add(dv_ref[...])
        grad = total[...]
        scaled, factor = unit_rows(h_ref[...].astype(jnp.float32))
        dgain_ref[...] = jnp.sum(grad * scaled, axis=0, keepdims=True)
        d_hidden = dh_ref[...] + norm_pull(grad, scaled, factor, gain_ref[...])
        dx_ref[...] = d_hidden.astype(jnp.bfloat16)


def project_qkv_back(d_query, d_key, d_value, whole, hidden, d_middle, gains):
    devices, rows, model = whole.shape
    rows = rows // 6
    tokens = hidden.shape[0]
    full = whole_spec((tokens, model))
    return wide_call(
        qkv_back_kernel,
        (4,),
        [
            whole_spec((tokens, 2 * model)),
            full,
            full,
            pl.BlockSpec((devices, rows, model), lambda j: (0, j + 2 * (j // 2), 0)),
            full,
            full,
            whole_spec((1, model)),
        ],
        [full, whole_spec((1, model))],
        [
            jax.ShapeDtypeStruct((tokens, model), jnp.bfloat16),
            jax.ShapeDtypeStruct((1, model), jnp.float32),
        ],
        scratch=[pltpu.VMEM((tokens, model), jnp.float32)],
        flops=8 * tokens * model * model,
        moved=8 * model * model + 16 * tokens * model,
    )(d_query, d_key, d_value, whole, hidden, d_middle, gains[0])


def grad_kernel(plan, chips, order_ref, *refs):
    count = len(plan)
    lefts, rights = refs[:count], refs[count : 2 * count]
    mine_ref, theirs_ref = refs[2 * count : 2 * count + 2]
    stores = refs[2 * count + 2 :]
    step = pl.program_id(0)
    core = order_ref[chips]

    @pl.when(step == 0)
    def _():
        for index, (rows, low, size, unit, start, blocks) in enumerate(plan):
            turned, mine, theirs = stores[3 * index : 3 * index + 3]
            turned[...] = jnp.transpose(lefts[index][...])

            def place(t, _, rows=rows, low=low, size=size, turned=turned, mine=mine, theirs=theirs):
                here = (2 * order_ref[t] + core) * rows + low
                there = (2 * order_ref[t] + 1 - core) * rows + low
                mine[t] = turned[pl.ds(pl.multiple_of(here, 16), size), :]
                theirs[t] = turned[pl.ds(pl.multiple_of(there, 16), size), :]
                return 0

            lax.fori_loop(0, chips, place, 0)

    for index, (rows, low, size, unit, start, blocks) in enumerate(plan):
        turned, mine, theirs = stores[3 * index : 3 * index + 3]
        split = size // unit

        @pl.when((step >= start) & (step < start + split * blocks))
        def _(index=index, unit=unit, start=start, split=split, mine=mine, theirs=theirs):
            part = pl.ds(pl.multiple_of(lax.rem(step - start, split) * unit, 16), unit)
            right = rights[index][...]
            for source, target in ((theirs, theirs_ref), (mine, mine_ref)):
                left = source[:, part, :]
                left = left.reshape(chips * unit, left.shape[2])
                value = dot_plain(left, right).astype(jnp.bfloat16)
                target[...] = value.reshape(target.shape)


def weight_grads(order, parts, unit):
    tokens = parts[0][0].shape[0]
    model = parts[0][4]
    chips = order.shape[0] - 1
    plan, specs_left, specs_right, scratch, start, flops = [], [], [], [], 0, 0
    for left, right, low, size, width in parts:
        rows = left.shape[1] // (2 * chips)
        blocks = right.shape[1] // width
        split = size // unit
        plan.append((rows, low, size, unit, start, blocks))
        specs_left.append(whole_spec(left.shape))

        def column(i, _, start=start, split=split, blocks=blocks):
            return (0, jnp.clip((i - start) // split, 0, blocks - 1))

        specs_right.append(pl.BlockSpec((tokens, width), column))
        scratch += [
            pltpu.VMEM((left.shape[1], tokens), jnp.bfloat16),
            pltpu.VMEM((chips, size, tokens), jnp.bfloat16),
            pltpu.VMEM((chips, size, tokens), jnp.bfloat16),
        ]
        start += split * blocks
        flops += 4 * chips * size * blocks * width * tokens
    out = pl.BlockSpec((chips, unit, model), lambda i, _: (0, i, 0))
    shape = jax.ShapeDtypeStruct((chips, start * unit, model), jnp.bfloat16)
    return wide_call(
        functools.partial(grad_kernel, tuple(plan), chips),
        (start,),
        specs_left + specs_right,
        [out, out],
        [shape, shape],
        scratch=scratch,
        flops=flops,
        moved=flops // tokens * 2,
        prefetch=1,
        vmem=56,
    )(order, *[part[0] for part in parts], *[part[1] for part in parts])


def local(
    inputs,
    teacher,
    lengths,
    attn_query,
    attn_key,
    attn_value,
    attn_out,
    ffn_gate,
    ffn_up,
    ffn_down,
    norm_attn,
    norm_ffn,
    norm_query,
    norm_key,
):
    section = lax.axis_index("section")
    index = lax.axis_index("dp")
    devices = lax.axis_size("dp")
    chips = devices // 2
    batches, _, model = inputs.shape
    slots = lengths.shape[2]
    tokens = batches * TOKENS_PER_SHARD
    rows = attn_query.shape[1]
    forward_rows = ffn_down.shape[1]

    attn_shard = jnp.concatenate(
        packed(attn_query[0], model)
        + [attn_out[0]]
        + packed(attn_key[0], model)
        + packed(attn_value[0], model),
        axis=0,
    )
    ffn_shard = jnp.concatenate(
        packed(ffn_gate[0], model) + [ffn_down[0]] + packed(ffn_up[0], model), axis=0
    )
    attn_whole, marks = gather_ring(attn_shard)
    ffn_whole, _ = gather_ring(ffn_shard, marks[RING_LEAD])

    gain_sizes = (norm_attn.shape[1], norm_query.shape[1], norm_key.shape[1], norm_ffn.shape[1])
    gain_shard = jnp.concatenate([norm_attn, norm_query, norm_key, norm_ffn], axis=1)
    gain_whole = spread(gain_shard.astype(jnp.float32))
    gains, low = [], 0
    for size in gain_sizes:
        gains.append(gain_whole[:, low : low + size].reshape(1, devices * size))
        low += size

    segments, places = jax.vmap(layout)(lengths[:, 0, :])
    keep = (segments < slots - 1).astype(jnp.float32).reshape(tokens)
    cosine_table, sine_table = rotary_tables(places.reshape(tokens))
    tables = (
        jnp.concatenate([cosine_table, cosine_table], axis=1),
        jnp.concatenate([-sine_table, sine_table], axis=1),
        segments.reshape(tokens, 1),
        segments.reshape(batches, 1, TOKENS_PER_SHARD),
    )

    first = inputs.reshape(tokens, model)
    _, qkv, _ = project_qkv(first, gains, tables, attn_whole)
    mixed = attend(qkv, tables)
    middle, normed = project_out(mixed, attn_whole, first, gains)
    (result,) = feed_forward(normed, middle, ffn_whole, False)
    carried = one_way(result, 0)

    hidden = jnp.where(section == 0, first, carried)
    normalized, qkv, pre = project_qkv(hidden, gains, tables, attn_whole)
    mixed = attend(qkv, tables)
    middle, normed = project_out(mixed, attn_whole, hidden, gains)
    result, gate, up, inner = feed_forward(normed, middle, ffn_whole, True)

    diff = result.astype(jnp.float32) - teacher.reshape(tokens, model)
    cotangent = keep[:, None] * diff
    squares = jnp.sum(cotangent * diff)

    def backward(d_result):
        d_middle, d_attn, d_gate, d_up, gain_ffn = feed_forward_back(
            d_result, middle, gains, gate, up, ffn_whole
        )
        d_mixed = project_out_back(d_attn, attn_whole)
        d_query, d_key, d_value, gain_query, gain_key = attend_back(
            qkv, pre, d_mixed, tables, gains
        )
        d_hidden, gain_attn = project_qkv_back(
            d_query, d_key, d_value, attn_whole, hidden, d_middle, gains
        )
        gain_grads = (gain_attn, gain_query, gain_key, gain_ffn)
        return d_hidden, d_attn, d_gate, d_up, d_query, d_key, d_value, gain_grads

    d_hidden = backward(cotangent)[0]
    incoming = one_way(d_hidden, 1)
    d_result = jnp.where(section == 1, cotangent, incoming.astype(jnp.float32))
    d_hidden, d_attn, d_gate, d_up, d_query, d_key, d_value, gain_grads = backward(d_result)

    core = index % 2
    place = ring_place(index // 2, chips)
    order = jnp.concatenate(
        [chip_at(place + jnp.arange(chips, dtype=jnp.int32), chips), core[None]]
    ).astype(jnp.int32)
    d_branch = d_result.astype(jnp.bfloat16)
    unit = rows // 2 if rows % 32 == 0 else rows
    cut = forward_rows // 2 if forward_rows // 2 % unit == 0 else 2 * unit
    ffn_grad = scatter_ring(
        weight_grads(
            order, [(normed, d_gate, 0, rows, model), (inner, d_branch, 0, cut, model)], unit
        ),
        weight_grads(
            order,
            [
                (inner, d_branch, cut, forward_rows - cut, model),
                (normed, d_up, 0, rows, model),
            ],
            unit,
        ),
    )
    attn_grad = scatter_ring(
        weight_grads(
            order, [(normalized, d_query, 0, rows, model), (mixed, d_attn, 0, rows, model)], rows
        ),
        weight_grads(
            order,
            [
                (mixed, d_attn, rows, rows, model),
                (normalized, d_key, 0, rows, model),
                (normalized, d_value, 0, rows, model),
            ],
            rows,
        ),
    )

    grad_gate = beside(ffn_grad, 0, 3, rows)
    grad_down = ffn_grad[3 * rows : 3 * rows + forward_rows]
    grad_up = beside(ffn_grad, 3 * rows + forward_rows, 3, rows)
    grad_query = beside(attn_grad, 0, 2, rows)
    grad_out = attn_grad[2 * rows : 4 * rows]
    grad_key = attn_grad[4 * rows : 5 * rows]
    grad_value = attn_grad[5 * rows :]

    small = jnp.concatenate(
        [*gain_grads, jnp.stack([squares, jnp.sum(keep)])[None]], axis=1
    )
    small_sum = summed(small)
    totals = small_sum[:, -2:]
    totals = jnp.where(section == 1, totals, one_way(totals, 1))[0]
    loss = totals[0] / (totals[1] * model)
    gain_grads, low = [], 0
    for size in gain_sizes:
        gain_grads.append(lax.dynamic_slice(small_sum, (0, low + index * size), (1, size)))
        low += devices * size
    grad_gain_attn, grad_gain_query, grad_gain_key, grad_gain_ffn = gain_grads

    half = batches // 2
    finals = result.reshape(batches, TOKENS_PER_SHARD, model)
    grads = d_hidden.reshape(batches, TOKENS_PER_SHARD, model)
    output = jnp.where(section == 0, one_way(finals[:half], 1), finals[half:])
    input_grad = jnp.where(section == 0, grads[:half], one_way(grads[half:], 0))
    return (
        output,
        loss,
        input_grad,
        grad_query[None],
        grad_key[None],
        grad_value[None],
        grad_out[None],
        grad_gate[None],
        grad_up[None],
        grad_down[None],
        grad_gain_attn,
        grad_gain_ffn,
        grad_gain_query,
        grad_gain_key,
    )


def solution(mesh):
    placed = (
        P(None, "dp", None),
        P(None, "dp", None),
        P(None, "dp", None),
        P("section", "dp", None),
        P("section", "dp", None),
        P("section", "dp", None),
        P("section", "dp", None),
        P("section", "dp", None),
        P("section", "dp", None),
        P("section", "dp", None),
        P("section", "dp"),
        P("section", "dp"),
        P("section", "dp"),
        P("section", "dp"),
    )
    return jax.shard_map(
        local,
        mesh=mesh,
        in_specs=placed,
        out_specs=(
            P("section", "dp", None),
            P(),
            P("section", "dp", None),
            P("section", "dp", None),
            P("section", "dp", None),
            P("section", "dp", None),
            P("section", "dp", None),
            P("section", "dp", None),
            P("section", "dp", None),
            P("section", "dp", None),
            P("section", "dp"),
            P("section", "dp"),
            P("section", "dp"),
            P("section", "dp"),
        ),
        check_vma=False,
    )
```

```python
import functools

import jax
import jax.numpy as jnp
from jax import lax
from jax.experimental import pallas as pl
from jax.experimental.pallas import tpu as pltpu
from jax.sharding import PartitionSpec as P

QUERY_HEADS = 16
KEY_VALUE_HEADS = 8
HEAD_SIZE = 128
TOKENS_PER_SHARD = 256


EPS = 1e-06
THETA = 1000000.0
NEGATIVE = -1e30
CONTRACT_ROWS = (((0,), (0,)), ((), ()))
CONTRACT_COLS = (((1,), (1,)), ((), ()))
RING_LEAD = 1
FIRST_WAIT = 3


def one_way(value, source):
    return lax.ppermute(value, "section", [(source, 1 - source)])


def chip_at(place, chips):
    place = lax.rem(place + 2 * chips, chips)
    return jnp.where(place < chips // 2, 2 * place, 2 * (chips - 1 - place) + 1)


def ring_place(chip, chips):
    return jnp.where(chip % 2 == 0, chip // 2, chips - 1 - chip // 2)


def ring_routes(devices):
    chips = devices // 2
    order = list(range(0, chips, 2)) + list(range(chips - 1, 0, -2))
    right, left = [], []
    for place in range(chips):
        here, there = order[place], order[(place + 1) % chips]
        for core in range(2):
            right.append((2 * here + core, 2 * there + core))
            left.append((2 * there + core, 2 * here + core))
    return right, left, [(device, device ^ 1) for device in range(devices)]


def tie(*values):
    return lax.optimization_barrier(values)


def spread(value):
    devices = lax.axis_size("dp")
    index = lax.axis_index("dp")
    step = 1
    while step < devices:
        other = lax.ppermute(value, "dp", [(low, low ^ step) for low in range(devices)])
        later = (index // step) % 2 == 1
        value = jnp.where(
            later,
            jnp.concatenate([other, value], axis=0),
            jnp.concatenate([value, other], axis=0),
        )
        step *= 2
    return value


def summed(value):
    devices = lax.axis_size("dp")
    step = 1
    while step < devices:
        value = value + lax.ppermute(value, "dp", [(low, low ^ step) for low in range(devices)])
        step *= 2
    return value


def blank(shape, dtype):
    return pl.pallas_call(
        lambda ref: None,
        out_specs=pl.BlockSpec(memory_space=pl.ANY),
        out_shape=jax.ShapeDtypeStruct(shape, dtype),
    )()


def gather_ring(shard, after=None):
    devices = lax.axis_size("dp")
    chips = devices // 2
    right, left, pair = ring_routes(devices)
    index = lax.axis_index("dp")
    core = index % 2
    place = ring_place(index // 2, chips)
    half = shard.shape[0] // 2
    if after is not None:
        shard, after = tie(shard, after)
    whole = blank((devices,) + shard.shape, shard.dtype)

    def put(whole, piece, owner, offset):
        return lax.dynamic_update_slice(whole, piece[None], (owner, offset, 0))

    forward, behind = shard[:half], shard[half:]
    marks = []
    other = None
    for step in range(1, chips):
        forward = lax.ppermute(forward, "dp", right)
        behind = lax.ppermute(behind, "dp", left)
        if other is None:
            other = lax.ppermute(shard, "dp", pair)
            whole = put(whole, shard, index, 0)
            whole = put(whole, other, index + 1 - 2 * core, 0)
        marks.append((forward, behind))
        forward_pair = lax.ppermute(forward, "dp", pair)
        behind_pair = lax.ppermute(behind, "dp", pair)
        owner = 2 * chip_at(place - step, chips)
        whole = put(whole, forward, owner + core, 0)
        whole = put(whole, forward_pair, owner + 1 - core, 0)
        owner = 2 * chip_at(place + step, chips)
        whole = put(whole, behind, owner + core, half)
        whole = put(whole, behind_pair, owner + 1 - core, half)
    return whole, marks


def scatter_ring(forward_parts, behind_parts):
    devices = lax.axis_size("dp")
    chips = devices // 2
    right, left, pair = ring_routes(devices)
    sums = []
    for mine, theirs in (forward_parts, behind_parts):
        got = lax.ppermute(theirs, "dp", pair)
        sums.append((mine, got))

    def own(which, place):
        mine, got = sums[which]
        return mine[place].astype(jnp.float32) + got[place].astype(jnp.float32)

    forward = own(0, chips - 1).astype(jnp.bfloat16)
    behind = own(1, 1).astype(jnp.bfloat16)
    marks = [(forward, behind)]
    for step in range(1, chips):
        forward = lax.ppermute(forward, "dp", right).astype(jnp.float32)
        behind = lax.ppermute(behind, "dp", left).astype(jnp.float32)
        forward = forward + own(0, chips - 1 - step)
        behind = behind + own(1, (step + 1) % chips)
        if step + 1 < chips:
            forward = forward.astype(jnp.bfloat16)
            behind = behind.astype(jnp.bfloat16)
            marks.append((forward, behind))
    return jnp.concatenate([forward, behind], axis=0), marks


def packed(shard, width):
    pieces = shard.shape[-1] // width
    return [shard[:, width * i : width * (i + 1)] for i in range(pieces)]


def beside(grad, low, pieces, rows):
    return jnp.concatenate(
        [grad[low + rows * i : low + rows * (i + 1)] for i in range(pieces)], axis=1
    )


def layout(lengths_row):
    ends = jnp.cumsum(lengths_row)
    places = jnp.arange(TOKENS_PER_SHARD, dtype=jnp.int32)
    passed = (ends[None, :] <= places[:, None]).astype(jnp.int32)
    segment_index = jnp.sum(passed, axis=1)
    start = jnp.sum(passed * lengths_row[None, :], axis=1)
    return (segment_index, places - start)


def rotary_tables(place):
    half = HEAD_SIZE // 2
    freqs = THETA ** (-(jnp.arange(half, dtype=jnp.float32) * 2.0 / HEAD_SIZE))
    angles = place.astype(jnp.float32)[:, None] * freqs[None, :]
    return (jnp.cos(angles), jnp.sin(angles))


LOCAL = pl.BlockSpec(memory_space=pltpu.VMEM)
SCALARS = pl.BlockSpec(memory_space=pltpu.SMEM)


def flat_call(body, arguments, out_shape, scratch=(), flops=0, moved=0, vmem=24, scalars=False):
    specs = [LOCAL] * len(arguments)
    if scalars:
        specs[0] = SCALARS
    return pl.pallas_call(
        body,
        in_specs=specs,
        out_specs=[LOCAL] * len(out_shape),
        out_shape=out_shape,
        scratch_shapes=list(scratch),
        compiler_params=pltpu.CompilerParams(vmem_limit_bytes=vmem << 20),
        cost_estimate=pl.CostEstimate(
            flops=int(flops), bytes_accessed=int(moved), transcendentals=0
        ),
    )(*arguments)


def low_shape(*shape):
    return jax.ShapeDtypeStruct(shape, jnp.bfloat16)


def full_shape(*shape):
    return jax.ShapeDtypeStruct(shape, jnp.float32)


def dot_plain(left, right):
    return jnp.dot(left, right, preferred_element_type=jnp.float32)


def dot_columns(left, right):
    return lax.dot_general(left, right, CONTRACT_COLS, preferred_element_type=jnp.float32)


def dot_rows(left, right):
    return lax.dot_general(left, right, CONTRACT_ROWS, preferred_element_type=jnp.float32)


def unit_rows(values):
    factor = lax.rsqrt(jnp.mean(values * values, axis=-1, keepdims=True) + EPS)
    return values * factor, factor


def norm_pull(grad, scaled, factor, gain):
    pulled = grad * gain
    return factor * (pulled - scaled * jnp.mean(pulled * scaled, axis=-1, keepdims=True))


def head_mean(values):
    average = jnp.full((HEAD_SIZE, HEAD_SIZE), 1.0 / HEAD_SIZE, jnp.bfloat16)
    return dot_plain(values.astype(jnp.bfloat16), average)


def slab(ref, low, rows):
    value = ref[:, low : low + rows, :]
    return value.reshape(value.shape[0] * rows, value.shape[2])


def part_of(index, width=HEAD_SIZE):
    return slice(index * width, (index + 1) * width)


def attention_kernel(
    keep, h_ref, gain_ref, gain_q_ref, gain_k_ref, gain_ffn_ref, cos_ref, sin_ref, row_ref,
    column_ref, w_ref, hm_ref, xf_ref, *rest,
):
    if keep:
        xf_t_ref, xa_t_ref, o_t_ref, qkv_ref, pre_ref, o_ref = rest
    else:
        qkv_ref, o_ref = rest
    tokens, model = h_ref.shape
    rows = w_ref.shape[1] // 6
    hidden = h_ref[...].astype(jnp.float32)
    scaled, _ = unit_rows(hidden)
    xa = (scaled * gain_ref[...]).astype(jnp.bfloat16)
    cosine, sine = cos_ref[...], sin_ref[...]
    for block, low in enumerate((0, rows, 4 * rows, 5 * rows)):
        pre = dot_plain(xa, slab(w_ref, low, rows))
        if block == 3:
            qkv_ref[:, part_of(block, model)] = pre.astype(jnp.bfloat16)
            continue
        if keep:
            pre_ref[:, part_of(block, model)] = pre.astype(jnp.bfloat16)
        gain = gain_q_ref[...] if block < 2 else gain_k_ref[...]
        for head in range(model // HEAD_SIZE):
            value = pre[:, part_of(head)]
            value = value * lax.rsqrt(head_mean(value * value) + EPS) * gain
            value = value * cosine + pltpu.roll(value, HEAD_SIZE // 2, 1) * sine
            qkv_ref[:, part_of(block * (model // HEAD_SIZE) + head)] = value.astype(jnp.bfloat16)
    causal = lax.broadcasted_iota(jnp.int32, (tokens, tokens), 0) >= lax.broadcasted_iota(
        jnp.int32, (tokens, tokens), 1
    )
    allowed = (row_ref[...] == column_ref[0]) & causal
    ones = jnp.ones((tokens, HEAD_SIZE), jnp.bfloat16)
    for shared in range(KEY_VALUE_HEADS):
        key = qkv_ref[:, part_of(QUERY_HEADS + shared)]
        value = qkv_ref[:, part_of(QUERY_HEADS + KEY_VALUE_HEADS + shared)]
        value = jnp.concatenate([value, ones], axis=1)
        for head in range(2 * shared, 2 * shared + 2):
            scores = dot_columns(qkv_ref[:, part_of(head)], key) * HEAD_SIZE ** (-0.5)
            raised = jnp.where(allowed, jnp.exp(scores), 0.0).astype(jnp.bfloat16)
            mixed = dot_plain(raised, value)
            mixed = mixed[:, :HEAD_SIZE] / mixed[:, HEAD_SIZE:]
            o_ref[:, part_of(head)] = mixed.astype(jnp.bfloat16)
    middle = hidden + dot_plain(o_ref[...], slab(w_ref, 2 * rows, 2 * rows))
    hm_ref[...] = middle
    scaled, _ = unit_rows(middle)
    xf = (scaled * gain_ffn_ref[...]).astype(jnp.bfloat16)
    xf_ref[...] = xf
    if keep:
        xf_t_ref[...] = jnp.transpose(xf)
        xa_t_ref[...] = jnp.transpose(xa)
        o_t_ref[...] = jnp.transpose(o_ref[...])


def attention(hidden, gains, tables, whole, keep):
    tokens, model = hidden.shape
    wide = QUERY_HEADS * HEAD_SIZE
    shapes = [full_shape(tokens, model), low_shape(tokens, model)]
    scratch = [pltpu.VMEM((tokens, wide), jnp.bfloat16)]
    if keep:
        shapes += [
            low_shape(model, tokens),
            low_shape(model, tokens),
            low_shape(wide, tokens),
            low_shape(tokens, 4 * model),
            low_shape(tokens, 3 * model),
        ]
    else:
        scratch = [pltpu.VMEM((tokens, 4 * model), jnp.bfloat16)] + scratch
    return flat_call(
        functools.partial(attention_kernel, keep),
        (hidden, *gains, *tables, whole),
        shapes,
        scratch=scratch,
        flops=2 * tokens * model * 6 * model + 8 * tokens * tokens * wide,
        moved=12 * model * model + 20 * tokens * model,
    )


def ffn_kernel(keep, xf_ref, hm_ref, w_ref, y_ref, *rest):
    if keep:
        g_ref, u_ref, z_t_ref, inner = rest
    else:
        (inner,) = rest
    tokens, model = xf_ref.shape
    rows = w_ref.shape[1] // 9
    xf = xf_ref[...]
    for block in range(3):
        gate = dot_plain(xf, slab(w_ref, block * rows, rows))
        up = dot_plain(xf, slab(w_ref, (6 + block) * rows, rows))
        mixed = (gate * jax.nn.sigmoid(gate) * up).astype(jnp.bfloat16)
        inner[:, part_of(block, model)] = mixed
        if keep:
            g_ref[:, part_of(block, model)] = gate.astype(jnp.bfloat16)
            u_ref[:, part_of(block, model)] = up.astype(jnp.bfloat16)
            z_t_ref[part_of(block, model), :] = jnp.transpose(mixed)
    total = hm_ref[...] + dot_plain(inner[...], slab(w_ref, 3 * rows, 3 * rows))
    y_ref[...] = total.astype(jnp.bfloat16)


def feed_forward(normed, middle, whole, keep):
    tokens, model = normed.shape
    width = 3 * model
    shapes = [low_shape(tokens, model)]
    if keep:
        shapes += [low_shape(tokens, width), low_shape(tokens, width), low_shape(width, tokens)]
    return flat_call(
        functools.partial(ffn_kernel, keep),
        (normed, middle, whole),
        shapes,
        scratch=[pltpu.VMEM((tokens, width), jnp.bfloat16)],
        flops=6 * tokens * width * model,
        moved=6 * width * model + 8 * tokens * model,
    )


def ffn_back_kernel(
    dy_ref, hm_ref, gain_ref, g_ref, u_ref, w_ref, dh_ref, low_ref, dg_ref, du_ref, dgain_ref
):
    devices, rows, model = w_ref.shape
    rows = rows // 9
    low_dy = dy_ref[...].astype(jnp.bfloat16)
    chunks = 4
    owners = devices // chunks
    chunk = 3 * model // chunks
    for block in range(chunks):
        part = part_of(block, chunk)
        down = w_ref[block * owners : (block + 1) * owners, 3 * rows : 6 * rows, :]
        d_inner = dot_columns(low_dy, down.reshape(chunk, model))
        gate = g_ref[:, part].astype(jnp.float32)
        sigma = jax.nn.sigmoid(gate)
        silu = gate * sigma
        d_gate = d_inner * u_ref[:, part].astype(jnp.float32) * (sigma + silu * (1.0 - sigma))
        dg_ref[:, part] = d_gate.astype(jnp.bfloat16)
        du_ref[:, part] = (d_inner * silu).astype(jnp.bfloat16)
    grad = None
    for block in range(3):
        part = part_of(block, model)
        term = dot_columns(dg_ref[:, part], slab(w_ref, block * rows, rows))
        term = term + dot_columns(du_ref[:, part], slab(w_ref, (6 + block) * rows, rows))
        grad = term if grad is None else grad + term
    scaled, factor = unit_rows(hm_ref[...])
    dgain_ref[...] = jnp.sum(grad * scaled, axis=0, keepdims=True)
    d_hidden = dy_ref[...] + norm_pull(grad, scaled, factor, gain_ref[...])
    dh_ref[...] = d_hidden
    low_ref[...] = d_hidden.astype(jnp.bfloat16)


def feed_forward_back(d_result, middle, gains, gate, up, whole):
    tokens, model = middle.shape
    width = 3 * model
    return flat_call(
        ffn_back_kernel,
        (d_result, middle, gains[3], gate, up, whole),
        [
            full_shape(tokens, model),
            low_shape(tokens, model),
            low_shape(tokens, width),
            low_shape(tokens, width),
            full_shape(1, model),
        ],
        flops=6 * tokens * width * model,
        moved=6 * width * model + 14 * tokens * model + 8 * tokens * width,
    )


def attention_back_kernel(
    low_ref, dh_ref, h_ref, qkv_ref, pre_ref, gain_ref, gain_q_ref, gain_k_ref, cos_ref, sin_ref,
    row_ref, column_ref, w_ref, dq_ref, dk_ref, dv_ref, dx_ref, dgain_ref, dgain_q_ref,
    dgain_k_ref, do_ref,
):
    tokens, model = h_ref.shape
    rows = w_ref.shape[1] // 6
    do_ref[...] = dot_columns(low_ref[...], slab(w_ref, 2 * rows, 2 * rows)).astype(jnp.bfloat16)
    causal = lax.broadcasted_iota(jnp.int32, (tokens, tokens), 0) <= lax.broadcasted_iota(
        jnp.int32, (tokens, tokens), 1
    )
    allowed = (row_ref[...] == column_ref[0]) & causal
    cosine, sine = cos_ref[...], sin_ref[...]
    scale = HEAD_SIZE ** (-0.5)
    gain_grads = [jnp.zeros((1, HEAD_SIZE), jnp.float32)] * 2

    def through_norm(grad, pre, gain_ref, which):
        gain = gain_ref[...]
        grad = grad * cosine - pltpu.roll(grad, HEAD_SIZE // 2, 1) * sine
        pre = pre.astype(jnp.float32)
        factor = lax.rsqrt(head_mean(pre * pre) + EPS)
        scaled = pre * factor
        gain_grads[which] = gain_grads[which] + jnp.sum(grad * scaled, axis=0, keepdims=True)
        pulled = grad * gain
        return (factor * (pulled - scaled * head_mean(pulled * scaled))).astype(jnp.bfloat16)

    for shared in range(KEY_VALUE_HEADS):
        lone = part_of(shared)
        key = qkv_ref[:, part_of(QUERY_HEADS + shared)]
        value = qkv_ref[:, part_of(QUERY_HEADS + KEY_VALUE_HEADS + shared)]
        d_key = d_value = None
        for head in range(2 * shared, 2 * shared + 2):
            part = part_of(head)
            query, d_mixed = qkv_ref[:, part], do_ref[:, part]
            scores = dot_columns(key, query) * scale
            raised = jnp.where(allowed, jnp.exp(scores), 0.0)
            weights = raised * (1.0 / jnp.sum(raised, axis=0, keepdims=True))
            value_term = dot_plain(weights.astype(jnp.bfloat16), d_mixed)
            d_weights = dot_columns(value, d_mixed)
            pulled = jnp.sum(d_weights * weights, axis=0, keepdims=True)
            d_scores = (weights * (d_weights - pulled)).astype(jnp.bfloat16)
            d_query = dot_rows(d_scores, key) * scale
            key_term = dot_plain(d_scores, query)
            d_key = key_term if d_key is None else d_key + key_term
            d_value = value_term if d_value is None else d_value + value_term
            dq_ref[:, part] = through_norm(d_query, pre_ref[:, part], gain_q_ref, 0)
        dk_ref[:, lone] = through_norm(
            d_key * scale, pre_ref[:, part_of(QUERY_HEADS + shared)], gain_k_ref, 1
        )
        dv_ref[:, lone] = d_value.astype(jnp.bfloat16)
    dgain_q_ref[...], dgain_k_ref[...] = gain_grads
    grad = dot_columns(dq_ref[:, part_of(0, model)], slab(w_ref, 0, rows))
    grad = grad + dot_columns(dq_ref[:, part_of(1, model)], slab(w_ref, rows, rows))
    grad = grad + dot_columns(dk_ref[...], slab(w_ref, 4 * rows, rows))
    grad = grad + dot_columns(dv_ref[...], slab(w_ref, 5 * rows, rows))
    scaled, factor = unit_rows(h_ref[...].astype(jnp.float32))
    dgain_ref[...] = jnp.sum(grad * scaled, axis=0, keepdims=True)
    d_hidden = dh_ref[...] + norm_pull(grad, scaled, factor, gain_ref[...])
    dx_ref[...] = d_hidden.astype(jnp.bfloat16)


def attention_back(low, d_middle, hidden, qkv, pre, gains, tables, whole):
    tokens, model = hidden.shape
    wide = QUERY_HEADS * HEAD_SIZE
    return flat_call(
        attention_back_kernel,
        (low, d_middle, hidden, qkv, pre, *gains[:3], *tables, whole),
        [
            low_shape(tokens, wide),
            low_shape(tokens, model),
            low_shape(tokens, model),
            low_shape(tokens, model),
            full_shape(1, model),
            full_shape(1, HEAD_SIZE),
            full_shape(1, HEAD_SIZE),
        ],
        scratch=[pltpu.VMEM((tokens, wide), jnp.bfloat16)],
        flops=2 * tokens * model * 6 * model + 20 * tokens * tokens * wide,
        moved=12 * model * model + 40 * tokens * model,
    )


def grad_kernel(plan, chips, batches, order_ref, *refs):
    count = len(plan) * batches
    lefts, rights = refs[:count], refs[count : 2 * count]
    mine_ref, theirs_ref = refs[2 * count : 2 * count + 2]
    stores = refs[2 * count + 2 :]
    core = order_ref[chips]
    model = mine_ref.shape[2]
    for index, (rows, low, size, blocks, start) in enumerate(plan):
        left, right = lefts[index * batches :][:batches], rights[index * batches :][:batches]
        for target, side, store in (
            (theirs_ref, 1 - core, stores[2 * index]),
            (mine_ref, core, stores[2 * index + 1]),
        ):
            for t in range(chips):
                place = pl.multiple_of((2 * order_ref[t] + side) * rows + low, 16)
                for batch in range(batches):
                    store[batch, t * size : (t + 1) * size, :] = left[batch][pl.ds(place, size), :]
            for block in range(blocks):
                value = None
                for batch in range(batches):
                    term = dot_plain(store[batch], right[batch][:, part_of(block, model)])
                    value = term if value is None else value + term
                value = value.astype(jnp.bfloat16).reshape(chips, size, model)
                target[:, start + block * size : start + (block + 1) * size, :] = value


def weight_grads(order, parts, model):
    batches = len(parts[0][0])
    tokens = parts[0][0][0].shape[1]
    chips = order.shape[0] - 1
    plan, scratch, start = [], [], 0
    for left, right, low, size in parts:
        rows = left[0].shape[0] // (2 * chips)
        blocks = right[0].shape[1] // model
        plan.append((rows, low, size, blocks, start))
        scratch += [pltpu.VMEM((batches, chips * size, tokens), jnp.bfloat16)] * 2
        start += size * blocks
    shape = low_shape(chips, start, model)
    lefts = [array for part in parts for array in part[0]]
    rights = [array for part in parts for array in part[1]]
    flops = 4 * chips * start * model * tokens * batches
    return flat_call(
        functools.partial(grad_kernel, tuple(plan), chips, batches),
        (order, *lefts, *rights),
        [shape, shape],
        scratch=scratch,
        flops=flops,
        moved=4 * chips * start * model + 8 * tokens * batches * model,
        scalars=True,
    )


def local(
    inputs,
    teacher,
    lengths,
    attn_query,
    attn_key,
    attn_value,
    attn_out,
    ffn_gate,
    ffn_up,
    ffn_down,
    norm_attn,
    norm_ffn,
    norm_query,
    norm_key,
):
    section = lax.axis_index("section")
    index = lax.axis_index("dp")
    devices = lax.axis_size("dp")
    chips = devices // 2
    batches, _, model = inputs.shape
    slots = lengths.shape[2]
    rows = attn_query.shape[1]
    forward_rows = ffn_down.shape[1]

    attn_shard = jnp.concatenate(
        packed(attn_query[0], model)
        + [attn_out[0]]
        + packed(attn_key[0], model)
        + packed(attn_value[0], model),
        axis=0,
    )
    ffn_shard = jnp.concatenate(
        packed(ffn_gate[0], model) + [ffn_down[0]] + packed(ffn_up[0], model), axis=0
    )
    attn_whole, attn_marks = gather_ring(attn_shard)
    ffn_whole, ffn_marks = gather_ring(ffn_shard, attn_marks[min(RING_LEAD, chips - 2)])

    gain_sizes = (norm_attn.shape[1], norm_query.shape[1], norm_key.shape[1], norm_ffn.shape[1])
    gain_shard = jnp.concatenate([norm_attn, norm_query, norm_key, norm_ffn], axis=1)
    gain_shard, _ = tie(gain_shard.astype(jnp.float32), attn_marks[min(2, chips - 2)])
    gain_whole = spread(gain_shard)
    gains, low = [], 0
    for size in gain_sizes:
        gains.append(gain_whole[:, low : low + size].reshape(1, devices * size))
        low += size

    segments, places = jax.vmap(layout)(lengths[:, 0, :])
    keep = (segments < slots - 1).astype(jnp.float32)
    tables = []
    for batch in range(batches):
        cosine_table, sine_table = rotary_tables(places[batch])
        tables.append(
            (
                jnp.concatenate([cosine_table, cosine_table], axis=1),
                jnp.concatenate([-sine_table, sine_table], axis=1),
                segments[batch].reshape(TOKENS_PER_SHARD, 1),
                segments[batch].reshape(1, 1, TOKENS_PER_SHARD),
            )
        )
    both = range(batches)

    def waiting(value, marks, step):
        return tie(value, marks[min(step, chips - 2)])[0]

    first = [inputs[batch] for batch in both]
    carried, seen = [], []
    for batch in both:
        start = waiting(first[batch], ffn_marks, FIRST_WAIT + batch)
        seen.append(attention(start, gains, tables[batch], attn_whole, False))
    for batch in both:
        (result,) = feed_forward(seen[batch][1], seen[batch][0], ffn_whole, False)
        carried.append(one_way(result, 0))

    kept = []
    for batch in both:
        hidden = jnp.where(section == 0, first[batch], carried[batch])
        mid, norm, norm_t, normalized_t, mix_t, qkv, pre = attention(
            hidden, gains, tables[batch], attn_whole, True
        )
        result, gate, up, inner_t = feed_forward(norm, mid, ffn_whole, True)
        kept.append((hidden, normalized_t, qkv, pre, mix_t, mid, norm_t, result, gate, up, inner_t))
    hidden, normalized_t, qkv, pre, mixed_t, middle, normed_t, result, gate, up, inner_t = (
        list(column) for column in zip(*kept)
    )

    cotangent, squares = [], 0.0
    for batch in both:
        diff = result[batch].astype(jnp.float32) - teacher[batch]
        cotangent.append(keep[batch][:, None] * diff)
        squares = squares + jnp.sum(cotangent[batch] * diff)

    core = index % 2
    place = ring_place(index // 2, chips)
    order = jnp.concatenate(
        [chip_at(place + jnp.arange(chips, dtype=jnp.int32), chips), core[None]]
    ).astype(jnp.int32)
    cut = forward_rows // 2 if forward_rows % 32 == 0 else 2 * rows

    incoming = []
    for batch in both:
        d_middle, d_attn, _, _, _ = feed_forward_back(
            cotangent[batch], middle[batch], gains, gate[batch], up[batch], ffn_whole
        )
        d_hidden = attention_back(
            d_attn, d_middle, hidden[batch], qkv[batch], pre[batch], gains, tables[batch], attn_whole
        )[3]
        incoming.append(one_way(d_hidden, 1))

    d_middle, d_attn, d_gate, d_up, d_branch, gain_ffn = [], [], [], [], [], 0.0
    for batch in both:
        d_result = jnp.where(
            section == 1, cotangent[batch], incoming[batch].astype(jnp.float32)
        )
        d_branch.append(d_result.astype(jnp.bfloat16))
        m, a, g, u, gain = feed_forward_back(
            d_result, middle[batch], gains, gate[batch], up[batch], ffn_whole
        )
        d_middle.append(m)
        d_attn.append(a)
        d_gate.append(g)
        d_up.append(u)
        gain_ffn = gain_ffn + gain
    forward_parts = weight_grads(
        order, [(normed_t, d_gate, 0, rows), (inner_t, d_branch, 0, cut)], model
    )
    behind_parts = weight_grads(
        order, [(inner_t, d_branch, cut, forward_rows - cut), (normed_t, d_up, 0, rows)], model
    )
    ffn_grad, marks = scatter_ring(forward_parts, behind_parts)
    d_query, d_key, d_value, d_hidden = [], [], [], []
    gain_attn, gain_query, gain_key = 0.0, 0.0, 0.0
    for batch in both:
        if batch == 0:
            value, _ = tie(d_attn[batch], (forward_parts, behind_parts))
        else:
            value = waiting(d_attn[batch], marks, batch - 1)
        q, k, v, x, gain_a, gain_q, gain_k = attention_back(
            value, d_middle[batch], hidden[batch], qkv[batch], pre[batch], gains, tables[batch],
            attn_whole,
        )
        d_query.append(q)
        d_key.append(k)
        d_value.append(v)
        d_hidden.append(x)
        gain_attn = gain_attn + gain_a
        gain_query = gain_query + gain_q
        gain_key = gain_key + gain_k
    gain_grads = (gain_attn, gain_query, gain_key, gain_ffn)
    attn_grad, attn_marks = scatter_ring(
        weight_grads(
            waiting(order, marks, 1),
            [(normalized_t, d_query, 0, rows), (mixed_t, d_attn, 0, rows)],
            model,
        ),
        weight_grads(
            waiting(order, marks, 2),
            [
                (mixed_t, d_attn, rows, rows),
                (normalized_t, d_key, 0, rows),
                (normalized_t, d_value, 0, rows),
            ],
            model,
        ),
    )

    grad_gate = beside(ffn_grad, 0, 3, rows)
    grad_down = ffn_grad[3 * rows : 3 * rows + forward_rows]
    grad_up = beside(ffn_grad, 3 * rows + forward_rows, 3, rows)
    grad_query = beside(attn_grad, 0, 2, rows)
    grad_out = attn_grad[2 * rows : 4 * rows]
    grad_key = attn_grad[4 * rows : 5 * rows]
    grad_value = attn_grad[5 * rows :]

    small = jnp.concatenate(
        [*gain_grads, jnp.stack([squares, jnp.sum(keep)])[None]], axis=1
    )
    small_sum = summed(waiting(small, attn_marks, 2))
    totals = small_sum[:, -2:]
    totals = jnp.where(section == 1, totals, one_way(totals, 1))[0]
    loss = totals[0] / (totals[1] * model)
    gain_grads, low = [], 0
    for size in gain_sizes:
        gain_grads.append(lax.dynamic_slice(small_sum, (0, low + index * size), (1, size)))
        low += devices * size
    grad_gain_attn, grad_gain_query, grad_gain_key, grad_gain_ffn = gain_grads

    half = batches // 2
    finals = jnp.stack(result)
    grads = jnp.stack(d_hidden)
    output = jnp.where(section == 0, one_way(finals[:half], 1), finals[half:])
    input_grad = jnp.where(section == 0, grads[:half], one_way(grads[half:], 0))
    return (
        output,
        loss,
        input_grad,
        grad_query[None],
        grad_key[None],
        grad_value[None],
        grad_out[None],
        grad_gate[None],
        grad_up[None],
        grad_down[None],
        grad_gain_attn,
        grad_gain_ffn,
        grad_gain_query,
        grad_gain_key,
    )


def solution(mesh):
    placed = (
        P(None, "dp", None),
        P(None, "dp", None),
        P(None, "dp", None),
        P("section", "dp", None),
        P("section", "dp", None),
        P("section", "dp", None),
        P("section", "dp", None),
        P("section", "dp", None),
        P("section", "dp", None),
        P("section", "dp", None),
        P("section", "dp"),
        P("section", "dp"),
        P("section", "dp"),
        P("section", "dp"),
    )
    return jax.shard_map(
        local,
        mesh=mesh,
        in_specs=placed,
        out_specs=(
            P("section", "dp", None),
            P(),
            P("section", "dp", None),
            P("section", "dp", None),
            P("section", "dp", None),
            P("section", "dp", None),
            P("section", "dp", None),
            P("section", "dp", None),
            P("section", "dp", None),
            P("section", "dp", None),
            P("section", "dp"),
            P("section", "dp"),
            P("section", "dp"),
            P("section", "dp"),
        ),
        check_vma=False,
    )
```

```python
import functools

import jax
import jax.numpy as jnp
from jax import lax
from jax.experimental import pallas as pl
from jax.experimental.pallas import tpu as pltpu
from jax.sharding import PartitionSpec as P

QUERY_HEADS = 16
KEY_VALUE_HEADS = 8
HEAD_SIZE = 128
TOKENS_PER_SHARD = 256


EPS = 1e-06
THETA = 1000000.0
NEGATIVE = -1e30
CONTRACT_ROWS = (((0,), (0,)), ((), ()))
CONTRACT_COLS = (((1,), (1,)), ((), ()))
RING_LEAD = 1
FIRST_WAIT = 3
SLOT_DEPTH = 2
VMEM_GRANT = 10
BLANK_SPACE = pl.ANY


def one_way(value, source):
    return lax.ppermute(value, "section", [(source, 1 - source)])


def chip_at(place, chips):
    place = lax.rem(place + 2 * chips, chips)
    return jnp.where(place < chips // 2, 2 * place, 2 * (chips - 1 - place) + 1)


def ring_place(chip, chips):
    return jnp.where(chip % 2 == 0, chip // 2, chips - 1 - chip // 2)


def ring_routes(devices):
    chips = devices // 2
    order = list(range(0, chips, 2)) + list(range(chips - 1, 0, -2))
    around = []
    for place in range(chips):
        here, there = order[place], order[(place + 1) % chips]
        around += [(2 * here, 2 * there), (2 * there + 1, 2 * here + 1)]
    return around, [(device, device ^ 1) for device in range(devices)]


def tie(*values):
    return lax.optimization_barrier(values)


def spread(value):
    devices = lax.axis_size("dp")
    index = lax.axis_index("dp")
    step = 1
    while step < devices:
        other = lax.ppermute(value, "dp", [(low, low ^ step) for low in range(devices)])
        later = (index // step) % 2 == 1
        value = jnp.where(
            later,
            jnp.concatenate([other, value], axis=0),
            jnp.concatenate([value, other], axis=0),
        )
        step *= 2
    return value


def summed(value):
    devices = lax.axis_size("dp")
    step = 1
    while step < devices:
        value = value + lax.ppermute(value, "dp", [(low, low ^ step) for low in range(devices)])
        step *= 2
    return value


def blank(shape, dtype):
    return pl.pallas_call(
        lambda ref: None,
        out_specs=pl.BlockSpec(memory_space=BLANK_SPACE),
        out_shape=jax.ShapeDtypeStruct(shape, dtype),
    )()


def gather_ring(packed, rows, after=None):
    devices = lax.axis_size("dp")
    chips = devices // 2
    around, pair = ring_routes(devices)
    index = lax.axis_index("dp")
    core = index % 2
    place = ring_place(index // 2, chips)
    if after is not None:
        packed, after = tie(packed, after)
    half, model = packed.shape[1:]
    whole = blank((devices, rows, model), packed.dtype)
    own_low = core * (rows - half)
    other_low = (1 - core) * (rows - half)

    def put(whole, piece, owner, offset):
        return lax.dynamic_update_slice(whole, piece, (owner, offset, 0))

    other = lax.ppermute(packed, "dp", pair)
    mine = lax.dynamic_slice_in_dim(packed, core, 1, 0)
    theirs = lax.dynamic_slice_in_dim(other, core, 1, 0)
    piece = jnp.where(
        core == 0,
        jnp.concatenate([mine, theirs], axis=0),
        jnp.concatenate([theirs, mine], axis=0),
    )
    marks = []
    for step in range(1, chips):
        start = piece
        piece = lax.ppermute(piece, "dp", around)
        if step == 1:
            whole = put(whole, start, index - core, own_low)
            start = lax.dynamic_slice_in_dim(other, 1 - core, 1, 0)
            whole = put(whole, start, index + 1 - 2 * core, other_low)
            start = lax.dynamic_slice_in_dim(packed, 1 - core, 1, 0)
            whole = put(whole, start, index, other_low)
        marks.append(piece)
        swapped = lax.ppermute(piece, "dp", pair)
        turn = (2 * core - 1) * step
        whole = put(whole, piece, 2 * chip_at(place + turn, chips), own_low)
        whole = put(whole, swapped, 2 * chip_at(place - turn, chips), other_low)
    return whole, marks


class ScatterRing:
    def __init__(self, mine, theirs):
        devices = lax.axis_size("dp")
        self.chips = devices // 2
        self.route, self.pair = ring_routes(devices)
        self.mine, self.theirs, self.got = mine, theirs, None
        early = lax.ppermute(theirs[1:2], "dp", self.pair)[0]
        value = mine[1].astype(jnp.float32) + early.astype(jnp.float32)
        self.value = value.astype(jnp.bfloat16)
        self.start = self.value
        self.step = 1

    def exchange(self):
        self.got = lax.ppermute(self.theirs, "dp", self.pair)

    def advance(self, before):
        if before is not None:
            self.value, _ = tie(self.value, before)
        self.step += 1
        place = self.step % self.chips
        value = lax.ppermute(self.value, "dp", self.route).astype(jnp.float32)
        value = value + self.mine[place].astype(jnp.float32)
        value = value + self.got[place].astype(jnp.float32)
        self.value = value.astype(jnp.bfloat16) if self.step < self.chips else value
        return self.value

    def halves(self):
        core = lax.axis_index("dp") % 2
        own = lax.dynamic_index_in_dim(self.value, core, 0, keepdims=False)
        other = lax.dynamic_index_in_dim(self.value, 1 - core, 0, keepdims=False)
        other = lax.ppermute(other, "dp", self.pair)
        return jnp.where(core == 0, own, other), jnp.where(core == 0, other, own)


def run_slots(slots, history, depth):
    for ring in slots:
        if ring.step < ring.chips:
            before = history[-depth] if len(history) >= depth else None
            history.append(ring.advance(before))


def beside(grad, low, pieces, rows):
    return jnp.concatenate(
        [grad[low + rows * i : low + rows * (i + 1)] for i in range(pieces)], axis=1
    )


def layout(lengths_row):
    ends = jnp.cumsum(lengths_row)
    places = jnp.arange(TOKENS_PER_SHARD, dtype=jnp.int32)
    passed = (ends[None, :] <= places[:, None]).astype(jnp.int32)
    segment_index = jnp.sum(passed, axis=1)
    start = jnp.sum(passed * lengths_row[None, :], axis=1)
    return (segment_index, places - start)


def rotary_tables(place):
    half = HEAD_SIZE // 2
    freqs = THETA ** (-(jnp.arange(half, dtype=jnp.float32) * 2.0 / HEAD_SIZE))
    angles = place.astype(jnp.float32)[:, None] * freqs[None, :]
    return (jnp.cos(angles), jnp.sin(angles))


LOCAL = pl.BlockSpec(memory_space=pltpu.VMEM)
SCALARS = pl.BlockSpec(memory_space=pltpu.SMEM)


def flat_call(body, arguments, out_shape, scratch=(), flops=0, moved=0, vmem=VMEM_GRANT):
    specs = [SCALARS] + [LOCAL] * (len(arguments) - 1)
    return pl.pallas_call(
        body,
        in_specs=specs,
        out_specs=[LOCAL] * len(out_shape),
        out_shape=out_shape,
        scratch_shapes=list(scratch),
        compiler_params=pltpu.CompilerParams(vmem_limit_bytes=vmem << 20),
        cost_estimate=pl.CostEstimate(
            flops=int(flops), bytes_accessed=int(moved), transcendentals=0
        ),
    )(*arguments)


def low_shape(*shape):
    return jax.ShapeDtypeStruct(shape, jnp.bfloat16)


def full_shape(*shape):
    return jax.ShapeDtypeStruct(shape, jnp.float32)


def dot_plain(left, right):
    return jnp.dot(left, right, preferred_element_type=jnp.float32)


def dot_columns(left, right):
    return lax.dot_general(left, right, CONTRACT_COLS, preferred_element_type=jnp.float32)


def dot_rows(left, right):
    return lax.dot_general(left, right, CONTRACT_ROWS, preferred_element_type=jnp.float32)


def unit_rows(values):
    factor = lax.rsqrt(jnp.mean(values * values, axis=-1, keepdims=True) + EPS)
    return values * factor, factor


def norm_pull(grad, scaled, factor, gain):
    pulled = grad * gain
    return factor * (pulled - scaled * jnp.mean(pulled * scaled, axis=-1, keepdims=True))


def head_mean(values):
    average = jnp.full((HEAD_SIZE, HEAD_SIZE), 1.0 / HEAD_SIZE, jnp.bfloat16)
    return dot_plain(values.astype(jnp.bfloat16), average)


def slab(ref, low, rows):
    value = ref[:, low : low + rows, :]
    return value.reshape(value.shape[0] * rows, value.shape[2])


def part_of(index, width=HEAD_SIZE):
    return slice(index * width, (index + 1) * width)


def attention_kernel(
    keep, section_ref, h_ref, came_ref, gain_ref, gain_q_ref, gain_k_ref, gain_ffn_ref, cos_ref,
    sin_ref, row_ref, column_ref, w_ref, hm_ref, xf_ref, *rest,
):
    if keep:
        xf_t_ref, xa_t_ref, o_t_ref, qkv_ref, pre_ref, hidden_ref, o_ref = rest
    else:
        qkv_ref, o_ref = rest
    tokens, model = h_ref.shape
    rows = w_ref.shape[1] // 6
    hidden = h_ref[...]
    if keep:
        hidden = jnp.where(section_ref[0] == 0, hidden, came_ref[...])
        hidden_ref[...] = hidden
    hidden = hidden.astype(jnp.float32)
    scaled, _ = unit_rows(hidden)
    xa = (scaled * gain_ref[...]).astype(jnp.bfloat16)
    cosine, sine = cos_ref[...], sin_ref[...]
    for block, low in enumerate((0, rows, 4 * rows, 5 * rows)):
        pre = dot_plain(xa, slab(w_ref, low, rows))
        if block == 3:
            qkv_ref[:, part_of(block, model)] = pre.astype(jnp.bfloat16)
            continue
        if keep:
            pre_ref[:, part_of(block, model)] = pre.astype(jnp.bfloat16)
        gain = gain_q_ref[...] if block < 2 else gain_k_ref[...]
        for head in range(model // HEAD_SIZE):
            value = pre[:, part_of(head)]
            value = value * lax.rsqrt(head_mean(value * value) + EPS) * gain
            value = value * cosine + pltpu.roll(value, HEAD_SIZE // 2, 1) * sine
            qkv_ref[:, part_of(block * (model // HEAD_SIZE) + head)] = value.astype(jnp.bfloat16)
    causal = lax.broadcasted_iota(jnp.int32, (tokens, tokens), 0) >= lax.broadcasted_iota(
        jnp.int32, (tokens, tokens), 1
    )
    allowed = (row_ref[...] == column_ref[0]) & causal
    ones = jnp.ones((tokens, HEAD_SIZE), jnp.bfloat16)
    for shared in range(KEY_VALUE_HEADS):
        key = qkv_ref[:, part_of(QUERY_HEADS + shared)]
        value = qkv_ref[:, part_of(QUERY_HEADS + KEY_VALUE_HEADS + shared)]
        value = jnp.concatenate([value, ones], axis=1)
        for head in range(2 * shared, 2 * shared + 2):
            scores = dot_columns(qkv_ref[:, part_of(head)], key) * HEAD_SIZE ** (-0.5)
            raised = jnp.where(allowed, jnp.exp(scores), 0.0).astype(jnp.bfloat16)
            mixed = dot_plain(raised, value)
            mixed = mixed[:, :HEAD_SIZE] / mixed[:, HEAD_SIZE:]
            o_ref[:, part_of(head)] = mixed.astype(jnp.bfloat16)
    middle = hidden + dot_plain(o_ref[...], slab(w_ref, 2 * rows, 2 * rows))
    hm_ref[...] = middle
    scaled, _ = unit_rows(middle)
    xf = (scaled * gain_ffn_ref[...]).astype(jnp.bfloat16)
    xf_ref[...] = xf
    if keep:
        xf_t_ref[...] = jnp.transpose(xf)
        xa_t_ref[...] = jnp.transpose(xa)
        o_t_ref[...] = jnp.transpose(o_ref[...])


def attention(section, hidden, came, gains, tables, whole, keep):
    tokens, model = hidden.shape
    wide = QUERY_HEADS * HEAD_SIZE
    shapes = [full_shape(tokens, model), low_shape(tokens, model)]
    scratch = [pltpu.VMEM((tokens, wide), jnp.bfloat16)]
    if keep:
        shapes += [
            low_shape(model, tokens),
            low_shape(model, tokens),
            low_shape(wide, tokens),
            low_shape(tokens, 4 * model),
            low_shape(tokens, 3 * model),
            low_shape(tokens, model),
        ]
    else:
        scratch = [pltpu.VMEM((tokens, 4 * model), jnp.bfloat16)] + scratch
    return flat_call(
        functools.partial(attention_kernel, keep),
        (section, hidden, came, *gains, *tables, whole),
        shapes,
        scratch=scratch,
        flops=2 * tokens * model * 6 * model + 8 * tokens * tokens * wide,
        moved=12 * model * model + 20 * tokens * model,
    )


def ffn_kernel(keep, _, xf_ref, hm_ref, w_ref, *rest):
    if keep:
        teacher_ref, keep_ref, y_ref, g_ref, u_ref, z_t_ref, pull_ref, square_ref, inner = rest
    else:
        y_ref, inner = rest
    tokens, model = xf_ref.shape
    rows = w_ref.shape[1] // 9
    xf = xf_ref[...]
    for block in range(3):
        gate = dot_plain(xf, slab(w_ref, block * rows, rows))
        up = dot_plain(xf, slab(w_ref, (6 + block) * rows, rows))
        mixed = (gate * jax.nn.sigmoid(gate) * up).astype(jnp.bfloat16)
        inner[:, part_of(block, model)] = mixed
        if keep:
            g_ref[:, part_of(block, model)] = gate.astype(jnp.bfloat16)
            u_ref[:, part_of(block, model)] = up.astype(jnp.bfloat16)
            z_t_ref[part_of(block, model), :] = jnp.transpose(mixed)
    total = hm_ref[...] + dot_plain(inner[...], slab(w_ref, 3 * rows, 3 * rows))
    low = total.astype(jnp.bfloat16)
    y_ref[...] = low
    if keep:
        error = low.astype(jnp.float32) - teacher_ref[...]
        pull = keep_ref[...] * error
        pull_ref[...] = pull
        square_ref[...] = jnp.sum(jnp.sum(pull * error, axis=0, keepdims=True), axis=1, keepdims=True)


def feed_forward(section, normed, middle, whole, target=()):
    tokens, model = normed.shape
    width = 3 * model
    shapes = [low_shape(tokens, model)]
    if target:
        shapes += [low_shape(tokens, width), low_shape(tokens, width), low_shape(width, tokens)]
        shapes += [full_shape(tokens, model), full_shape(1, 1)]
    return flat_call(
        functools.partial(ffn_kernel, bool(target)),
        (section, normed, middle, whole, *target),
        shapes,
        scratch=[pltpu.VMEM((tokens, width), jnp.bfloat16)],
        flops=6 * tokens * width * model,
        moved=6 * width * model + 8 * tokens * model,
    )


def ffn_back_kernel(
    section_ref, dy_ref, came_ref, hm_ref, gain_ref, g_ref, u_ref, w_ref, dh_ref, low_ref, dg_ref,
    du_ref, dgain_ref, low_dy_ref,
):
    devices, rows, model = w_ref.shape
    rows = rows // 9
    d_result = jnp.where(section_ref[0] == 1, dy_ref[...], came_ref[...].astype(jnp.float32))
    low_dy = d_result.astype(jnp.bfloat16)
    low_dy_ref[...] = low_dy
    chunks = 4
    owners = devices // chunks
    chunk = 3 * model // chunks
    for block in range(chunks):
        part = part_of(block, chunk)
        down = w_ref[block * owners : (block + 1) * owners, 3 * rows : 6 * rows, :]
        d_inner = dot_columns(low_dy, down.reshape(chunk, model))
        gate = g_ref[:, part].astype(jnp.float32)
        sigma = jax.nn.sigmoid(gate)
        silu = gate * sigma
        d_gate = d_inner * u_ref[:, part].astype(jnp.float32) * (sigma + silu * (1.0 - sigma))
        dg_ref[:, part] = d_gate.astype(jnp.bfloat16)
        du_ref[:, part] = (d_inner * silu).astype(jnp.bfloat16)
    grad = None
    for block in range(3):
        part = part_of(block, model)
        term = dot_columns(dg_ref[:, part], slab(w_ref, block * rows, rows))
        term = term + dot_columns(du_ref[:, part], slab(w_ref, (6 + block) * rows, rows))
        grad = term if grad is None else grad + term
    scaled, factor = unit_rows(hm_ref[...])
    dgain_ref[...] = jnp.sum(grad * scaled, axis=0, keepdims=True)
    d_result = jnp.where(section_ref[0] == 1, dy_ref[...], came_ref[...].astype(jnp.float32))
    d_hidden = d_result + norm_pull(grad, scaled, factor, gain_ref[...])
    dh_ref[...] = d_hidden
    low_ref[...] = d_hidden.astype(jnp.bfloat16)


def feed_forward_back(section, pull, came, middle, gains, gate, up, whole):
    tokens, model = middle.shape
    width = 3 * model
    return flat_call(
        ffn_back_kernel,
        (section, pull, came, middle, gains[3], gate, up, whole),
        [
            full_shape(tokens, model),
            low_shape(tokens, model),
            low_shape(tokens, width),
            low_shape(tokens, width),
            full_shape(1, model),
            low_shape(tokens, model),
        ],
        flops=6 * tokens * width * model,
        moved=6 * width * model + 14 * tokens * model + 8 * tokens * width,
    )


def attention_back_kernel(
    _, low_ref, dh_ref, h_ref, qkv_ref, pre_ref, gain_ref, gain_q_ref, gain_k_ref, cos_ref, sin_ref,
    row_ref, column_ref, w_ref, dq_ref, dkv_ref, dx_ref, dgain_ref, dgain_q_ref,
    dgain_k_ref, do_ref,
):
    tokens, model = h_ref.shape
    rows = w_ref.shape[1] // 6
    do_ref[...] = dot_columns(low_ref[...], slab(w_ref, 2 * rows, 2 * rows)).astype(jnp.bfloat16)
    causal = lax.broadcasted_iota(jnp.int32, (tokens, tokens), 0) <= lax.broadcasted_iota(
        jnp.int32, (tokens, tokens), 1
    )
    allowed = (row_ref[...] == column_ref[0]) & causal
    cosine, sine = cos_ref[...], sin_ref[...]
    scale = HEAD_SIZE ** (-0.5)
    gain_grads = [jnp.zeros((1, HEAD_SIZE), jnp.float32)] * 2

    def through_norm(grad, pre, gain_ref, which):
        gain = gain_ref[...]
        grad = grad * cosine - pltpu.roll(grad, HEAD_SIZE // 2, 1) * sine
        pre = pre.astype(jnp.float32)
        factor = lax.rsqrt(head_mean(pre * pre) + EPS)
        scaled = pre * factor
        gain_grads[which] = gain_grads[which] + jnp.sum(grad * scaled, axis=0, keepdims=True)
        pulled = grad * gain
        return (factor * (pulled - scaled * head_mean(pulled * scaled))).astype(jnp.bfloat16)

    for shared in range(KEY_VALUE_HEADS):
        lone = part_of(shared)
        key = qkv_ref[:, part_of(QUERY_HEADS + shared)]
        value = qkv_ref[:, part_of(QUERY_HEADS + KEY_VALUE_HEADS + shared)]
        d_key = d_value = None
        for head in range(2 * shared, 2 * shared + 2):
            part = part_of(head)
            query, d_mixed = qkv_ref[:, part], do_ref[:, part]
            scores = dot_columns(key, query) * scale
            raised = jnp.where(allowed, jnp.exp(scores), 0.0)
            weights = raised * (1.0 / jnp.sum(raised, axis=0, keepdims=True))
            value_term = dot_plain(weights.astype(jnp.bfloat16), d_mixed)
            d_weights = dot_columns(value, d_mixed)
            pulled = jnp.sum(d_weights * weights, axis=0, keepdims=True)
            d_scores = (weights * (d_weights - pulled)).astype(jnp.bfloat16)
            d_query = dot_rows(d_scores, key) * scale
            key_term = dot_plain(d_scores, query)
            d_key = key_term if d_key is None else d_key + key_term
            d_value = value_term if d_value is None else d_value + value_term
            dq_ref[:, part] = through_norm(d_query, pre_ref[:, part], gain_q_ref, 0)
        dkv_ref[:, lone] = through_norm(
            d_key * scale, pre_ref[:, part_of(QUERY_HEADS + shared)], gain_k_ref, 1
        )
        dkv_ref[:, part_of(KEY_VALUE_HEADS + shared)] = d_value.astype(jnp.bfloat16)
    dgain_q_ref[...], dgain_k_ref[...] = gain_grads
    grad = dot_columns(dq_ref[:, part_of(0, model)], slab(w_ref, 0, rows))
    grad = grad + dot_columns(dq_ref[:, part_of(1, model)], slab(w_ref, rows, rows))
    grad = grad + dot_columns(dkv_ref[:, part_of(0, model)], slab(w_ref, 4 * rows, rows))
    grad = grad + dot_columns(dkv_ref[:, part_of(1, model)], slab(w_ref, 5 * rows, rows))
    scaled, factor = unit_rows(h_ref[...].astype(jnp.float32))
    dgain_ref[...] = jnp.sum(grad * scaled, axis=0, keepdims=True)
    d_hidden = dh_ref[...] + norm_pull(grad, scaled, factor, gain_ref[...])
    dx_ref[...] = d_hidden.astype(jnp.bfloat16)


def attention_back(section, low, d_middle, hidden, qkv, pre, gains, tables, whole):
    tokens, model = hidden.shape
    wide = QUERY_HEADS * HEAD_SIZE
    return flat_call(
        attention_back_kernel,
        (section, low, d_middle, hidden, qkv, pre, *gains[:3], *tables, whole),
        [
            low_shape(tokens, wide),
            low_shape(tokens, 2 * model),
            low_shape(tokens, model),
            full_shape(1, model),
            full_shape(1, HEAD_SIZE),
            full_shape(1, HEAD_SIZE),
        ],
        scratch=[pltpu.VMEM((tokens, wide), jnp.bfloat16)],
        flops=2 * tokens * model * 6 * model + 20 * tokens * tokens * wide,
        moved=12 * model * model + 40 * tokens * model,
    )


def grad_kernel(plan, chips, batches, order_ref, *refs):
    side = order_ref[chips]
    count = sum(1 + len(entry[4]) for entry in plan) * batches
    target, stores = refs[count], refs[count + 1 :]
    model = target.shape[3]
    taken, start = 0, 0

    def take():
        nonlocal taken
        taken += batches
        return refs[taken - batches : taken]

    for (rows, size, low, blocks, choices), store in zip(plan, stores):
        left, rights = take(), [take() for _ in choices]
        first = side * low
        for t in range(chips):
            owner = 2 * order_ref[t]
            for core in range(2):
                place = pl.multiple_of((owner + core) * rows + first, 16)
                to = slice((2 * t + core) * size, (2 * t + core + 1) * size)
                for batch in range(batches):
                    store[batch, to, :] = left[batch][pl.ds(place, size), :]
        for block in range(blocks):
            part = part_of(block, model)
            right = []
            for batch in range(batches):
                value = rights[0][batch][:, part]
                if len(rights) > 1:
                    value = jnp.where(side == 0, value, rights[1][batch][:, part])
                right.append(value)
            for half in range(2):
                value = None
                span = slice(half * chips * size, (half + 1) * chips * size)
                for batch in range(batches):
                    term = dot_plain(store[batch, span, :], right[batch])
                    value = term if value is None else value + term
                value = value.astype(jnp.bfloat16).reshape(chips // 2, 2, size, model)
                into = slice(start + block * size, start + (block + 1) * size)
                target[half * chips // 2 : (half + 1) * chips // 2, :, into, :] = value
        start += blocks * size


def weight_grads(order, parts, model):
    batches = len(parts[0][0])
    tokens = parts[0][0][0].shape[1]
    chips = order.shape[0] - 1
    plan, scratch, operands, total = [], [], [], 0
    for left, rights, size, low in parts:
        rows = left[0].shape[0] // (2 * chips)
        blocks = rights[0][0].shape[1] // model
        plan.append((rows, size, low, blocks, tuple(range(len(rights)))))
        scratch.append(pltpu.VMEM((batches, 2 * chips * size, tokens), jnp.bfloat16))
        operands += list(left) + [array for right in rights for array in right]
        total += size * blocks
    return flat_call(
        functools.partial(grad_kernel, tuple(plan), chips, batches),
        (order, *operands),
        [low_shape(chips, 2, total, model)],
        scratch=scratch,
        flops=4 * chips * total * model * tokens * batches,
        moved=4 * chips * total * model + 8 * tokens * batches * model,
        vmem=14,
    )[0]


def pack_kernel(plan, count, *refs):
    target, sem = refs[count], refs[count + 1]
    model = target.shape[2]
    copies = []
    for half, entries in enumerate(plan):
        low = 0
        for source, start, rows, block in entries:
            copies.append(
                pltpu.make_async_copy(
                    refs[source].at[start : start + rows, part_of(block, model)],
                    target.at[half, low : low + rows, :],
                    sem.at[len(copies)],
                )
            )
            low += rows
    for copy in copies:
        copy.start()
    for copy in copies:
        copy.wait()


def pack(shards, plan, model):
    rows = sum(entry[2] for entry in plan[0])
    return pl.pallas_call(
        functools.partial(pack_kernel, plan, len(shards)),
        in_specs=[pl.BlockSpec(memory_space=pl.ANY)] * len(shards),
        out_specs=LOCAL,
        out_shape=low_shape(2, rows, model),
        scratch_shapes=[pltpu.SemaphoreType.DMA((len(plan[0]) + len(plan[1]),))],
        compiler_params=pltpu.CompilerParams(vmem_limit_bytes=VMEM_GRANT << 20),
    )(*shards)


def local(
    inputs,
    teacher,
    lengths,
    attn_query,
    attn_key,
    attn_value,
    attn_out,
    ffn_gate,
    ffn_up,
    ffn_down,
    norm_attn,
    norm_ffn,
    norm_query,
    norm_key,
):
    section = lax.axis_index("section")
    index = lax.axis_index("dp")
    devices = lax.axis_size("dp")
    chips = devices // 2
    batches, _, model = inputs.shape
    slots = lengths.shape[2]
    rows = attn_query.shape[1]
    forward_rows = ffn_down.shape[1]

    cut = forward_rows // 2 if forward_rows % 32 == 0 else 2 * rows
    attn_packed = pack(
        (attn_query[0], attn_out[0], attn_key[0], attn_value[0]),
        (
            ((0, 0, rows, 0), (0, 0, rows, 1), (1, 0, rows, 0)),
            ((1, rows, rows, 0), (2, 0, rows, 0), (3, 0, rows, 0)),
        ),
        model,
    )
    attn_whole, attn_marks = gather_ring(attn_packed, 6 * rows)
    (ffn_gate, ffn_up, ffn_down, lengths), _ = tie(
        (ffn_gate, ffn_up, ffn_down, lengths), attn_marks[0]
    )
    ffn_packed = pack(
        (ffn_gate[0], ffn_down[0], ffn_up[0]),
        (
            ((0, 0, rows, 0), (0, 0, rows, 1), (0, 0, rows, 2), (1, 0, cut, 0)),
            ((1, forward_rows - cut, cut, 0), (2, 0, rows, 0), (2, 0, rows, 1), (2, 0, rows, 2)),
        ),
        model,
    )
    ffn_whole, ffn_marks = gather_ring(
        ffn_packed, 9 * rows, attn_marks[min(RING_LEAD, chips - 2)]
    )

    gain_sizes = (norm_attn.shape[1], norm_query.shape[1], norm_key.shape[1], norm_ffn.shape[1])
    gain_shard = jnp.concatenate([norm_attn, norm_query, norm_key, norm_ffn], axis=1)
    gain_shard, _ = tie(gain_shard.astype(jnp.float32), attn_marks[min(2, chips - 2)])
    gain_whole = spread(gain_shard)
    gains, low = [], 0
    for size in gain_sizes:
        gains.append(gain_whole[:, low : low + size].reshape(1, devices * size))
        low += size

    segments, places = jax.vmap(layout)(lengths[:, 0, :])
    keep = (segments < slots - 1).astype(jnp.float32)
    tables = []
    for batch in range(batches):
        cosine_table, sine_table = rotary_tables(places[batch])
        tables.append(
            (
                jnp.concatenate([cosine_table, cosine_table], axis=1),
                jnp.concatenate([-sine_table, sine_table], axis=1),
                segments[batch].reshape(TOKENS_PER_SHARD, 1),
                segments[batch].reshape(1, 1, TOKENS_PER_SHARD),
            )
        )
    both = range(batches)

    def waiting(value, marks, step):
        return tie(value, marks[min(step, chips - 2)])[0]

    first = [inputs[batch] for batch in both]
    where = section[None].astype(jnp.int32)
    last = jnp.ones((1,), jnp.int32)
    carried, seen = [], []
    for batch in both:
        start = waiting(first[batch], ffn_marks, FIRST_WAIT + batch)
        seen.append(attention(where, start, start, gains, tables[batch], attn_whole, False))
    for batch in both:
        (result,) = feed_forward(where, seen[batch][1], seen[batch][0], ffn_whole)
        carried.append(one_way(result, 0))

    kept = []
    for batch in both:
        mid, norm, norm_t, normalized_t, mix_t, qkv, pre, hidden = attention(
            where, first[batch], carried[batch], gains, tables[batch], attn_whole, True
        )
        result, gate, up, inner_t, pull, square = feed_forward(
            where, norm, mid, ffn_whole, (teacher[batch], keep[batch][:, None])
        )
        kept.append(
            (hidden, normalized_t, qkv, pre, mix_t, mid, norm_t, result, gate, up, inner_t, pull, square)
        )
    (
        hidden, normalized_t, qkv, pre, mixed_t, middle, normed_t, result, gate, up, inner_t, pull,
        squares,
    ) = (list(column) for column in zip(*kept))

    core = index % 2
    place = ring_place(index // 2, chips)
    away = jnp.arange(chips, dtype=jnp.int32) * (2 * core - 1)
    order = jnp.concatenate([chip_at(place + away, chips), core[None]]).astype(jnp.int32)
    other_order = jnp.concatenate([chip_at(place - away, chips), 1 - core[None]]).astype(jnp.int32)

    incoming = []
    for batch in both:
        d_middle, d_attn = feed_forward_back(
            last, pull[batch], result[batch], middle[batch], gains, gate[batch], up[batch], ffn_whole
        )[:2]
        d_hidden = attention_back(
            where, d_attn, d_middle, hidden[batch], qkv[batch], pre[batch], gains, tables[batch],
            attn_whole,
        )[2]
        incoming.append(one_way(d_hidden, 1))

    d_middle, d_attn, d_gate, d_up, d_branch, gain_ffn = [], [], [], [], [], 0.0
    for batch in both:
        m, a, g, u, gain, low = feed_forward_back(
            where, pull[batch], incoming[batch], middle[batch], gains, gate[batch], up[batch],
            ffn_whole,
        )
        d_branch.append(low)
        d_middle.append(m)
        d_attn.append(a)
        d_gate.append(g)
        d_up.append(u)
        gain_ffn = gain_ffn + gain
    ffn_parts = [
        (normed_t, (d_gate, d_up), rows, 0),
        (inner_t, (d_branch,), cut, forward_rows - cut),
    ]
    theirs = weight_grads(other_order, ffn_parts, model)
    mine = weight_grads(tie(order, theirs)[0], ffn_parts, model)
    ffn_ring = ScatterRing(mine, theirs)
    ffn_ring.exchange()
    history = []
    run_slots([ffn_ring], history, SLOT_DEPTH)
    d_query, d_pair, d_hidden = [], [], []
    gain_attn, gain_query, gain_key = 0.0, 0.0, 0.0
    for batch in both:
        value, _ = tie(d_attn[batch], (ffn_ring.start, history[0])[batch])
        q, kv, x, gain_a, gain_q, gain_k = attention_back(
            where, value, d_middle[batch], hidden[batch], qkv[batch], pre[batch], gains,
            tables[batch], attn_whole,
        )
        d_query.append(q)
        d_pair.append(kv)
        d_hidden.append(x)
        gain_attn = gain_attn + gain_a
        gain_query = gain_query + gain_q
        gain_key = gain_key + gain_k
    gain_grads = (gain_attn, gain_query, gain_key, gain_ffn)
    run_slots([ffn_ring], history, SLOT_DEPTH)
    attn_parts = [
        (normalized_t, (d_query, d_pair), rows, 0),
        (mixed_t, (d_attn,), rows, rows),
    ]
    theirs = weight_grads(tie(other_order, history[1])[0], attn_parts, model)
    mine = weight_grads(tie(order, theirs)[0], attn_parts, model)
    run_slots([ffn_ring], history, SLOT_DEPTH)
    attn_ring = ScatterRing(mine, theirs)
    attn_ring.exchange()
    tail_mark = history[-1]
    while ffn_ring.step < chips or attn_ring.step < chips:
        run_slots([attn_ring, ffn_ring], history, SLOT_DEPTH)
        if attn_ring.step == 3:
            tail_mark = history[-1]

    first_half, second_half = ffn_ring.halves()
    grad_gate = beside(first_half, 0, 3, rows)
    grad_up = beside(second_half, 0, 3, rows)
    grad_down = jnp.concatenate(
        [first_half[3 * rows :], second_half[3 * rows + 2 * cut - forward_rows :]], axis=0
    )
    first_half, second_half = attn_ring.halves()
    grad_query = beside(first_half, 0, 2, rows)
    grad_key, grad_value = second_half[:rows], second_half[rows : 2 * rows]
    grad_out = jnp.concatenate([first_half[2 * rows :], second_half[2 * rows :]], axis=0)

    small = jnp.concatenate(
        [*gain_grads, sum(squares), jnp.sum(keep).reshape(1, 1)], axis=1
    )
    small_sum = summed(tie(small, tail_mark)[0])
    totals = small_sum[:, -2:]
    totals = jnp.where(section == 1, totals, one_way(totals, 1))[0]
    loss = totals[0] / (totals[1] * model)
    gain_grads, low = [], 0
    for size in gain_sizes:
        gain_grads.append(lax.dynamic_slice(small_sum, (0, low + index * size), (1, size)))
        low += devices * size
    grad_gain_attn, grad_gain_query, grad_gain_key, grad_gain_ffn = gain_grads

    half = batches // 2
    finals = jnp.stack(result)
    grads = jnp.stack(d_hidden)
    output = jnp.where(section == 0, one_way(finals[:half], 1), finals[half:])
    input_grad = jnp.where(section == 0, grads[:half], one_way(grads[half:], 0))
    return (
        output,
        loss,
        input_grad,
        grad_query[None],
        grad_key[None],
        grad_value[None],
        grad_out[None],
        grad_gate[None],
        grad_up[None],
        grad_down[None],
        grad_gain_attn,
        grad_gain_ffn,
        grad_gain_query,
        grad_gain_key,
    )


def solution(mesh):
    placed = (
        P(None, "dp", None),
        P(None, "dp", None),
        P(None, "dp", None),
        P("section", "dp", None),
        P("section", "dp", None),
        P("section", "dp", None),
        P("section", "dp", None),
        P("section", "dp", None),
        P("section", "dp", None),
        P("section", "dp", None),
        P("section", "dp"),
        P("section", "dp"),
        P("section", "dp"),
        P("section", "dp"),
    )
    return jax.shard_map(
        local,
        mesh=mesh,
        in_specs=placed,
        out_specs=(
            P("section", "dp", None),
            P(),
            P("section", "dp", None),
            P("section", "dp", None),
            P("section", "dp", None),
            P("section", "dp", None),
            P("section", "dp", None),
            P("section", "dp", None),
            P("section", "dp", None),
            P("section", "dp", None),
            P("section", "dp"),
            P("section", "dp"),
            P("section", "dp"),
            P("section", "dp"),
        ),
        check_vma=False,
    )
```

```python
import functools

import jax
import jax.numpy as jnp
from jax import lax
from jax.experimental import pallas as pl
from jax.experimental.pallas import tpu as pltpu
from jax.sharding import PartitionSpec as P

QUERY_HEADS = 16
KEY_VALUE_HEADS = 8
HEAD_SIZE = 128
TOKENS_PER_SHARD = 256


EPS = 1e-06
THETA = 1000000.0
NEGATIVE = -1e30
CONTRACT_ROWS = (((0,), (0,)), ((), ()))
CONTRACT_COLS = (((1,), (1,)), ((), ()))
SMALL_LAST = True
VMEM_GRANT = 10


def one_way(value, source):
    return lax.ppermute(value, "section", [(source, 1 - source)])


def chip_at(place, chips):
    place = lax.rem(place + 2 * chips, chips)
    return jnp.where(place < chips // 2, 2 * place, 2 * (chips - 1 - place) + 1)


def ring_place(chip, chips):
    return jnp.where(chip % 2 == 0, chip // 2, chips - 1 - chip // 2)


def ring_routes(devices):
    chips = devices // 2
    order = list(range(0, chips, 2)) + list(range(chips - 1, 0, -2))
    around = []
    for place in range(chips):
        here, there = order[place], order[(place + 1) % chips]
        around += [(2 * here, 2 * there), (2 * there + 1, 2 * here + 1)]
    return around, [(device, device ^ 1) for device in range(devices)]


def cycles(value):
    devices = lax.axis_size("dp")
    index = lax.axis_index("dp")
    width = 1
    while width < devices:
        base = min(4, devices // width)
        got = [value]
        for turn in range(1, base):
            route = []
            for low in range(devices):
                digit = low // width % base
                route.append((low, low + ((digit + turn) % base - digit) * width))
            got.append(lax.ppermute(value, "dp", route))
        value = yield got, index // width % base
        width *= base


def joined(got, digit):
    base, size = len(got), got[0].shape[0]
    turned = [got[-place % base] for place in range(base)] * 2
    start = (base - digit) % base * size
    return lax.dynamic_slice_in_dim(jnp.concatenate(turned, axis=0), start, base * size, 0)


class GatherRing:
    def __init__(self, packed):
        devices = lax.axis_size("dp")
        self.chips = devices // 2
        self.route, self.pair = ring_routes(devices)
        self.packed = packed
        self.other = lax.ppermute(packed, "dp", self.pair)
        core = lax.axis_index("dp") % 2
        self.pieces = [self.stack(core)]
        self.others = [self.stack(1 - core)]
        self.step = 1

    def stack(self, which):
        core = lax.axis_index("dp") % 2
        first = lax.dynamic_slice_in_dim(self.packed, which, 1, 0)
        second = lax.dynamic_slice_in_dim(self.other, which, 1, 0)
        return jnp.where(
            core == 0,
            jnp.concatenate([first, second], axis=0),
            jnp.concatenate([second, first], axis=0),
        )

    def advance(self, *before):
        value = self.pieces[-1]
        if before:
            value = self.pieces[-1] = hold(value, *before)
        self.pieces.append(lax.ppermute(value, "dp", self.route))
        self.swap(value)
        self.step += 1
        if self.step == self.chips:
            self.swap(self.pieces[-1])
        return self.pieces[-1]

    def swap(self, value):
        if len(self.pieces) > 2 or self.step == self.chips:
            self.others.append(lax.ppermute(value, "dp", self.pair))


class ScatterRing:
    def __init__(self, mine, theirs):
        devices = lax.axis_size("dp")
        self.chips = devices // 2
        self.route, self.pair = ring_routes(devices)
        self.mine = mine
        self.got = lax.ppermute(theirs, "dp", self.pair)
        value = mine[1].astype(jnp.float32) + self.got[1].astype(jnp.float32)
        self.value = value.astype(jnp.bfloat16)
        self.step = 1

    def advance(self, *before):
        if before:
            self.value = hold(self.value, *before)
        self.step += 1
        place = self.step % self.chips
        value = lax.ppermute(self.value, "dp", self.route).astype(jnp.float32)
        value = value + self.mine[place].astype(jnp.float32)
        value = value + self.got[place].astype(jnp.float32)
        self.value = value.astype(jnp.bfloat16) if self.step < self.chips else value
        return self.value

    def halves(self):
        core = lax.axis_index("dp") % 2
        own = lax.dynamic_index_in_dim(self.value, core, 0, keepdims=False)
        other = lax.dynamic_index_in_dim(self.value, 1 - core, 0, keepdims=False)
        other = lax.ppermute(other, "dp", self.pair)
        return jnp.where(core == 0, own, other), jnp.where(core == 0, other, own)


def beside(grad, low, pieces, rows):
    return jnp.concatenate(
        [grad[low + rows * i : low + rows * (i + 1)] for i in range(pieces)], axis=1
    )


def layout(lengths_row):
    ends = jnp.cumsum(lengths_row)
    places = jnp.arange(TOKENS_PER_SHARD, dtype=jnp.int32)
    passed = (ends[None, :] <= places[:, None]).astype(jnp.int32)
    segment_index = jnp.sum(passed, axis=1)
    start = jnp.sum(passed * lengths_row[None, :], axis=1)
    return (segment_index, places - start)


def rotary_tables(place):
    half = HEAD_SIZE // 2
    freqs = THETA ** (-(jnp.arange(half, dtype=jnp.float32) * 2.0 / HEAD_SIZE))
    angles = place.astype(jnp.float32)[:, None] * freqs[None, :]
    return (jnp.cos(angles), jnp.sin(angles))


LOCAL = pl.BlockSpec(memory_space=pltpu.VMEM)
SCALARS = pl.BlockSpec(memory_space=pltpu.SMEM)
ANYWHERE = pl.BlockSpec(memory_space=pl.ANY)


def hold(value, *after):
    return pl.pallas_call(
        lambda *refs: None,
        in_specs=[ANYWHERE] * (1 + len(after)),
        out_specs=ANYWHERE,
        out_shape=jax.ShapeDtypeStruct(value.shape, value.dtype),
        input_output_aliases={0: 0},
    )(value, *after)


def flat_call(body, arguments, out_shape, scratch=(), flops=0, moved=0, vmem=VMEM_GRANT, after=()):
    specs = [SCALARS] + [LOCAL] * (len(arguments) - 1) + [ANYWHERE] * len(after)
    count = len(arguments)

    def run(*refs):
        body(*refs[:count], *refs[count + len(after) :])

    return pl.pallas_call(
        run,
        in_specs=specs,
        out_specs=[LOCAL] * len(out_shape),
        out_shape=out_shape,
        scratch_shapes=list(scratch),
        compiler_params=pltpu.CompilerParams(vmem_limit_bytes=vmem << 20),
        cost_estimate=pl.CostEstimate(
            flops=int(flops), bytes_accessed=int(moved), transcendentals=0
        ),
    )(*arguments, *after)


def low_shape(*shape):
    return jax.ShapeDtypeStruct(shape, jnp.bfloat16)


def full_shape(*shape):
    return jax.ShapeDtypeStruct(shape, jnp.float32)


def dot_plain(left, right):
    return jnp.dot(left, right, preferred_element_type=jnp.float32)


def dot_columns(left, right):
    return lax.dot_general(left, right, CONTRACT_COLS, preferred_element_type=jnp.float32)


def dot_rows(left, right):
    return lax.dot_general(left, right, CONTRACT_ROWS, preferred_element_type=jnp.float32)


def unit_rows(values):
    factor = lax.rsqrt(jnp.mean(values * values, axis=-1, keepdims=True) + EPS)
    return values * factor, factor


def norm_pull(grad, scaled, factor, gain):
    pulled = grad * gain
    return factor * (pulled - scaled * jnp.mean(pulled * scaled, axis=-1, keepdims=True))


def head_mean(values):
    average = jnp.full((HEAD_SIZE, HEAD_SIZE), 1.0 / HEAD_SIZE, jnp.bfloat16)
    return dot_plain(values.astype(jnp.bfloat16), average)


def slab(ref, low, rows):
    value = ref[:, low : low + rows, :]
    return value.reshape(value.shape[0] * rows, value.shape[2])


def part_of(index, width=HEAD_SIZE):
    return slice(index * width, (index + 1) * width)


def attention_kernel(
    keep, section_ref, h_ref, came_ref, gain_ref, gain_q_ref, gain_k_ref, gain_ffn_ref, cos_ref,
    sin_ref, row_ref, column_ref, w_ref, hm_ref, xf_ref, *rest,
):
    if keep:
        xf_t_ref, xa_t_ref, o_t_ref, qkv_ref, pre_ref, hidden_ref, o_ref = rest
    else:
        qkv_ref, o_ref = rest
    tokens, model = h_ref.shape
    rows = w_ref.shape[1] // 6
    hidden = h_ref[...]
    if keep:
        hidden = jnp.where(section_ref[0] == 0, hidden, came_ref[...])
        hidden_ref[...] = hidden
    hidden = hidden.astype(jnp.float32)
    scaled, _ = unit_rows(hidden)
    xa = (scaled * gain_ref[...]).astype(jnp.bfloat16)
    cosine, sine = cos_ref[...], sin_ref[...]
    for block, low in enumerate((0, rows, 4 * rows, 5 * rows)):
        pre = dot_plain(xa, slab(w_ref, low, rows))
        if block == 3:
            qkv_ref[:, part_of(block, model)] = pre.astype(jnp.bfloat16)
            continue
        if keep:
            pre_ref[:, part_of(block, model)] = pre.astype(jnp.bfloat16)
        gain = gain_q_ref[...] if block < 2 else gain_k_ref[...]
        for head in range(model // HEAD_SIZE):
            value = pre[:, part_of(head)]
            value = value * lax.rsqrt(head_mean(value * value) + EPS) * gain
            value = value * cosine + pltpu.roll(value, HEAD_SIZE // 2, 1) * sine
            qkv_ref[:, part_of(block * (model // HEAD_SIZE) + head)] = value.astype(jnp.bfloat16)
    causal = lax.broadcasted_iota(jnp.int32, (tokens, tokens), 0) >= lax.broadcasted_iota(
        jnp.int32, (tokens, tokens), 1
    )
    allowed = (row_ref[...] == column_ref[0]) & causal
    ones = jnp.ones((tokens, HEAD_SIZE), jnp.bfloat16)
    for shared in range(KEY_VALUE_HEADS):
        key = qkv_ref[:, part_of(QUERY_HEADS + shared)]
        value = qkv_ref[:, part_of(QUERY_HEADS + KEY_VALUE_HEADS + shared)]
        value = jnp.concatenate([value, ones], axis=1)
        for head in range(2 * shared, 2 * shared + 2):
            scores = dot_columns(qkv_ref[:, part_of(head)], key) * HEAD_SIZE ** (-0.5)
            raised = jnp.where(allowed, jnp.exp(scores), 0.0).astype(jnp.bfloat16)
            mixed = dot_plain(raised, value)
            mixed = mixed[:, :HEAD_SIZE] / mixed[:, HEAD_SIZE:]
            o_ref[:, part_of(head)] = mixed.astype(jnp.bfloat16)
    middle = hidden + dot_plain(o_ref[...], slab(w_ref, 2 * rows, 2 * rows))
    hm_ref[...] = middle
    scaled, _ = unit_rows(middle)
    xf = (scaled * gain_ffn_ref[...]).astype(jnp.bfloat16)
    xf_ref[...] = xf
    if keep:
        xf_t_ref[...] = jnp.transpose(xf)
        xa_t_ref[...] = jnp.transpose(xa)
        o_t_ref[...] = jnp.transpose(o_ref[...])


def attention(section, hidden, came, gains, tables, whole, keep):
    tokens, model = hidden.shape
    wide = QUERY_HEADS * HEAD_SIZE
    shapes = [full_shape(tokens, model), low_shape(tokens, model)]
    scratch = [pltpu.VMEM((tokens, wide), jnp.bfloat16)]
    if keep:
        shapes += [
            low_shape(model, tokens),
            low_shape(model, tokens),
            low_shape(wide, tokens),
            low_shape(tokens, 4 * model),
            low_shape(tokens, 3 * model),
            low_shape(tokens, model),
        ]
    else:
        scratch = [pltpu.VMEM((tokens, 4 * model), jnp.bfloat16)] + scratch
    return flat_call(
        functools.partial(attention_kernel, keep),
        (section, hidden, came, *gains, *tables, whole),
        shapes,
        scratch=scratch,
        flops=2 * tokens * model * 6 * model + 8 * tokens * tokens * wide,
        moved=12 * model * model + 20 * tokens * model,
    )


def ffn_kernel(keep, _, xf_ref, hm_ref, w_ref, *rest):
    if keep:
        teacher_ref, keep_ref, y_ref, g_ref, u_ref, z_t_ref, pull_ref, square_ref, inner = rest
    else:
        y_ref, inner = rest
    tokens, model = xf_ref.shape
    rows = w_ref.shape[1] // 9
    xf = xf_ref[...]
    for block in range(3):
        gate = dot_plain(xf, slab(w_ref, block * rows, rows))
        up = dot_plain(xf, slab(w_ref, (6 + block) * rows, rows))
        mixed = (gate * jax.nn.sigmoid(gate) * up).astype(jnp.bfloat16)
        inner[:, part_of(block, model)] = mixed
        if keep:
            g_ref[:, part_of(block, model)] = gate.astype(jnp.bfloat16)
            u_ref[:, part_of(block, model)] = up.astype(jnp.bfloat16)
            z_t_ref[part_of(block, model), :] = jnp.transpose(mixed)
    total = hm_ref[...] + dot_plain(inner[...], slab(w_ref, 3 * rows, 3 * rows))
    low = total.astype(jnp.bfloat16)
    y_ref[...] = low
    if keep:
        error = low.astype(jnp.float32) - teacher_ref[...]
        pull = keep_ref[...] * error
        pull_ref[...] = pull
        square_ref[...] = jnp.sum(jnp.sum(pull * error, axis=0, keepdims=True), axis=1, keepdims=True)


def feed_forward(section, normed, middle, whole, target=()):
    tokens, model = normed.shape
    width = 3 * model
    shapes = [low_shape(tokens, model)]
    if target:
        shapes += [low_shape(tokens, width), low_shape(tokens, width), low_shape(width, tokens)]
        shapes += [full_shape(tokens, model), full_shape(1, 1)]
    return flat_call(
        functools.partial(ffn_kernel, bool(target)),
        (section, normed, middle, whole, *target),
        shapes,
        scratch=[pltpu.VMEM((tokens, width), jnp.bfloat16)],
        flops=6 * tokens * width * model,
        moved=6 * width * model + 8 * tokens * model,
    )


def ffn_back_kernel(
    section_ref, dy_ref, came_ref, hm_ref, gain_ref, g_ref, u_ref, w_ref, dh_ref, low_ref, dg_ref,
    du_ref, dgain_ref, low_dy_ref,
):
    devices, rows, model = w_ref.shape
    rows = rows // 9
    d_result = jnp.where(section_ref[0] == 1, dy_ref[...], came_ref[...].astype(jnp.float32))
    low_dy = d_result.astype(jnp.bfloat16)
    low_dy_ref[...] = low_dy
    chunks = 4
    owners = devices // chunks
    chunk = 3 * model // chunks
    for block in range(chunks):
        part = part_of(block, chunk)
        down = w_ref[block * owners : (block + 1) * owners, 3 * rows : 6 * rows, :]
        d_inner = dot_columns(low_dy, down.reshape(chunk, model))
        gate = g_ref[:, part].astype(jnp.float32)
        sigma = jax.nn.sigmoid(gate)
        silu = gate * sigma
        d_gate = d_inner * u_ref[:, part].astype(jnp.float32) * (sigma + silu * (1.0 - sigma))
        dg_ref[:, part] = d_gate.astype(jnp.bfloat16)
        du_ref[:, part] = (d_inner * silu).astype(jnp.bfloat16)
    grad = None
    for block in range(3):
        part = part_of(block, model)
        term = dot_columns(dg_ref[:, part], slab(w_ref, block * rows, rows))
        term = term + dot_columns(du_ref[:, part], slab(w_ref, (6 + block) * rows, rows))
        grad = term if grad is None else grad + term
    scaled, factor = unit_rows(hm_ref[...])
    dgain_ref[...] = jnp.sum(grad * scaled, axis=0, keepdims=True)
    d_result = jnp.where(section_ref[0] == 1, dy_ref[...], came_ref[...].astype(jnp.float32))
    d_hidden = d_result + norm_pull(grad, scaled, factor, gain_ref[...])
    dh_ref[...] = d_hidden
    low_ref[...] = d_hidden.astype(jnp.bfloat16)


def feed_forward_back(section, pull, came, middle, gains, gate, up, whole):
    tokens, model = middle.shape
    width = 3 * model
    return flat_call(
        ffn_back_kernel,
        (section, pull, came, middle, gains[3], gate, up, whole),
        [
            full_shape(tokens, model),
            low_shape(tokens, model),
            low_shape(tokens, width),
            low_shape(tokens, width),
            full_shape(1, model),
            low_shape(tokens, model),
        ],
        flops=6 * tokens * width * model,
        moved=6 * width * model + 14 * tokens * model + 8 * tokens * width,
    )


def attention_back_kernel(
    _, low_ref, dh_ref, h_ref, qkv_ref, pre_ref, gain_ref, gain_q_ref, gain_k_ref, cos_ref, sin_ref,
    row_ref, column_ref, w_ref, dq_ref, dkv_ref, dx_ref, dgain_ref, dgain_q_ref,
    dgain_k_ref, do_ref,
):
    tokens, model = h_ref.shape
    rows = w_ref.shape[1] // 6
    do_ref[...] = dot_columns(low_ref[...], slab(w_ref, 2 * rows, 2 * rows)).astype(jnp.bfloat16)
    causal = lax.broadcasted_iota(jnp.int32, (tokens, tokens), 0) <= lax.broadcasted_iota(
        jnp.int32, (tokens, tokens), 1
    )
    allowed = (row_ref[...] == column_ref[0]) & causal
    cosine, sine = cos_ref[...], sin_ref[...]
    scale = HEAD_SIZE ** (-0.5)
    gain_grads = [jnp.zeros((1, HEAD_SIZE), jnp.float32)] * 2

    def through_norm(grad, pre, gain_ref, which):
        gain = gain_ref[...]
        grad = grad * cosine - pltpu.roll(grad, HEAD_SIZE // 2, 1) * sine
        pre = pre.astype(jnp.float32)
        factor = lax.rsqrt(head_mean(pre * pre) + EPS)
        scaled = pre * factor
        gain_grads[which] = gain_grads[which] + jnp.sum(grad * scaled, axis=0, keepdims=True)
        pulled = grad * gain
        return (factor * (pulled - scaled * head_mean(pulled * scaled))).astype(jnp.bfloat16)

    for shared in range(KEY_VALUE_HEADS):
        lone = part_of(shared)
        key = qkv_ref[:, part_of(QUERY_HEADS + shared)]
        value = qkv_ref[:, part_of(QUERY_HEADS + KEY_VALUE_HEADS + shared)]
        d_key = d_value = None
        for head in range(2 * shared, 2 * shared + 2):
            part = part_of(head)
            query, d_mixed = qkv_ref[:, part], do_ref[:, part]
            scores = dot_columns(key, query) * scale
            raised = jnp.where(allowed, jnp.exp(scores), 0.0)
            weights = raised * (1.0 / jnp.sum(raised, axis=0, keepdims=True))
            value_term = dot_plain(weights.astype(jnp.bfloat16), d_mixed)
            d_weights = dot_columns(value, d_mixed)
            pulled = jnp.sum(d_weights * weights, axis=0, keepdims=True)
            d_scores = (weights * (d_weights - pulled)).astype(jnp.bfloat16)
            d_query = dot_rows(d_scores, key) * scale
            key_term = dot_plain(d_scores, query)
            d_key = key_term if d_key is None else d_key + key_term
            d_value = value_term if d_value is None else d_value + value_term
            dq_ref[:, part] = through_norm(d_query, pre_ref[:, part], gain_q_ref, 0)
        dkv_ref[:, lone] = through_norm(
            d_key * scale, pre_ref[:, part_of(QUERY_HEADS + shared)], gain_k_ref, 1
        )
        dkv_ref[:, part_of(KEY_VALUE_HEADS + shared)] = d_value.astype(jnp.bfloat16)
    dgain_q_ref[...], dgain_k_ref[...] = gain_grads
    grad = dot_columns(dq_ref[:, part_of(0, model)], slab(w_ref, 0, rows))
    grad = grad + dot_columns(dq_ref[:, part_of(1, model)], slab(w_ref, rows, rows))
    grad = grad + dot_columns(dkv_ref[:, part_of(0, model)], slab(w_ref, 4 * rows, rows))
    grad = grad + dot_columns(dkv_ref[:, part_of(1, model)], slab(w_ref, 5 * rows, rows))
    scaled, factor = unit_rows(h_ref[...].astype(jnp.float32))
    dgain_ref[...] = jnp.sum(grad * scaled, axis=0, keepdims=True)
    d_hidden = dh_ref[...] + norm_pull(grad, scaled, factor, gain_ref[...])
    dx_ref[...] = d_hidden.astype(jnp.bfloat16)


def attention_back(section, low, d_middle, hidden, qkv, pre, gains, tables, whole, after=()):
    tokens, model = hidden.shape
    wide = QUERY_HEADS * HEAD_SIZE
    return flat_call(
        attention_back_kernel,
        (section, low, d_middle, hidden, qkv, pre, *gains[:3], *tables, whole),
        [
            low_shape(tokens, wide),
            low_shape(tokens, 2 * model),
            low_shape(tokens, model),
            full_shape(1, model),
            full_shape(1, HEAD_SIZE),
            full_shape(1, HEAD_SIZE),
        ],
        scratch=[pltpu.VMEM((tokens, wide), jnp.bfloat16)],
        flops=2 * tokens * model * 6 * model + 20 * tokens * tokens * wide,
        moved=12 * model * model + 40 * tokens * model,
        after=after,
    )


def grad_kernel(plan, chips, batches, order_ref, *refs):
    count = sum(1 + len(entry[5]) for entry in plan) * batches
    targets, stores = refs[count : count + 2], refs[count + 2 :]
    model = targets[0].shape[3]
    for target, base in ((targets[0], 0), (targets[1], chips + 1)):
        side = order_ref[base + chips]
        taken, start = 0, 0
        for (rows, size, low, least, blocks, choices), store in zip(plan, stores):
            left = refs[taken : taken + batches]
            taken += batches
            rights = []
            for _ in choices:
                rights.append(refs[taken : taken + batches])
                taken += batches
            first = least + side * low
            for t in range(chips):
                owner = 2 * order_ref[base + t]
                for core in range(2):
                    place = pl.multiple_of((owner + core) * rows + first, 16)
                    to = slice((2 * t + core) * size, (2 * t + core + 1) * size)
                    for batch in range(batches):
                        store[batch, to, :] = left[batch][pl.ds(place, size), :]
            for block in range(blocks):
                part = part_of(block, model)
                right = []
                for batch in range(batches):
                    value = rights[0][batch][:, part]
                    if len(rights) > 1:
                        value = jnp.where(side == 0, value, rights[1][batch][:, part])
                    right.append(value)
                for half in range(2):
                    value = None
                    span = slice(half * chips * size, (half + 1) * chips * size)
                    for batch in range(batches):
                        term = dot_plain(store[batch, span, :], right[batch])
                        value = term if value is None else value + term
                    value = value.astype(jnp.bfloat16).reshape(chips // 2, 2, size, model)
                    into = slice(start + block * size, start + (block + 1) * size)
                    target[half * chips // 2 : (half + 1) * chips // 2, :, into, :] = value
            start += blocks * size


def weight_grads(orders, parts, model, after=()):
    batches = len(parts[0][0])
    tokens = parts[0][0][0].shape[1]
    chips = orders.shape[0] // 2 - 1
    plan, scratch, operands, total = [], [], [], 0
    for left, rights, size, low, least in parts:
        rows = left[0].shape[0] // (2 * chips)
        blocks = rights[0][0].shape[1] // model
        plan.append((rows, size, low, least, blocks, tuple(range(len(rights)))))
        scratch.append(pltpu.VMEM((batches, 2 * chips * size, tokens), jnp.bfloat16))
        operands += list(left) + [array for right in rights for array in right]
        total += size * blocks
    shape = low_shape(chips, 2, total, model)
    return flat_call(
        functools.partial(grad_kernel, tuple(plan), chips, batches),
        (orders, *operands),
        [shape, shape],
        scratch=scratch,
        flops=8 * chips * total * model * tokens * batches,
        moved=8 * chips * total * model + 8 * tokens * batches * model,
        vmem=14,
        after=after,
    )


def pack_kernel(plan, *refs):
    target, sem = refs[-2:]
    model = target.shape[2]
    copies = []
    for half, entries in enumerate(plan):
        low = 0
        for source, start, rows, block in entries:
            copies.append(
                pltpu.make_async_copy(
                    refs[source].at[start : start + rows, part_of(block, model)],
                    target.at[half, low : low + rows, :],
                    sem.at[len(copies)],
                )
            )
            low += rows
    for copy in copies:
        copy.start()
    for copy in copies:
        copy.wait()


def pack(shards, plan, model, after=()):
    rows = sum(entry[2] for entry in plan[0])
    return pl.pallas_call(
        functools.partial(pack_kernel, plan),
        in_specs=[ANYWHERE] * (len(shards) + len(after)),
        out_specs=LOCAL,
        out_shape=low_shape(2, rows, model),
        scratch_shapes=[pltpu.SemaphoreType.DMA((len(plan[0]) + len(plan[1]),))],
        compiler_params=pltpu.CompilerParams(vmem_limit_bytes=VMEM_GRANT << 20),
    )(*shards, *after)


def assemble_kernel(chips, plan, order_ref, *refs):
    target, sem = refs[-2:]
    copies = []
    for group, (low, rows, start, further) in enumerate(plan):
        for turn in range(2):
            base = turn * (chips + 1)
            place = pl.multiple_of(start + order_ref[base + chips] * further, 16)
            for t in range(chips):
                piece = refs[(2 * group + turn) * chips + t]
                copies.append(
                    pltpu.make_async_copy(
                        piece.at[:, low : low + rows, :],
                        target.at[pl.ds(2 * order_ref[base + t], 2), pl.ds(place, rows), :],
                        sem.at[len(copies)],
                    )
                )
    for copy in copies:
        copy.start()
    for copy in copies:
        copy.wait()


def assemble(orders, sources, rows):
    chips = sources[0][0].chips
    pieces = [piece for source in sources for piece in source[0].pieces + source[0].others]
    model = pieces[0].shape[2]
    return pl.pallas_call(
        functools.partial(assemble_kernel, chips, tuple(source[1:] for source in sources)),
        in_specs=[SCALARS] + [ANYWHERE] * len(pieces),
        out_specs=LOCAL,
        out_shape=low_shape(2 * chips, rows, model),
        scratch_shapes=[pltpu.SemaphoreType.DMA((len(pieces),))],
        compiler_params=pltpu.CompilerParams(vmem_limit_bytes=VMEM_GRANT << 20),
        cost_estimate=pl.CostEstimate(
            flops=0, bytes_accessed=8 * chips * rows * model, transcendentals=0
        ),
    )(orders, *pieces)


def local(
    inputs,
    teacher,
    lengths,
    attn_query,
    attn_key,
    attn_value,
    attn_out,
    ffn_gate,
    ffn_up,
    ffn_down,
    norm_attn,
    norm_ffn,
    norm_query,
    norm_key,
):
    section = lax.axis_index("section")
    index = lax.axis_index("dp")
    devices = lax.axis_size("dp")
    chips = devices // 2
    batches, _, model = inputs.shape
    slots = lengths.shape[2]
    rows = attn_query.shape[1]
    forward_rows = ffn_down.shape[1]

    cut = forward_rows // 2 if forward_rows % 32 == 0 else 2 * rows
    core = index % 2
    place = ring_place(index // 2, chips)
    away = jnp.arange(chips, dtype=jnp.int32) * (2 * core - 1)
    order = jnp.concatenate([chip_at(place + away, chips), core[None]]).astype(jnp.int32)
    other_order = jnp.concatenate([chip_at(place - away, chips), 1 - core[None]]).astype(jnp.int32)
    orders = jnp.concatenate([order, other_order])
    gain_sizes = (norm_attn.shape[1], norm_query.shape[1], norm_key.shape[1], norm_ffn.shape[1])
    gain_shard = jnp.concatenate([norm_attn, norm_query, norm_key, norm_ffn], axis=1)
    moved = cut // 2
    attn_packed = pack(
        (attn_query[0], attn_out[0], attn_key[0], attn_value[0]),
        (
            ((0, 0, rows, 0), (0, 0, rows, 1), (1, 0, rows, 0)),
            ((1, rows, rows, 0), (2, 0, rows, 0), (3, 0, rows, 0)),
        ),
        model,
    )
    ffn_packed = pack(
        (ffn_gate[0], ffn_down[0], ffn_up[0]),
        (
            ((0, 0, rows, 0), (0, 0, rows, 1), (0, 0, rows, 2), (1, 0, cut, 0)),
            (
                (1, forward_rows - cut, cut, 0),
                (2, 0, rows, 0),
                (2, 0, rows, 1),
                (2, 0, rows, 2),
            ),
        ),
        model,
    )
    segments, places = jax.vmap(layout)(lengths[:, 0, :])
    keep = (segments < slots - 1).astype(jnp.float32)
    tables = []
    for batch in range(batches):
        cosine_table, sine_table = rotary_tables(places[batch])
        tables.append(
            (
                jnp.concatenate([cosine_table, cosine_table], axis=1),
                jnp.concatenate([-sine_table, sine_table], axis=1),
                segments[batch].reshape(TOKENS_PER_SHARD, 1),
                segments[batch].reshape(1, 1, TOKENS_PER_SHARD),
            )
        )
    keep_columns = [keep[batch][:, None] for batch in range(batches)]
    early = [array for table in tables for array in table] + keep_columns + [orders]
    attn_ring = GatherRing(attn_packed)
    ffn_ring = GatherRing(ffn_packed)
    gain_rounds = cycles(gain_shard.astype(jnp.float32))
    got, digit = next(gain_rounds)
    attn_ring.advance()
    ffn_ring.advance()
    attn_ring.advance(*early)
    ffn_ring.advance(attn_ring.others[0], ffn_ring.others[0])
    while True:
        gain_whole = joined(got, digit)
        attn_ring.advance(gain_whole)
        ffn_ring.advance()
        try:
            got, digit = gain_rounds.send(gain_whole)
        except StopIteration:
            break
    gains, low = [], 0
    for size in gain_sizes:
        gains.append(gain_whole[:, low : low + size].reshape(1, devices * size))
        low += size

    attn_ring.advance(*gains)
    while ffn_ring.step < chips:
        ffn_ring.advance()
        if attn_ring.step < chips:
            attn_ring.advance()
    half = 3 * rows + cut
    ffn_low = 9 * rows - half
    attn_whole = assemble(orders, [(attn_ring, 0, 3 * rows, 0, 3 * rows)], 6 * rows)
    ffn_whole = assemble(orders, [(ffn_ring, 0, half, 0, ffn_low)], 9 * rows)
    both = range(batches)

    first = [inputs[batch] for batch in both]
    where = section[None].astype(jnp.int32)
    last = jnp.ones((1,), jnp.int32)
    carried, seen = [], []
    for batch in both:
        seen.append(attention(where, first[batch], first[batch], gains, tables[batch], attn_whole, False))
    for batch in both:
        (result,) = feed_forward(where, seen[batch][1], seen[batch][0], ffn_whole)
        carried.append(one_way(result, 0))

    kept = []
    for batch in both:
        mid, norm, norm_t, normalized_t, mix_t, qkv, pre, hidden = attention(
            where, first[batch], carried[batch], gains, tables[batch], attn_whole, True
        )
        result, gate, up, inner_t, pull, square = feed_forward(
            where, norm, mid, ffn_whole, (teacher[batch], keep_columns[batch])
        )
        kept.append(
            (hidden, normalized_t, qkv, pre, mix_t, mid, norm_t, result, gate, up, inner_t, pull, square)
        )
    (
        hidden, normalized_t, qkv, pre, mixed_t, middle, normed_t, result, gate, up, inner_t, pull,
        squares,
    ) = (list(column) for column in zip(*kept))

    incoming = []
    for batch in both:
        d_middle, d_attn = feed_forward_back(
            last, pull[batch], result[batch], middle[batch], gains, gate[batch], up[batch], ffn_whole
        )[:2]
        d_hidden = attention_back(
            where, d_attn, d_middle, hidden[batch], qkv[batch], pre[batch], gains, tables[batch],
            attn_whole,
        )[2]
        incoming.append(one_way(d_hidden, 1))

    d_middle, d_attn, d_gate, d_up, d_branch, gain_ffn = [], [], [], [], [], 0.0
    for batch in both:
        m, a, g, u, gain, low = feed_forward_back(
            where, pull[batch], incoming[batch], middle[batch], gains, gate[batch], up[batch],
            ffn_whole,
        )
        d_branch.append(low)
        d_middle.append(m)
        d_attn.append(a)
        d_gate.append(g)
        d_up.append(u)
        gain_ffn = gain_ffn + gain
    ffn_parts = [
        (normed_t, (d_gate, d_up), rows, 0, 0),
        (inner_t, (d_branch,), cut - moved, forward_rows - cut + moved, 0),
    ]
    their_orders = jnp.concatenate([other_order, order])
    d_query, d_pair, d_hidden = [], [], []
    gain_attn, gain_query, gain_key = 0.0, 0.0, 0.0
    for batch in both:
        if batch + 1 == batches:
            theirs, mine = weight_grads(their_orders, ffn_parts, model, tuple(d_query))
            ffn_ring = ScatterRing(mine, theirs)
        q, kv, x, gain_a, gain_q, gain_k = attention_back(
            where, d_attn[batch], d_middle[batch], hidden[batch], qkv[batch], pre[batch], gains,
            tables[batch], attn_whole, (mine,) if batch + 1 == batches else (),
        )
        d_query.append(q)
        d_pair.append(kv)
        d_hidden.append(x)
        gain_attn = gain_attn + gain_a
        gain_query = gain_query + gain_q
        gain_key = gain_key + gain_k
    gain_grads = (gain_attn, gain_query, gain_key, gain_ffn)
    attn_parts = [
        (normalized_t, (d_query, d_pair), rows, 0, 0),
        (mixed_t, (d_attn,), rows, rows, 0),
        (inner_t, (d_branch,), moved, forward_rows - 2 * cut + moved, cut - moved),
    ]
    theirs, mine = weight_grads(their_orders, attn_parts, model, (ffn_ring.value,))
    attn_ring = ScatterRing(mine, theirs)
    small = jnp.concatenate([*gain_grads, sum(squares), jnp.sum(keep).reshape(1, 1)], axis=1)
    small_rounds = cycles(small)
    got, _ = next(small_rounds)
    waits = []
    while ffn_ring.step < chips:
        ffn_ring.advance(*waits)
        attn_ring.advance()
        waits = []
        if ffn_ring.step % 2 == 1 and got is not None:
            small = sum(got)
            waits = [small]
            try:
                got, _ = small_rounds.send(small)
            except StopIteration:
                got = None
    while got is not None:
        small = sum(got)
        try:
            got, _ = small_rounds.send(small)
        except StopIteration:
            got = None

    ffn_first, ffn_second = ffn_ring.halves()
    attn_first, attn_second = attn_ring.halves()
    grad_gate = beside(ffn_first, 0, 3, rows)
    grad_up = beside(ffn_second, 0, 3, rows)
    grad_query = beside(attn_first, 0, 2, rows)
    grad_key, grad_value = attn_second[:rows], attn_second[rows : 2 * rows]
    grad_out = jnp.concatenate(
        [attn_first[2 * rows : 3 * rows], attn_second[2 * rows : 3 * rows]], axis=0
    )
    again = 3 * rows + max(0, 2 * cut - forward_rows)
    grad_down = jnp.concatenate(
        [ffn_first[3 * rows :], attn_first[3 * rows :], attn_second[again:], ffn_second[3 * rows :]],
        axis=0,
    )
    small_sum = small
    totals = small_sum[:, -2:]
    totals = jnp.where(section == 1, totals, one_way(totals, 1))[0]
    loss = totals[0] / (totals[1] * model)
    gain_grads, low = [], 0
    for size in gain_sizes:
        gain_grads.append(lax.dynamic_slice(small_sum, (0, low + index * size), (1, size)))
        low += devices * size
    grad_gain_attn, grad_gain_query, grad_gain_key, grad_gain_ffn = gain_grads

    half = batches // 2
    finals = jnp.stack(result)
    grads = jnp.stack(d_hidden)
    output = jnp.where(section == 0, one_way(finals[:half], 1), finals[half:])
    input_grad = jnp.where(section == 0, grads[:half], one_way(grads[half:], 0))
    return (
        output,
        loss,
        input_grad,
        grad_query[None],
        grad_key[None],
        grad_value[None],
        grad_out[None],
        grad_gate[None],
        grad_up[None],
        grad_down[None],
        grad_gain_attn,
        grad_gain_ffn,
        grad_gain_query,
        grad_gain_key,
    )


def solution(mesh):
    placed = (
        P(None, "dp", None),
        P(None, "dp", None),
        P(None, "dp", None),
        P("section", "dp", None),
        P("section", "dp", None),
        P("section", "dp", None),
        P("section", "dp", None),
        P("section", "dp", None),
        P("section", "dp", None),
        P("section", "dp", None),
        P("section", "dp"),
        P("section", "dp"),
        P("section", "dp"),
        P("section", "dp"),
    )
    return jax.shard_map(
        local,
        mesh=mesh,
        in_specs=placed,
        out_specs=(
            P("section", "dp", None),
            P(),
            P("section", "dp", None),
            P("section", "dp", None),
            P("section", "dp", None),
            P("section", "dp", None),
            P("section", "dp", None),
            P("section", "dp", None),
            P("section", "dp", None),
            P("section", "dp", None),
            P("section", "dp"),
            P("section", "dp"),
            P("section", "dp"),
            P("section", "dp"),
        ),
        check_vma=False,
    )
```

```python
import functools

import jax
import jax.numpy as jnp
from jax import lax
from jax.experimental import pallas as pl
from jax.experimental.pallas import tpu as pltpu
from jax.sharding import PartitionSpec as P

QUERY_HEADS = 16
KEY_VALUE_HEADS = 8
HEAD_SIZE = 128
TOKENS_PER_SHARD = 256


EPS = 1e-06
THETA = 1000000.0
NEGATIVE = -1e30
CONTRACT_ROWS = (((0,), (0,)), ((), ()))
CONTRACT_COLS = (((1,), (1,)), ((), ()))
GAIN_ROWS = 16
HOLD_FLOPS = 4400000000
SMALL_LAST = True
VMEM_GRANT = 8


def one_way(value, source):
    return lax.ppermute(value, "section", [(source, 1 - source)])


def chip_at(place, chips):
    place = lax.rem(place + 2 * chips, chips)
    return jnp.where(place < chips // 2, 2 * place, 2 * (chips - 1 - place) + 1)


def ring_place(chip, chips):
    return jnp.where(chip % 2 == 0, chip // 2, chips - 1 - chip // 2)


def ring_routes(devices):
    chips = devices // 2
    order = list(range(0, chips, 2)) + list(range(chips - 1, 0, -2))
    around = []
    for place in range(chips):
        here, there = order[place], order[(place + 1) % chips]
        around += [(2 * here, 2 * there), (2 * there + 1, 2 * here + 1)]
    return around, [(device, device ^ 1) for device in range(devices)]


def cycles(value):
    devices = lax.axis_size("dp")
    index = lax.axis_index("dp")
    width = 1
    while width < devices:
        base = min(4, devices // width)
        got = [value]
        for turn in range(1, base):
            route = []
            for low in range(devices):
                digit = low // width % base
                route.append((low, low + ((digit + turn) % base - digit) * width))
            got.append(lax.ppermute(value, "dp", route))
        value = yield got, index // width % base
        width *= base


class GatherRing:
    def __init__(self, packed, paced=False):
        self.paced = paced
        devices = lax.axis_size("dp")
        self.chips = devices // 2
        self.route, self.pair = ring_routes(devices)
        self.packed = packed
        self.other = lax.ppermute(packed, "dp", self.pair)
        core = lax.axis_index("dp") % 2
        self.pieces = [self.stack(core)]
        self.others = [self.stack(1 - core)]
        self.step = 1

    def stack(self, which):
        core = lax.axis_index("dp") % 2
        first = lax.dynamic_slice_in_dim(self.packed, which, 1, 0)
        second = lax.dynamic_slice_in_dim(self.other, which, 1, 0)
        return jnp.where(
            core == 0,
            jnp.concatenate([first, second], axis=0),
            jnp.concatenate([second, first], axis=0),
        )

    def advance(self, *before):
        value = self.pieces[-1]
        if before or self.paced and self.step > 1:
            value = self.pieces[-1] = hold(value, *before)
        self.pieces.append(lax.ppermute(value, "dp", self.route))
        self.swap(value)
        self.step += 1
        if self.step == self.chips:
            self.swap(self.pieces[-1])
        return self.pieces[-1]

    def swap(self, value):
        if len(self.pieces) > 2 or self.step == self.chips:
            self.others.append(lax.ppermute(value, "dp", self.pair))


class ScatterRing:
    def __init__(self, mine, theirs):
        devices = lax.axis_size("dp")
        self.chips = devices // 2
        self.route, self.pair = ring_routes(devices)
        self.mine = mine
        self.got = lax.ppermute(theirs, "dp", self.pair)
        value = mine[1].astype(jnp.float32) + self.got[1].astype(jnp.float32)
        self.value = value.astype(jnp.bfloat16)
        self.step = 1

    def advance(self, *before):
        if before:
            self.value = hold(self.value, *before)
        self.step += 1
        place = self.step % self.chips
        value = lax.ppermute(self.value, "dp", self.route).astype(jnp.float32)
        value = value + self.mine[place].astype(jnp.float32)
        value = value + self.got[place].astype(jnp.float32)
        self.value = value.astype(jnp.bfloat16) if self.step < self.chips else value
        return self.value

    def halves(self):
        core = lax.axis_index("dp") % 2
        own = lax.dynamic_index_in_dim(self.value, core, 0, keepdims=False)
        other = lax.dynamic_index_in_dim(self.value, 1 - core, 0, keepdims=False)
        other = lax.ppermute(other, "dp", self.pair)
        return jnp.where(core == 0, own, other), jnp.where(core == 0, other, own)


def beside(grad, low, pieces, rows):
    return jnp.concatenate(
        [grad[low + rows * i : low + rows * (i + 1)] for i in range(pieces)], axis=1
    )


def layout(lengths_row):
    ends = jnp.cumsum(lengths_row)
    places = jnp.arange(TOKENS_PER_SHARD, dtype=jnp.int32)
    passed = (ends[None, :] <= places[:, None]).astype(jnp.int32)
    segment_index = jnp.sum(passed, axis=1)
    start = jnp.sum(passed * lengths_row[None, :], axis=1)
    return (segment_index, places - start)


def rotary_tables(place):
    half = HEAD_SIZE // 2
    freqs = THETA ** (-(jnp.arange(half, dtype=jnp.float32) * 2.0 / HEAD_SIZE))
    angles = place.astype(jnp.float32)[:, None] * freqs[None, :]
    return (jnp.cos(angles), jnp.sin(angles))


LOCAL = pl.BlockSpec(memory_space=pltpu.VMEM)
SCALARS = pl.BlockSpec(memory_space=pltpu.SMEM)
ANYWHERE = pl.BlockSpec(memory_space=pl.ANY)


def hold(value, *after):
    return pl.pallas_call(
        lambda *refs: None,
        in_specs=[ANYWHERE] * (1 + len(after)),
        out_specs=ANYWHERE,
        out_shape=jax.ShapeDtypeStruct(value.shape, value.dtype),
        input_output_aliases={0: 0},
        cost_estimate=pl.CostEstimate(flops=HOLD_FLOPS, bytes_accessed=0, transcendentals=0),
    )(value, *after)


def flat_call(body, arguments, out_shape, scratch=(), flops=0, moved=0, vmem=VMEM_GRANT, after=()):
    specs = [SCALARS] + [LOCAL] * (len(arguments) - 1) + [ANYWHERE] * len(after)
    count = len(arguments)

    def run(*refs):
        body(*refs[:count], *refs[count + len(after) :])

    return pl.pallas_call(
        run,
        in_specs=specs,
        out_specs=[LOCAL] * len(out_shape),
        out_shape=out_shape,
        scratch_shapes=list(scratch),
        compiler_params=pltpu.CompilerParams(vmem_limit_bytes=vmem << 20),
        cost_estimate=pl.CostEstimate(
            flops=int(flops), bytes_accessed=int(moved), transcendentals=0
        ),
    )(*arguments, *after)


def low_shape(*shape):
    return jax.ShapeDtypeStruct(shape, jnp.bfloat16)


def full_shape(*shape):
    return jax.ShapeDtypeStruct(shape, jnp.float32)


def dot_plain(left, right):
    return jnp.dot(left, right, preferred_element_type=jnp.float32)


def dot_columns(left, right):
    return lax.dot_general(left, right, CONTRACT_COLS, preferred_element_type=jnp.float32)


def dot_rows(left, right):
    return lax.dot_general(left, right, CONTRACT_ROWS, preferred_element_type=jnp.float32)


def unit_rows(values):
    factor = lax.rsqrt(jnp.mean(values * values, axis=-1, keepdims=True) + EPS)
    return values * factor, factor


def norm_pull(grad, scaled, factor, gain):
    pulled = grad * gain
    return factor * (pulled - scaled * jnp.mean(pulled * scaled, axis=-1, keepdims=True))


def head_mean(values):
    average = jnp.full((HEAD_SIZE, HEAD_SIZE), 1.0 / HEAD_SIZE, jnp.bfloat16)
    return dot_plain(values.astype(jnp.bfloat16), average)


def slab(ref, low, rows):
    value = ref[:, low : low + rows, :]
    return value.reshape(value.shape[0] * rows, value.shape[2])


def part_of(index, width=HEAD_SIZE):
    return slice(index * width, (index + 1) * width)


def attention_kernel(
    keep, section_ref, h_ref, came_ref, gain_ref, gain_q_ref, gain_k_ref, gain_ffn_ref, cos_ref,
    sin_ref, row_ref, column_ref, w_ref, hm_ref, xf_ref, *rest,
):
    if keep:
        xf_t_ref, xa_t_ref, o_t_ref, qkv_ref, pre_ref, hidden_ref, o_ref = rest
    else:
        qkv_ref, o_ref = rest
    tokens, model = h_ref.shape
    rows = w_ref.shape[1] // 6
    hidden = h_ref[...]
    if keep:
        hidden = jnp.where(section_ref[0] == 0, hidden, came_ref[...])
        hidden_ref[...] = hidden
    hidden = hidden.astype(jnp.float32)
    scaled, _ = unit_rows(hidden)
    xa = (scaled * gain_ref[...]).astype(jnp.bfloat16)
    cosine, sine = cos_ref[...], sin_ref[...]
    for block, low in enumerate((0, rows, 4 * rows, 5 * rows)):
        pre = dot_plain(xa, slab(w_ref, low, rows))
        if block == 3:
            qkv_ref[:, part_of(block, model)] = pre.astype(jnp.bfloat16)
            continue
        if keep:
            pre_ref[:, part_of(block, model)] = pre.astype(jnp.bfloat16)
        gain = gain_q_ref[...] if block < 2 else gain_k_ref[...]
        for head in range(model // HEAD_SIZE):
            value = pre[:, part_of(head)]
            value = value * lax.rsqrt(head_mean(value * value) + EPS) * gain
            value = value * cosine + pltpu.roll(value, HEAD_SIZE // 2, 1) * sine
            qkv_ref[:, part_of(block * (model // HEAD_SIZE) + head)] = value.astype(jnp.bfloat16)
    causal = lax.broadcasted_iota(jnp.int32, (tokens, tokens), 0) >= lax.broadcasted_iota(
        jnp.int32, (tokens, tokens), 1
    )
    allowed = (row_ref[...] == column_ref[0]) & causal
    ones = jnp.ones((tokens, HEAD_SIZE), jnp.bfloat16)
    for shared in range(KEY_VALUE_HEADS):
        key = qkv_ref[:, part_of(QUERY_HEADS + shared)]
        value = qkv_ref[:, part_of(QUERY_HEADS + KEY_VALUE_HEADS + shared)]
        value = jnp.concatenate([value, ones], axis=1)
        for head in range(2 * shared, 2 * shared + 2):
            scores = dot_columns(qkv_ref[:, part_of(head)], key) * HEAD_SIZE ** (-0.5)
            raised = jnp.where(allowed, jnp.exp(scores), 0.0).astype(jnp.bfloat16)
            mixed = dot_plain(raised, value)
            mixed = mixed[:, :HEAD_SIZE] / mixed[:, HEAD_SIZE:]
            o_ref[:, part_of(head)] = mixed.astype(jnp.bfloat16)
    middle = hidden + dot_plain(o_ref[...], slab(w_ref, 2 * rows, 2 * rows))
    hm_ref[...] = middle
    scaled, _ = unit_rows(middle)
    xf = (scaled * gain_ffn_ref[...]).astype(jnp.bfloat16)
    xf_ref[...] = xf
    if keep:
        xf_t_ref[...] = jnp.transpose(xf)
        xa_t_ref[...] = jnp.transpose(xa)
        o_t_ref[...] = jnp.transpose(o_ref[...])


def attention(section, hidden, came, gains, tables, whole, keep):
    tokens, model = hidden.shape
    wide = QUERY_HEADS * HEAD_SIZE
    shapes = [full_shape(tokens, model), low_shape(tokens, model)]
    scratch = [pltpu.VMEM((tokens, wide), jnp.bfloat16)]
    if keep:
        shapes += [
            low_shape(model, tokens),
            low_shape(model, tokens),
            low_shape(wide, tokens),
            low_shape(tokens, 4 * model),
            low_shape(tokens, 3 * model),
            low_shape(tokens, model),
        ]
    else:
        scratch = [pltpu.VMEM((tokens, 4 * model), jnp.bfloat16)] + scratch
    return flat_call(
        functools.partial(attention_kernel, keep),
        (section, hidden, came, *gains, *tables, whole),
        shapes,
        scratch=scratch,
        flops=2 * tokens * model * 6 * model + 8 * tokens * tokens * wide,
        moved=12 * model * model + 20 * tokens * model,
    )


def ffn_kernel(keep, _, xf_ref, hm_ref, w_ref, *rest):
    if keep:
        teacher_ref, keep_ref, y_ref, g_ref, u_ref, z_t_ref, pull_ref, square_ref, inner = rest
    else:
        y_ref, inner = rest
    tokens, model = xf_ref.shape
    rows = w_ref.shape[1] // 9
    xf = xf_ref[...]
    for block in range(3):
        gate = dot_plain(xf, slab(w_ref, block * rows, rows))
        up = dot_plain(xf, slab(w_ref, (6 + block) * rows, rows))
        mixed = (gate * jax.nn.sigmoid(gate) * up).astype(jnp.bfloat16)
        inner[:, part_of(block, model)] = mixed
        if keep:
            g_ref[:, part_of(block, model)] = gate.astype(jnp.bfloat16)
            u_ref[:, part_of(block, model)] = up.astype(jnp.bfloat16)
            z_t_ref[part_of(block, model), :] = jnp.transpose(mixed)
    total = hm_ref[...] + dot_plain(inner[...], slab(w_ref, 3 * rows, 3 * rows))
    low = total.astype(jnp.bfloat16)
    y_ref[...] = low
    if keep:
        error = low.astype(jnp.float32) - teacher_ref[...]
        pull = keep_ref[...] * error
        pull_ref[...] = pull
        square_ref[...] = jnp.sum(jnp.sum(pull * error, axis=0, keepdims=True), axis=1, keepdims=True)


def feed_forward(section, normed, middle, whole, target=()):
    tokens, model = normed.shape
    width = 3 * model
    shapes = [low_shape(tokens, model)]
    if target:
        shapes += [low_shape(tokens, width), low_shape(tokens, width), low_shape(width, tokens)]
        shapes += [full_shape(tokens, model), full_shape(1, 1)]
    return flat_call(
        functools.partial(ffn_kernel, bool(target)),
        (section, normed, middle, whole, *target),
        shapes,
        scratch=[pltpu.VMEM((tokens, width), jnp.bfloat16)],
        flops=6 * tokens * width * model,
        moved=6 * width * model + 8 * tokens * model,
    )


def ffn_back_kernel(
    section_ref, dy_ref, came_ref, hm_ref, gain_ref, g_ref, u_ref, w_ref, dh_ref, low_ref, dg_ref,
    du_ref, dgain_ref, low_dy_ref,
):
    devices, rows, model = w_ref.shape
    rows = rows // 9
    d_result = jnp.where(section_ref[0] == 1, dy_ref[...], came_ref[...].astype(jnp.float32))
    low_dy = d_result.astype(jnp.bfloat16)
    low_dy_ref[...] = low_dy
    chunks = 4
    owners = devices // chunks
    chunk = 3 * model // chunks
    for block in range(chunks):
        part = part_of(block, chunk)
        down = w_ref[block * owners : (block + 1) * owners, 3 * rows : 6 * rows, :]
        d_inner = dot_columns(low_dy, down.reshape(chunk, model))
        gate = g_ref[:, part].astype(jnp.float32)
        sigma = jax.nn.sigmoid(gate)
        silu = gate * sigma
        d_gate = d_inner * u_ref[:, part].astype(jnp.float32) * (sigma + silu * (1.0 - sigma))
        dg_ref[:, part] = d_gate.astype(jnp.bfloat16)
        du_ref[:, part] = (d_inner * silu).astype(jnp.bfloat16)
    grad = None
    for block in range(3):
        part = part_of(block, model)
        term = dot_columns(dg_ref[:, part], slab(w_ref, block * rows, rows))
        term = term + dot_columns(du_ref[:, part], slab(w_ref, (6 + block) * rows, rows))
        grad = term if grad is None else grad + term
    scaled, factor = unit_rows(hm_ref[...])
    dgain_ref[...] = jnp.sum(grad * scaled, axis=0, keepdims=True)
    d_result = jnp.where(section_ref[0] == 1, dy_ref[...], came_ref[...].astype(jnp.float32))
    d_hidden = d_result + norm_pull(grad, scaled, factor, gain_ref[...])
    dh_ref[...] = d_hidden
    low_ref[...] = d_hidden.astype(jnp.bfloat16)


def feed_forward_back(section, pull, came, middle, gains, gate, up, whole):
    tokens, model = middle.shape
    width = 3 * model
    return flat_call(
        ffn_back_kernel,
        (section, pull, came, middle, gains[3], gate, up, whole),
        [
            full_shape(tokens, model),
            low_shape(tokens, model),
            low_shape(tokens, width),
            low_shape(tokens, width),
            full_shape(1, model),
            low_shape(tokens, model),
        ],
        flops=6 * tokens * width * model,
        moved=6 * width * model + 14 * tokens * model + 8 * tokens * width,
    )


def attention_back_kernel(
    _, low_ref, dh_ref, h_ref, qkv_ref, pre_ref, gain_ref, gain_q_ref, gain_k_ref, cos_ref, sin_ref,
    row_ref, column_ref, w_ref, dq_ref, dkv_ref, dx_ref, dgain_ref, dgain_q_ref,
    dgain_k_ref, do_ref,
):
    tokens, model = h_ref.shape
    rows = w_ref.shape[1] // 6
    do_ref[...] = dot_columns(low_ref[...], slab(w_ref, 2 * rows, 2 * rows)).astype(jnp.bfloat16)
    causal = lax.broadcasted_iota(jnp.int32, (tokens, tokens), 0) <= lax.broadcasted_iota(
        jnp.int32, (tokens, tokens), 1
    )
    allowed = (row_ref[...] == column_ref[0]) & causal
    cosine, sine = cos_ref[...], sin_ref[...]
    scale = HEAD_SIZE ** (-0.5)
    gain_grads = [jnp.zeros((1, HEAD_SIZE), jnp.float32)] * 2

    def through_norm(grad, pre, gain_ref, which):
        gain = gain_ref[...]
        grad = grad * cosine - pltpu.roll(grad, HEAD_SIZE // 2, 1) * sine
        pre = pre.astype(jnp.float32)
        factor = lax.rsqrt(head_mean(pre * pre) + EPS)
        scaled = pre * factor
        gain_grads[which] = gain_grads[which] + jnp.sum(grad * scaled, axis=0, keepdims=True)
        pulled = grad * gain
        return (factor * (pulled - scaled * head_mean(pulled * scaled))).astype(jnp.bfloat16)

    for shared in range(KEY_VALUE_HEADS):
        lone = part_of(shared)
        key = qkv_ref[:, part_of(QUERY_HEADS + shared)]
        value = qkv_ref[:, part_of(QUERY_HEADS + KEY_VALUE_HEADS + shared)]
        d_key = d_value = None
        for head in range(2 * shared, 2 * shared + 2):
            part = part_of(head)
            query, d_mixed = qkv_ref[:, part], do_ref[:, part]
            scores = dot_columns(key, query) * scale
            raised = jnp.where(allowed, jnp.exp(scores), 0.0)
            weights = raised * (1.0 / jnp.sum(raised, axis=0, keepdims=True))
            value_term = dot_plain(weights.astype(jnp.bfloat16), d_mixed)
            d_weights = dot_columns(value, d_mixed)
            pulled = jnp.sum(d_weights * weights, axis=0, keepdims=True)
            d_scores = (weights * (d_weights - pulled)).astype(jnp.bfloat16)
            d_query = dot_rows(d_scores, key) * scale
            key_term = dot_plain(d_scores, query)
            d_key = key_term if d_key is None else d_key + key_term
            d_value = value_term if d_value is None else d_value + value_term
            dq_ref[:, part] = through_norm(d_query, pre_ref[:, part], gain_q_ref, 0)
        dkv_ref[:, lone] = through_norm(
            d_key * scale, pre_ref[:, part_of(QUERY_HEADS + shared)], gain_k_ref, 1
        )
        dkv_ref[:, part_of(KEY_VALUE_HEADS + shared)] = d_value.astype(jnp.bfloat16)
    dgain_q_ref[...], dgain_k_ref[...] = gain_grads
    grad = dot_columns(dq_ref[:, part_of(0, model)], slab(w_ref, 0, rows))
    grad = grad + dot_columns(dq_ref[:, part_of(1, model)], slab(w_ref, rows, rows))
    grad = grad + dot_columns(dkv_ref[:, part_of(0, model)], slab(w_ref, 4 * rows, rows))
    grad = grad + dot_columns(dkv_ref[:, part_of(1, model)], slab(w_ref, 5 * rows, rows))
    scaled, factor = unit_rows(h_ref[...].astype(jnp.float32))
    dgain_ref[...] = jnp.sum(grad * scaled, axis=0, keepdims=True)
    d_hidden = dh_ref[...] + norm_pull(grad, scaled, factor, gain_ref[...])
    dx_ref[...] = d_hidden.astype(jnp.bfloat16)


def attention_back(section, low, d_middle, hidden, qkv, pre, gains, tables, whole, after=()):
    tokens, model = hidden.shape
    wide = QUERY_HEADS * HEAD_SIZE
    return flat_call(
        attention_back_kernel,
        (section, low, d_middle, hidden, qkv, pre, *gains[:3], *tables, whole),
        [
            low_shape(tokens, wide),
            low_shape(tokens, 2 * model),
            low_shape(tokens, model),
            full_shape(1, model),
            full_shape(1, HEAD_SIZE),
            full_shape(1, HEAD_SIZE),
        ],
        scratch=[pltpu.VMEM((tokens, wide), jnp.bfloat16)],
        flops=2 * tokens * model * 6 * model + 20 * tokens * tokens * wide,
        moved=12 * model * model + 40 * tokens * model,
        after=after,
    )


def grad_kernel(plan, chips, batches, order_ref, *refs):
    count = sum(1 + len(entry[5]) for entry in plan) * batches
    targets, stores = refs[count : count + 2], refs[count + 2 :]
    model = targets[0].shape[3]
    for target, base in ((targets[0], 0), (targets[1], chips + 1)):
        side = order_ref[base + chips]
        taken, start = 0, 0
        for (rows, size, low, least, blocks, choices), store in zip(plan, stores):
            left = refs[taken : taken + batches]
            taken += batches
            rights = []
            for _ in choices:
                rights.append(refs[taken : taken + batches])
                taken += batches
            first = least + side * low
            for t in range(chips):
                owner = 2 * order_ref[base + t]
                for core in range(2):
                    place = pl.multiple_of((owner + core) * rows + first, 16)
                    to = slice((2 * t + core) * size, (2 * t + core + 1) * size)
                    for batch in range(batches):
                        store[batch, to, :] = left[batch][pl.ds(place, size), :]
            for block in range(blocks):
                part = part_of(block, model)
                right = []
                for batch in range(batches):
                    value = rights[0][batch][:, part]
                    if len(rights) > 1:
                        value = jnp.where(side == 0, value, rights[1][batch][:, part])
                    right.append(value)
                for half in range(2):
                    value = None
                    span = slice(half * chips * size, (half + 1) * chips * size)
                    for batch in range(batches):
                        term = dot_plain(store[batch, span, :], right[batch])
                        value = term if value is None else value + term
                    value = value.astype(jnp.bfloat16).reshape(chips // 2, 2, size, model)
                    into = slice(start + block * size, start + (block + 1) * size)
                    target[half * chips // 2 : (half + 1) * chips // 2, :, into, :] = value
            start += blocks * size


def weight_grads(orders, parts, model, after=()):
    batches = len(parts[0][0])
    tokens = parts[0][0][0].shape[1]
    chips = orders.shape[0] // 2 - 1
    plan, scratch, operands, total = [], [], [], 0
    for left, rights, size, low, least in parts:
        rows = left[0].shape[0] // (2 * chips)
        blocks = rights[0][0].shape[1] // model
        plan.append((rows, size, low, least, blocks, tuple(range(len(rights)))))
        scratch.append(pltpu.VMEM((batches, 2 * chips * size, tokens), jnp.bfloat16))
        operands += list(left) + [array for right in rights for array in right]
        total += size * blocks
    shape = low_shape(chips, 2, total, model)
    return flat_call(
        functools.partial(grad_kernel, tuple(plan), chips, batches),
        (orders, *operands),
        [shape, shape],
        scratch=scratch,
        flops=8 * chips * total * model * tokens * batches,
        moved=8 * chips * total * model + 8 * tokens * batches * model,
        vmem=14,
        after=after,
    )


def pack_kernel(plan, *refs):
    target, sem = refs[-2:]
    model = target.shape[2]
    copies = []
    for half, entries in enumerate(plan):
        low = 0
        for source, start, rows, block in entries:
            copies.append(
                pltpu.make_async_copy(
                    refs[source].at[start : start + rows, part_of(block, model)],
                    target.at[half, low : low + rows, :],
                    sem.at[len(copies)],
                )
            )
            low += rows
    for copy in copies:
        copy.start()
    for copy in copies:
        copy.wait()


def pack(shards, plan, model, after=()):
    rows = sum(entry[2] for entry in plan[0])
    return pl.pallas_call(
        functools.partial(pack_kernel, plan),
        in_specs=[ANYWHERE] * (len(shards) + len(after)),
        out_specs=LOCAL,
        out_shape=low_shape(2, rows, model),
        scratch_shapes=[pltpu.SemaphoreType.DMA((len(plan[0]) + len(plan[1]),))],
        compiler_params=pltpu.CompilerParams(vmem_limit_bytes=VMEM_GRANT << 20),
    )(*shards, *after)


def assemble_kernel(chips, plan, order_ref, *refs):
    target, sem = refs[-2:]
    copies = []
    for group, (low, rows, start, further) in enumerate(plan):
        for turn in range(2):
            base = turn * (chips + 1)
            place = pl.multiple_of(start + order_ref[base + chips] * further, 16)
            for t in range(chips):
                piece = refs[(2 * group + turn) * chips + t]
                copies.append(
                    pltpu.make_async_copy(
                        piece.at[:, low : low + rows, :],
                        target.at[pl.ds(2 * order_ref[base + t], 2), pl.ds(place, rows), :],
                        sem.at[len(copies)],
                    )
                )
    for copy in copies:
        copy.start()
    for copy in copies:
        copy.wait()


def assemble(orders, sources, rows):
    chips = sources[0][0].chips
    pieces = [piece for source in sources for piece in source[0].pieces + source[0].others]
    model = pieces[0].shape[2]
    return pl.pallas_call(
        functools.partial(assemble_kernel, chips, tuple(source[1:] for source in sources)),
        in_specs=[SCALARS] + [ANYWHERE] * len(pieces),
        out_specs=LOCAL,
        out_shape=low_shape(2 * chips, rows, model),
        scratch_shapes=[pltpu.SemaphoreType.DMA((len(pieces),))],
        compiler_params=pltpu.CompilerParams(vmem_limit_bytes=VMEM_GRANT << 20),
        cost_estimate=pl.CostEstimate(
            flops=0, bytes_accessed=8 * chips * rows * model, transcendentals=0
        ),
    )(orders, *pieces)


def local(
    inputs,
    teacher,
    lengths,
    attn_query,
    attn_key,
    attn_value,
    attn_out,
    ffn_gate,
    ffn_up,
    ffn_down,
    norm_attn,
    norm_ffn,
    norm_query,
    norm_key,
):
    section = lax.axis_index("section")
    index = lax.axis_index("dp")
    devices = lax.axis_size("dp")
    chips = devices // 2
    batches, _, model = inputs.shape
    slots = lengths.shape[2]
    rows = attn_query.shape[1]
    forward_rows = ffn_down.shape[1]

    cut = forward_rows // 2 if forward_rows % 32 == 0 else 2 * rows
    core = index % 2
    place = ring_place(index // 2, chips)
    away = jnp.arange(chips, dtype=jnp.int32) * (2 * core - 1)
    order = jnp.concatenate([chip_at(place + away, chips), core[None]]).astype(jnp.int32)
    other_order = jnp.concatenate([chip_at(place - away, chips), 1 - core[None]]).astype(jnp.int32)
    orders = jnp.concatenate([order, other_order])
    gain_sizes = (norm_attn.shape[1], norm_query.shape[1], norm_key.shape[1], norm_ffn.shape[1])
    gain_shard = jnp.concatenate([norm_attn, norm_query, norm_key, norm_ffn], axis=1)
    gain_count = gain_shard.shape[1]
    gain_shard = jnp.pad(gain_shard, ((0, GAIN_ROWS - 1), (0, model - gain_count)))
    moved = cut // 2
    attn_packed = pack(
        (attn_query[0], attn_out[0], attn_key[0], attn_value[0], gain_shard),
        (
            ((0, 0, rows, 0), (0, 0, rows, 1), (1, 0, rows, 0), (4, 0, GAIN_ROWS, 0)),
            ((1, rows, rows, 0), (2, 0, rows, 0), (3, 0, rows, 0), (4, 0, GAIN_ROWS, 0)),
        ),
        model,
    )
    ffn_packed = pack(
        (ffn_gate[0], ffn_down[0], ffn_up[0]),
        (
            ((0, 0, rows, 0), (0, 0, rows, 1), (0, 0, rows, 2), (1, 0, cut, 0)),
            (
                (1, forward_rows - cut, cut, 0),
                (2, 0, rows, 0),
                (2, 0, rows, 1),
                (2, 0, rows, 2),
            ),
        ),
        model,
    )
    segments, places = jax.vmap(layout)(lengths[:, 0, :])
    keep = (segments < slots - 1).astype(jnp.float32)
    tables = []
    for batch in range(batches):
        cosine_table, sine_table = rotary_tables(places[batch])
        tables.append(
            (
                jnp.concatenate([cosine_table, cosine_table], axis=1),
                jnp.concatenate([-sine_table, sine_table], axis=1),
                segments[batch].reshape(TOKENS_PER_SHARD, 1),
                segments[batch].reshape(1, 1, TOKENS_PER_SHARD),
            )
        )
    keep_columns = [keep[batch][:, None] for batch in range(batches)]
    first = [inputs[batch] for batch in range(batches)]
    target = [teacher[batch] for batch in range(batches)]
    early = [array for table in tables for array in table] + keep_columns + first + target + [orders]
    attn_ring = GatherRing(attn_packed, True)
    ffn_ring = GatherRing(ffn_packed)
    attn_ring.advance()
    ffn_ring.advance()
    attn_ring.advance(*early)
    ffn_ring.advance(attn_ring.others[0], ffn_ring.others[0])
    while ffn_ring.step < chips:
        attn_ring.advance()
        ffn_ring.advance()
    carried_gains = jnp.stack([piece[:, 3 * rows, :gain_count] for piece in attn_ring.pieces])
    chip = jnp.arange(chips, dtype=jnp.int32)
    found = lax.rem((2 * core - 1) * (ring_place(chip, chips) - place) + chips, chips)
    gain_whole = jnp.take(carried_gains, found, axis=0).reshape(devices, gain_count)
    gain_whole = gain_whole.astype(jnp.float32)
    gains, low = [], 0
    for size in gain_sizes:
        gains.append(gain_whole[:, low : low + size].reshape(1, devices * size))
        low += size

    half = 3 * rows + cut
    ffn_low = 9 * rows - half
    attn_whole = assemble(orders, [(attn_ring, 0, 3 * rows, 0, 3 * rows)], 6 * rows)
    ffn_whole = assemble(orders, [(ffn_ring, 0, half, 0, ffn_low)], 9 * rows)
    both = range(batches)

    where = section[None].astype(jnp.int32)
    last = jnp.ones((1,), jnp.int32)
    carried, seen = [], []
    for batch in both:
        seen.append(attention(where, first[batch], first[batch], gains, tables[batch], attn_whole, False))
    for batch in both:
        (result,) = feed_forward(where, seen[batch][1], seen[batch][0], ffn_whole)
        carried.append(one_way(result, 0))

    kept = []
    for batch in both:
        mid, norm, norm_t, normalized_t, mix_t, qkv, pre, hidden = attention(
            where, first[batch], carried[batch], gains, tables[batch], attn_whole, True
        )
        result, gate, up, inner_t, pull, square = feed_forward(
            where, norm, mid, ffn_whole, (target[batch], keep_columns[batch])
        )
        kept.append(
            (hidden, normalized_t, qkv, pre, mix_t, mid, norm_t, result, gate, up, inner_t, pull, square)
        )
    (
        hidden, normalized_t, qkv, pre, mixed_t, middle, normed_t, result, gate, up, inner_t, pull,
        squares,
    ) = (list(column) for column in zip(*kept))

    incoming = []
    for batch in both:
        d_middle, d_attn = feed_forward_back(
            last, pull[batch], result[batch], middle[batch], gains, gate[batch], up[batch], ffn_whole
        )[:2]
        d_hidden = attention_back(
            where, d_attn, d_middle, hidden[batch], qkv[batch], pre[batch], gains, tables[batch],
            attn_whole,
        )[2]
        incoming.append(one_way(d_hidden, 1))

    d_middle, d_attn, d_gate, d_up, d_branch, gain_ffn = [], [], [], [], [], 0.0
    for batch in both:
        m, a, g, u, gain, low = feed_forward_back(
            where, pull[batch], incoming[batch], middle[batch], gains, gate[batch], up[batch],
            ffn_whole,
        )
        d_branch.append(low)
        d_middle.append(m)
        d_attn.append(a)
        d_gate.append(g)
        d_up.append(u)
        gain_ffn = gain_ffn + gain
    ffn_parts = [
        (normed_t, (d_gate, d_up), rows, 0, 0),
        (inner_t, (d_branch,), cut - moved, forward_rows - cut + moved, 0),
    ]
    their_orders = jnp.concatenate([other_order, order])
    d_query, d_pair, d_hidden = [], [], []
    gain_attn, gain_query, gain_key = 0.0, 0.0, 0.0
    for batch in both:
        if batch + 1 == batches:
            theirs, mine = weight_grads(their_orders, ffn_parts, model, tuple(d_query))
            ffn_ring = ScatterRing(mine, theirs)
        q, kv, x, gain_a, gain_q, gain_k = attention_back(
            where, d_attn[batch], d_middle[batch], hidden[batch], qkv[batch], pre[batch], gains,
            tables[batch], attn_whole, (mine,) if batch + 1 == batches else (),
        )
        d_query.append(q)
        d_pair.append(kv)
        d_hidden.append(x)
        gain_attn = gain_attn + gain_a
        gain_query = gain_query + gain_q
        gain_key = gain_key + gain_k
    gain_grads = (gain_attn, gain_query, gain_key, gain_ffn)
    attn_parts = [
        (normalized_t, (d_query, d_pair), rows, 0, 0),
        (mixed_t, (d_attn,), rows, rows, 0),
        (inner_t, (d_branch,), moved, forward_rows - 2 * cut + moved, cut - moved),
    ]
    theirs, mine = weight_grads(their_orders, attn_parts, model, (ffn_ring.value,))
    attn_ring = ScatterRing(mine, theirs)
    small = jnp.concatenate([*gain_grads, sum(squares), jnp.sum(keep).reshape(1, 1)], axis=1)
    small_rounds = cycles(small)
    got, _ = next(small_rounds)
    waits = []
    while ffn_ring.step < chips:
        ffn_ring.advance(*waits)
        attn_ring.advance()
        waits = []
        if ffn_ring.step % 2 == 1 and got is not None:
            small = sum(got)
            waits = [small]
            try:
                got, _ = small_rounds.send(small)
            except StopIteration:
                got = None
    while got is not None:
        small = sum(got)
        try:
            got, _ = small_rounds.send(small)
        except StopIteration:
            got = None

    ffn_first, ffn_second = ffn_ring.halves()
    attn_first, attn_second = attn_ring.halves()
    grad_gate = beside(ffn_first, 0, 3, rows)
    grad_up = beside(ffn_second, 0, 3, rows)
    grad_query = beside(attn_first, 0, 2, rows)
    grad_key, grad_value = attn_second[:rows], attn_second[rows : 2 * rows]
    grad_out = jnp.concatenate(
        [attn_first[2 * rows : 3 * rows], attn_second[2 * rows : 3 * rows]], axis=0
    )
    again = 3 * rows + max(0, 2 * cut - forward_rows)
    grad_down = jnp.concatenate(
        [ffn_first[3 * rows :], attn_first[3 * rows :], attn_second[again:], ffn_second[3 * rows :]],
        axis=0,
    )
    small_sum = small
    totals = small_sum[:, -2:]
    totals = jnp.where(section == 1, totals, one_way(totals, 1))[0]
    loss = totals[0] / (totals[1] * model)
    gain_grads, low = [], 0
    for size in gain_sizes:
        gain_grads.append(lax.dynamic_slice(small_sum, (0, low + index * size), (1, size)))
        low += devices * size
    grad_gain_attn, grad_gain_query, grad_gain_key, grad_gain_ffn = gain_grads

    half = batches // 2
    finals = jnp.stack(result)
    grads = jnp.stack(d_hidden)
    output = jnp.where(section == 0, one_way(finals[:half], 1), finals[half:])
    input_grad = jnp.where(section == 0, grads[:half], one_way(grads[half:], 0))
    return (
        output,
        loss,
        input_grad,
        grad_query[None],
        grad_key[None],
        grad_value[None],
        grad_out[None],
        grad_gate[None],
        grad_up[None],
        grad_down[None],
        grad_gain_attn,
        grad_gain_ffn,
        grad_gain_query,
        grad_gain_key,
    )


def solution(mesh):
    placed = (
        P(None, "dp", None),
        P(None, "dp", None),
        P(None, "dp", None),
        P("section", "dp", None),
        P("section", "dp", None),
        P("section", "dp", None),
        P("section", "dp", None),
        P("section", "dp", None),
        P("section", "dp", None),
        P("section", "dp", None),
        P("section", "dp"),
        P("section", "dp"),
        P("section", "dp"),
        P("section", "dp"),
    )
    return jax.shard_map(
        local,
        mesh=mesh,
        in_specs=placed,
        out_specs=(
            P("section", "dp", None),
            P(),
            P("section", "dp", None),
            P("section", "dp", None),
            P("section", "dp", None),
            P("section", "dp", None),
            P("section", "dp", None),
            P("section", "dp", None),
            P("section", "dp", None),
            P("section", "dp", None),
            P("section", "dp"),
            P("section", "dp"),
            P("section", "dp"),
            P("section", "dp"),
        ),
        check_vma=False,
    )
```

```python
import functools

import jax
import jax.numpy as jnp
from jax import lax
from jax.experimental import pallas as pl
from jax.experimental.pallas import tpu as pltpu
from jax.sharding import PartitionSpec as P

QUERY_HEADS = 16
KEY_VALUE_HEADS = 8
HEAD_SIZE = 128
TOKENS_PER_SHARD = 256


EPS = 1e-06
THETA = 1000000.0
NEGATIVE = -1e30
CONTRACT_ROWS = (((0,), (0,)), ((), ()))
CONTRACT_COLS = (((1,), (1,)), ((), ()))
GAIN_ROWS = 16
HOLD_FLOPS = 4400000000
SMALL_LAST = True
VMEM_GRANT = 8


def one_way(value, source):
    return lax.ppermute(value, "section", [(source, 1 - source)])


def chip_at(place, chips):
    place = lax.rem(place + 2 * chips, chips)
    return jnp.where(place < chips // 2, 2 * place, 2 * (chips - 1 - place) + 1)


def ring_place(chip, chips):
    return jnp.where(chip % 2 == 0, chip // 2, chips - 1 - chip // 2)


def ring_routes(devices):
    chips = devices // 2
    order = list(range(0, chips, 2)) + list(range(chips - 1, 0, -2))
    around = []
    for place in range(chips):
        here, there = order[place], order[(place + 1) % chips]
        around += [(2 * here, 2 * there), (2 * there + 1, 2 * here + 1)]
    return around, [(device, device ^ 1) for device in range(devices)]


def cycles(value):
    devices = lax.axis_size("dp")
    index = lax.axis_index("dp")
    width = 1
    while width < devices:
        base = min(4, devices // width)
        got = [value]
        for turn in range(1, base):
            route = []
            for low in range(devices):
                digit = low // width % base
                route.append((low, low + ((digit + turn) % base - digit) * width))
            got.append(lax.ppermute(value, "dp", route))
        value = yield got, index // width % base
        width *= base


class GatherRing:
    def __init__(self, packed, paced=False):
        self.paced = paced
        devices = lax.axis_size("dp")
        self.chips = devices // 2
        self.route, self.pair = ring_routes(devices)
        self.packed = packed
        self.other = lax.ppermute(packed, "dp", self.pair)
        core = lax.axis_index("dp") % 2
        self.pieces = [self.stack(core)]
        self.others = [self.stack(1 - core)]
        self.step = 1

    def stack(self, which):
        core = lax.axis_index("dp") % 2
        first = lax.dynamic_slice_in_dim(self.packed, which, 1, 0)
        second = lax.dynamic_slice_in_dim(self.other, which, 1, 0)
        return jnp.where(
            core == 0,
            jnp.concatenate([first, second], axis=0),
            jnp.concatenate([second, first], axis=0),
        )

    def advance(self, *before):
        value = self.pieces[-1]
        if before or self.paced and self.step > 1:
            value = self.pieces[-1] = hold(value, *before)
        self.pieces.append(lax.ppermute(value, "dp", self.route))
        self.swap(value)
        self.step += 1
        if self.step == self.chips:
            self.swap(self.pieces[-1])
        return self.pieces[-1]

    def swap(self, value):
        if len(self.pieces) > 2 or self.step == self.chips:
            self.others.append(lax.ppermute(value, "dp", self.pair))


class ScatterRing:
    def __init__(self, mine, theirs):
        devices = lax.axis_size("dp")
        self.chips = devices // 2
        self.route, self.pair = ring_routes(devices)
        self.mine = mine
        self.got = lax.ppermute(theirs, "dp", self.pair)
        value = mine[1].astype(jnp.float32) + self.got[1].astype(jnp.float32)
        self.value = value.astype(jnp.bfloat16)
        self.step = 1

    def advance(self, *before):
        if before:
            self.value = hold(self.value, *before)
        self.step += 1
        place = self.step % self.chips
        value = lax.ppermute(self.value, "dp", self.route).astype(jnp.float32)
        value = value + self.mine[place].astype(jnp.float32)
        value = value + self.got[place].astype(jnp.float32)
        self.value = value.astype(jnp.bfloat16) if self.step < self.chips else value
        return self.value

    def halves(self):
        core = lax.axis_index("dp") % 2
        own = lax.dynamic_index_in_dim(self.value, core, 0, keepdims=False)
        other = lax.dynamic_index_in_dim(self.value, 1 - core, 0, keepdims=False)
        other = lax.ppermute(other, "dp", self.pair)
        return jnp.where(core == 0, own, other), jnp.where(core == 0, other, own)


def beside(grad, low, pieces, rows):
    return jnp.concatenate(
        [grad[low + rows * i : low + rows * (i + 1)] for i in range(pieces)], axis=1
    )


def layout(lengths_row):
    ends = jnp.cumsum(lengths_row)
    places = jnp.arange(TOKENS_PER_SHARD, dtype=jnp.int32)
    passed = (ends[None, :] <= places[:, None]).astype(jnp.int32)
    segment_index = jnp.sum(passed, axis=1)
    start = jnp.sum(passed * lengths_row[None, :], axis=1)
    return (segment_index, places - start)


def rotary_tables(place):
    half = HEAD_SIZE // 2
    freqs = THETA ** (-(jnp.arange(half, dtype=jnp.float32) * 2.0 / HEAD_SIZE))
    angles = place.astype(jnp.float32)[:, None] * freqs[None, :]
    return (jnp.cos(angles), jnp.sin(angles))


LOCAL = pl.BlockSpec(memory_space=pltpu.VMEM)
SCALARS = pl.BlockSpec(memory_space=pltpu.SMEM)
ANYWHERE = pl.BlockSpec(memory_space=pl.ANY)


def hold(value, *after):
    return pl.pallas_call(
        lambda *refs: None,
        in_specs=[ANYWHERE] * (1 + len(after)),
        out_specs=ANYWHERE,
        out_shape=jax.ShapeDtypeStruct(value.shape, value.dtype),
        input_output_aliases={0: 0},
        cost_estimate=pl.CostEstimate(flops=HOLD_FLOPS, bytes_accessed=0, transcendentals=0),
    )(value, *after)


def flat_call(body, arguments, out_shape, scratch=(), flops=0, moved=0, vmem=VMEM_GRANT, after=()):
    specs = [SCALARS] + [LOCAL] * (len(arguments) - 1) + [ANYWHERE] * len(after)
    count = len(arguments)

    def run(*refs):
        body(*refs[:count], *refs[count + len(after) :])

    return pl.pallas_call(
        run,
        in_specs=specs,
        out_specs=[LOCAL] * len(out_shape),
        out_shape=out_shape,
        scratch_shapes=list(scratch),
        compiler_params=pltpu.CompilerParams(vmem_limit_bytes=vmem << 20),
        cost_estimate=pl.CostEstimate(
            flops=int(flops), bytes_accessed=int(moved), transcendentals=0
        ),
    )(*arguments, *after)


def low_shape(*shape):
    return jax.ShapeDtypeStruct(shape, jnp.bfloat16)


def full_shape(*shape):
    return jax.ShapeDtypeStruct(shape, jnp.float32)


def dot_plain(left, right):
    return jnp.dot(left, right, preferred_element_type=jnp.float32)


def dot_columns(left, right):
    return lax.dot_general(left, right, CONTRACT_COLS, preferred_element_type=jnp.float32)


def dot_rows(left, right):
    return lax.dot_general(left, right, CONTRACT_ROWS, preferred_element_type=jnp.float32)


def unit_rows(values):
    factor = lax.rsqrt(jnp.mean(values * values, axis=-1, keepdims=True) + EPS)
    return values * factor, factor


def norm_pull(grad, scaled, factor, gain):
    pulled = grad * gain
    return factor * (pulled - scaled * jnp.mean(pulled * scaled, axis=-1, keepdims=True))


def head_mean(values):
    average = jnp.full((HEAD_SIZE, HEAD_SIZE), 1.0 / HEAD_SIZE, jnp.bfloat16)
    return dot_plain(values.astype(jnp.bfloat16), average)


def slab(ref, low, rows):
    value = ref[:, low : low + rows, :]
    return value.reshape(value.shape[0] * rows, value.shape[2])


def part_of(index, width=HEAD_SIZE):
    return slice(index * width, (index + 1) * width)


def attention_kernel(
    keep, section_ref, h_ref, came_ref, gain_ref, gain_q_ref, gain_k_ref, gain_ffn_ref, cos_ref,
    sin_ref, row_ref, column_ref, w_ref, hm_ref, xf_ref, *rest,
):
    if keep:
        xf_t_ref, xa_t_ref, o_t_ref, qkv_ref, pre_ref, hidden_ref, o_ref = rest
    else:
        qkv_ref, o_ref = rest
    tokens, model = h_ref.shape
    rows = w_ref.shape[1] // 6
    hidden = h_ref[...]
    if keep:
        hidden = jnp.where(section_ref[0] == 0, hidden, came_ref[...])
        hidden_ref[...] = hidden
    hidden = hidden.astype(jnp.float32)
    scaled, _ = unit_rows(hidden)
    xa = (scaled * gain_ref[...]).astype(jnp.bfloat16)
    cosine, sine = cos_ref[...], sin_ref[...]
    for block, low in enumerate((0, rows, 4 * rows, 5 * rows)):
        pre = dot_plain(xa, slab(w_ref, low, rows))
        if block == 3:
            qkv_ref[:, part_of(block, model)] = pre.astype(jnp.bfloat16)
            continue
        if keep:
            pre_ref[:, part_of(block, model)] = pre.astype(jnp.bfloat16)
        gain = gain_q_ref[...] if block < 2 else gain_k_ref[...]
        for head in range(model // HEAD_SIZE):
            value = pre[:, part_of(head)]
            value = value * lax.rsqrt(head_mean(value * value) + EPS) * gain
            value = value * cosine + pltpu.roll(value, HEAD_SIZE // 2, 1) * sine
            qkv_ref[:, part_of(block * (model // HEAD_SIZE) + head)] = value.astype(jnp.bfloat16)
    causal = lax.broadcasted_iota(jnp.int32, (tokens, tokens), 0) >= lax.broadcasted_iota(
        jnp.int32, (tokens, tokens), 1
    )
    allowed = (row_ref[...] == column_ref[0]) & causal
    ones = jnp.ones((tokens, HEAD_SIZE), jnp.bfloat16)
    for shared in range(KEY_VALUE_HEADS):
        key = qkv_ref[:, part_of(QUERY_HEADS + shared)]
        value = qkv_ref[:, part_of(QUERY_HEADS + KEY_VALUE_HEADS + shared)]
        value = jnp.concatenate([value, ones], axis=1)
        for head in range(2 * shared, 2 * shared + 2):
            scores = dot_columns(qkv_ref[:, part_of(head)], key) * HEAD_SIZE ** (-0.5)
            raised = jnp.where(allowed, jnp.exp(scores), 0.0).astype(jnp.bfloat16)
            mixed = dot_plain(raised, value)
            mixed = mixed[:, :HEAD_SIZE] / mixed[:, HEAD_SIZE:]
            o_ref[:, part_of(head)] = mixed.astype(jnp.bfloat16)
    middle = hidden + dot_plain(o_ref[...], slab(w_ref, 2 * rows, 2 * rows))
    hm_ref[...] = middle
    scaled, _ = unit_rows(middle)
    xf = (scaled * gain_ffn_ref[...]).astype(jnp.bfloat16)
    xf_ref[...] = xf
    if keep:
        xf_t_ref[...] = jnp.transpose(xf)
        xa_t_ref[...] = jnp.transpose(xa)
        o_t_ref[...] = jnp.transpose(o_ref[...])


def attention(section, hidden, came, gains, tables, whole, keep):
    tokens, model = hidden.shape
    wide = QUERY_HEADS * HEAD_SIZE
    shapes = [full_shape(tokens, model), low_shape(tokens, model)]
    scratch = [pltpu.VMEM((tokens, wide), jnp.bfloat16)]
    if keep:
        shapes += [
            low_shape(model, tokens),
            low_shape(model, tokens),
            low_shape(wide, tokens),
            low_shape(tokens, 4 * model),
            low_shape(tokens, 3 * model),
            low_shape(tokens, model),
        ]
    else:
        scratch = [pltpu.VMEM((tokens, 4 * model), jnp.bfloat16)] + scratch
    return flat_call(
        functools.partial(attention_kernel, keep),
        (section, hidden, came, *gains, *tables, whole),
        shapes,
        scratch=scratch,
        flops=2 * tokens * model * 6 * model + 8 * tokens * tokens * wide,
        moved=12 * model * model + 20 * tokens * model,
    )


def ffn_kernel(keep, _, xf_ref, hm_ref, w_ref, *rest):
    if keep:
        teacher_ref, keep_ref, y_ref, g_ref, u_ref, z_t_ref, pull_ref, square_ref, inner = rest
    else:
        y_ref, inner = rest
    tokens, model = xf_ref.shape
    rows = w_ref.shape[1] // 9
    xf = xf_ref[...]
    for block in range(3):
        gate = dot_plain(xf, slab(w_ref, block * rows, rows))
        up = dot_plain(xf, slab(w_ref, (6 + block) * rows, rows))
        mixed = (gate * jax.nn.sigmoid(gate) * up).astype(jnp.bfloat16)
        inner[:, part_of(block, model)] = mixed
        if keep:
            g_ref[:, part_of(block, model)] = gate.astype(jnp.bfloat16)
            u_ref[:, part_of(block, model)] = up.astype(jnp.bfloat16)
            z_t_ref[part_of(block, model), :] = jnp.transpose(mixed)
    total = hm_ref[...] + dot_plain(inner[...], slab(w_ref, 3 * rows, 3 * rows))
    low = total.astype(jnp.bfloat16)
    y_ref[...] = low
    if keep:
        error = low.astype(jnp.float32) - teacher_ref[...]
        pull = keep_ref[...] * error
        pull_ref[...] = pull
        square_ref[...] = jnp.sum(jnp.sum(pull * error, axis=0, keepdims=True), axis=1, keepdims=True)


def feed_forward(section, normed, middle, whole, target=()):
    tokens, model = normed.shape
    width = 3 * model
    shapes = [low_shape(tokens, model)]
    if target:
        shapes += [low_shape(tokens, width), low_shape(tokens, width), low_shape(width, tokens)]
        shapes += [full_shape(tokens, model), full_shape(1, 1)]
    return flat_call(
        functools.partial(ffn_kernel, bool(target)),
        (section, normed, middle, whole, *target),
        shapes,
        scratch=[pltpu.VMEM((tokens, width), jnp.bfloat16)],
        flops=6 * tokens * width * model,
        moved=6 * width * model + 8 * tokens * model,
    )


def ffn_back_kernel(
    section_ref, dy_ref, came_ref, hm_ref, gain_ref, g_ref, u_ref, w_ref, dh_ref, low_ref, dg_ref,
    du_ref, dgain_ref, low_dy_ref,
):
    devices, rows, model = w_ref.shape
    rows = rows // 9
    d_result = jnp.where(section_ref[0] == 1, dy_ref[...], came_ref[...].astype(jnp.float32))
    low_dy = d_result.astype(jnp.bfloat16)
    low_dy_ref[...] = low_dy
    chunks = 4
    owners = devices // chunks
    chunk = 3 * model // chunks
    for block in range(chunks):
        part = part_of(block, chunk)
        down = w_ref[block * owners : (block + 1) * owners, 3 * rows : 6 * rows, :]
        d_inner = dot_columns(low_dy, down.reshape(chunk, model))
        gate = g_ref[:, part].astype(jnp.float32)
        sigma = jax.nn.sigmoid(gate)
        silu = gate * sigma
        d_gate = d_inner * u_ref[:, part].astype(jnp.float32) * (sigma + silu * (1.0 - sigma))
        dg_ref[:, part] = d_gate.astype(jnp.bfloat16)
        du_ref[:, part] = (d_inner * silu).astype(jnp.bfloat16)
    grad = None
    for block in range(3):
        part = part_of(block, model)
        term = dot_columns(dg_ref[:, part], slab(w_ref, block * rows, rows))
        term = term + dot_columns(du_ref[:, part], slab(w_ref, (6 + block) * rows, rows))
        grad = term if grad is None else grad + term
    scaled, factor = unit_rows(hm_ref[...])
    dgain_ref[...] = jnp.sum(grad * scaled, axis=0, keepdims=True)
    d_result = jnp.where(section_ref[0] == 1, dy_ref[...], came_ref[...].astype(jnp.float32))
    d_hidden = d_result + norm_pull(grad, scaled, factor, gain_ref[...])
    dh_ref[...] = d_hidden
    low_ref[...] = d_hidden.astype(jnp.bfloat16)


def feed_forward_back(section, pull, came, middle, gains, gate, up, whole):
    tokens, model = middle.shape
    width = 3 * model
    return flat_call(
        ffn_back_kernel,
        (section, pull, came, middle, gains[3], gate, up, whole),
        [
            full_shape(tokens, model),
            low_shape(tokens, model),
            low_shape(tokens, width),
            low_shape(tokens, width),
            full_shape(1, model),
            low_shape(tokens, model),
        ],
        flops=6 * tokens * width * model,
        moved=6 * width * model + 14 * tokens * model + 8 * tokens * width,
    )


def attention_back_kernel(
    _, low_ref, dh_ref, h_ref, qkv_ref, pre_ref, gain_ref, gain_q_ref, gain_k_ref, cos_ref, sin_ref,
    row_ref, column_ref, w_ref, dq_ref, dkv_ref, dx_ref, dgain_ref, dgain_q_ref,
    dgain_k_ref, do_ref,
):
    tokens, model = h_ref.shape
    rows = w_ref.shape[1] // 6
    do_ref[...] = dot_columns(low_ref[...], slab(w_ref, 2 * rows, 2 * rows)).astype(jnp.bfloat16)
    causal = lax.broadcasted_iota(jnp.int32, (tokens, tokens), 0) <= lax.broadcasted_iota(
        jnp.int32, (tokens, tokens), 1
    )
    allowed = (row_ref[...] == column_ref[0]) & causal
    cosine, sine = cos_ref[...], sin_ref[...]
    scale = HEAD_SIZE ** (-0.5)
    gain_grads = [jnp.zeros((1, HEAD_SIZE), jnp.float32)] * 2

    def through_norm(grad, pre, gain_ref, which):
        gain = gain_ref[...]
        grad = grad * cosine - pltpu.roll(grad, HEAD_SIZE // 2, 1) * sine
        pre = pre.astype(jnp.float32)
        factor = lax.rsqrt(head_mean(pre * pre) + EPS)
        scaled = pre * factor
        gain_grads[which] = gain_grads[which] + jnp.sum(grad * scaled, axis=0, keepdims=True)
        pulled = grad * gain
        return (factor * (pulled - scaled * head_mean(pulled * scaled))).astype(jnp.bfloat16)

    for shared in range(KEY_VALUE_HEADS):
        lone = part_of(shared)
        key = qkv_ref[:, part_of(QUERY_HEADS + shared)]
        value = qkv_ref[:, part_of(QUERY_HEADS + KEY_VALUE_HEADS + shared)]
        d_key = d_value = None
        for head in range(2 * shared, 2 * shared + 2):
            part = part_of(head)
            query, d_mixed = qkv_ref[:, part], do_ref[:, part]
            scores = dot_columns(key, query) * scale
            raised = jnp.where(allowed, jnp.exp(scores), 0.0)
            weights = raised * (1.0 / jnp.sum(raised, axis=0, keepdims=True))
            value_term = dot_plain(weights.astype(jnp.bfloat16), d_mixed)
            d_weights = dot_columns(value, d_mixed)
            pulled = jnp.sum(d_weights * weights, axis=0, keepdims=True)
            d_scores = (weights * (d_weights - pulled)).astype(jnp.bfloat16)
            d_query = dot_rows(d_scores, key) * scale
            key_term = dot_plain(d_scores, query)
            d_key = key_term if d_key is None else d_key + key_term
            d_value = value_term if d_value is None else d_value + value_term
            dq_ref[:, part] = through_norm(d_query, pre_ref[:, part], gain_q_ref, 0)
        dkv_ref[:, lone] = through_norm(
            d_key * scale, pre_ref[:, part_of(QUERY_HEADS + shared)], gain_k_ref, 1
        )
        dkv_ref[:, part_of(KEY_VALUE_HEADS + shared)] = d_value.astype(jnp.bfloat16)
    dgain_q_ref[...], dgain_k_ref[...] = gain_grads
    grad = dot_columns(dq_ref[:, part_of(0, model)], slab(w_ref, 0, rows))
    grad = grad + dot_columns(dq_ref[:, part_of(1, model)], slab(w_ref, rows, rows))
    grad = grad + dot_columns(dkv_ref[:, part_of(0, model)], slab(w_ref, 4 * rows, rows))
    grad = grad + dot_columns(dkv_ref[:, part_of(1, model)], slab(w_ref, 5 * rows, rows))
    scaled, factor = unit_rows(h_ref[...].astype(jnp.float32))
    dgain_ref[...] = jnp.sum(grad * scaled, axis=0, keepdims=True)
    d_hidden = dh_ref[...] + norm_pull(grad, scaled, factor, gain_ref[...])
    dx_ref[...] = d_hidden.astype(jnp.bfloat16)


def attention_back(section, low, d_middle, hidden, qkv, pre, gains, tables, whole, after=()):
    tokens, model = hidden.shape
    wide = QUERY_HEADS * HEAD_SIZE
    return flat_call(
        attention_back_kernel,
        (section, low, d_middle, hidden, qkv, pre, *gains[:3], *tables, whole),
        [
            low_shape(tokens, wide),
            low_shape(tokens, 2 * model),
            low_shape(tokens, model),
            full_shape(1, model),
            full_shape(1, HEAD_SIZE),
            full_shape(1, HEAD_SIZE),
        ],
        scratch=[pltpu.VMEM((tokens, wide), jnp.bfloat16)],
        flops=2 * tokens * model * 6 * model + 20 * tokens * tokens * wide,
        moved=12 * model * model + 40 * tokens * model,
        after=after,
    )


def grad_kernel(plan, chips, batches, order_ref, *refs):
    count = sum(1 + len(entry[5]) for entry in plan) * batches
    targets, stores = refs[count : count + 2], refs[count + 2 :]
    model = targets[0].shape[3]
    for target, base in ((targets[0], 0), (targets[1], chips + 1)):
        side = order_ref[base + chips]
        taken, start = 0, 0
        for (rows, size, low, least, blocks, choices), store in zip(plan, stores):
            left = refs[taken : taken + batches]
            taken += batches
            rights = []
            for _ in choices:
                rights.append(refs[taken : taken + batches])
                taken += batches
            first = least + side * low
            for t in range(chips):
                owner = 2 * order_ref[base + t]
                for core in range(2):
                    place = pl.multiple_of((owner + core) * rows + first, 16)
                    to = slice((2 * t + core) * size, (2 * t + core + 1) * size)
                    for batch in range(batches):
                        store[batch, to, :] = left[batch][pl.ds(place, size), :]
            for block in range(blocks):
                part = part_of(block, model)
                right = []
                for batch in range(batches):
                    value = rights[0][batch][:, part]
                    if len(rights) > 1:
                        value = jnp.where(side == 0, value, rights[1][batch][:, part])
                    right.append(value)
                for half in range(2):
                    value = None
                    span = slice(half * chips * size, (half + 1) * chips * size)
                    for batch in range(batches):
                        term = dot_plain(store[batch, span, :], right[batch])
                        value = term if value is None else value + term
                    value = value.astype(jnp.bfloat16).reshape(chips // 2, 2, size, model)
                    into = slice(start + block * size, start + (block + 1) * size)
                    target[half * chips // 2 : (half + 1) * chips // 2, :, into, :] = value
            start += blocks * size


def weight_grads(orders, parts, model, after=()):
    batches = len(parts[0][0])
    tokens = parts[0][0][0].shape[1]
    chips = orders.shape[0] // 2 - 1
    plan, scratch, operands, total = [], [], [], 0
    for left, rights, size, low, least in parts:
        rows = left[0].shape[0] // (2 * chips)
        blocks = rights[0][0].shape[1] // model
        plan.append((rows, size, low, least, blocks, tuple(range(len(rights)))))
        scratch.append(pltpu.VMEM((batches, 2 * chips * size, tokens), jnp.bfloat16))
        operands += list(left) + [array for right in rights for array in right]
        total += size * blocks
    shape = low_shape(chips, 2, total, model)
    return flat_call(
        functools.partial(grad_kernel, tuple(plan), chips, batches),
        (orders, *operands),
        [shape, shape],
        scratch=scratch,
        flops=8 * chips * total * model * tokens * batches,
        moved=8 * chips * total * model + 8 * tokens * batches * model,
        vmem=14,
        after=after,
    )


def pack_kernel(plan, *refs):
    target, sem = refs[-2:]
    model = target.shape[2]
    copies = []
    for half, entries in enumerate(plan):
        low = 0
        for source, start, rows, block in entries:
            copies.append(
                pltpu.make_async_copy(
                    refs[source].at[start : start + rows, part_of(block, model)],
                    target.at[half, low : low + rows, :],
                    sem.at[len(copies)],
                )
            )
            low += rows
    for copy in copies:
        copy.start()
    for copy in copies:
        copy.wait()


def pack(shards, plan, model, after=()):
    rows = sum(entry[2] for entry in plan[0])
    return pl.pallas_call(
        functools.partial(pack_kernel, plan),
        in_specs=[ANYWHERE] * (len(shards) + len(after)),
        out_specs=LOCAL,
        out_shape=low_shape(2, rows, model),
        scratch_shapes=[pltpu.SemaphoreType.DMA((len(plan[0]) + len(plan[1]),))],
        compiler_params=pltpu.CompilerParams(vmem_limit_bytes=VMEM_GRANT << 20),
    )(*shards, *after)


def assemble_kernel(chips, plan, order_ref, *refs):
    target, sem = refs[-2:]
    copies = []
    for group, (low, rows, start, further) in enumerate(plan):
        for turn in range(2):
            base = turn * (chips + 1)
            place = pl.multiple_of(start + order_ref[base + chips] * further, 16)
            for t in range(chips):
                piece = refs[(2 * group + turn) * chips + t]
                copies.append(
                    pltpu.make_async_copy(
                        piece.at[:, low : low + rows, :],
                        target.at[pl.ds(2 * order_ref[base + t], 2), pl.ds(place, rows), :],
                        sem.at[len(copies)],
                    )
                )
    for copy in copies:
        copy.start()
    for copy in copies:
        copy.wait()


def assemble(orders, sources, rows):
    chips = sources[0][0].chips
    pieces = [piece for source in sources for piece in source[0].pieces + source[0].others]
    model = pieces[0].shape[2]
    return pl.pallas_call(
        functools.partial(assemble_kernel, chips, tuple(source[1:] for source in sources)),
        in_specs=[SCALARS] + [ANYWHERE] * len(pieces),
        out_specs=LOCAL,
        out_shape=low_shape(2 * chips, rows, model),
        scratch_shapes=[pltpu.SemaphoreType.DMA((len(pieces),))],
        compiler_params=pltpu.CompilerParams(vmem_limit_bytes=VMEM_GRANT << 20),
        cost_estimate=pl.CostEstimate(
            flops=0, bytes_accessed=8 * chips * rows * model, transcendentals=0
        ),
    )(orders, *pieces)


def local(
    inputs,
    teacher,
    lengths,
    attn_query,
    attn_key,
    attn_value,
    attn_out,
    ffn_gate,
    ffn_up,
    ffn_down,
    norm_attn,
    norm_ffn,
    norm_query,
    norm_key,
):
    section = lax.axis_index("section")
    index = lax.axis_index("dp")
    devices = lax.axis_size("dp")
    chips = devices // 2
    batches, _, model = inputs.shape
    slots = lengths.shape[2]
    rows = attn_query.shape[1]
    forward_rows = ffn_down.shape[1]

    cut = forward_rows // 2 if forward_rows % 32 == 0 else 2 * rows
    core = index % 2
    place = ring_place(index // 2, chips)
    away = jnp.arange(chips, dtype=jnp.int32) * (2 * core - 1)
    order = jnp.concatenate([chip_at(place + away, chips), core[None]]).astype(jnp.int32)
    other_order = jnp.concatenate([chip_at(place - away, chips), 1 - core[None]]).astype(jnp.int32)
    orders = jnp.concatenate([order, other_order])
    gain_sizes = (norm_attn.shape[1], norm_query.shape[1], norm_key.shape[1], norm_ffn.shape[1])
    gain_shard = jnp.concatenate([norm_attn, norm_query, norm_key, norm_ffn], axis=1)
    gain_count = gain_shard.shape[1]
    gain_shard = jnp.pad(gain_shard, ((0, GAIN_ROWS - 1), (0, model - gain_count)))
    moved = cut // 2
    attn_packed = pack(
        (attn_query[0], attn_out[0], attn_key[0], attn_value[0], gain_shard),
        (
            ((0, 0, rows, 0), (0, 0, rows, 1), (1, 0, rows, 0), (4, 0, GAIN_ROWS, 0)),
            ((1, rows, rows, 0), (2, 0, rows, 0), (3, 0, rows, 0), (4, 0, GAIN_ROWS, 0)),
        ),
        model,
    )
    ffn_packed = pack(
        (ffn_gate[0], ffn_down[0], ffn_up[0]),
        (
            ((0, 0, rows, 0), (0, 0, rows, 1), (0, 0, rows, 2), (1, 0, cut, 0)),
            (
                (1, forward_rows - cut, cut, 0),
                (2, 0, rows, 0),
                (2, 0, rows, 1),
                (2, 0, rows, 2),
            ),
        ),
        model,
    )
    segments, places = jax.vmap(layout)(lengths[:, 0, :])
    keep = (segments < slots - 1).astype(jnp.float32)
    tables = []
    for batch in range(batches):
        cosine_table, sine_table = rotary_tables(places[batch])
        tables.append(
            (
                jnp.concatenate([cosine_table, cosine_table], axis=1),
                jnp.concatenate([-sine_table, sine_table], axis=1),
                segments[batch].reshape(TOKENS_PER_SHARD, 1),
                segments[batch].reshape(1, 1, TOKENS_PER_SHARD),
            )
        )
    keep_columns = [keep[batch][:, None] for batch in range(batches)]
    first = [inputs[batch] for batch in range(batches)]
    target = [teacher[batch] for batch in range(batches)]
    early = [array for table in tables for array in table] + keep_columns + first + target + [orders]
    attn_ring = GatherRing(attn_packed, True)
    ffn_ring = GatherRing(ffn_packed)
    attn_ring.advance()
    ffn_ring.advance()
    attn_ring.advance(*early)
    ffn_ring.advance(attn_ring.others[0], ffn_ring.others[0])
    while ffn_ring.step < chips:
        attn_ring.advance()
        ffn_ring.advance()
    carried_gains = jnp.stack([piece[:, 3 * rows, :gain_count] for piece in attn_ring.pieces])
    chip = jnp.arange(chips, dtype=jnp.int32)
    found = lax.rem((2 * core - 1) * (ring_place(chip, chips) - place) + chips, chips)
    gain_whole = jnp.take(carried_gains, found, axis=0).reshape(devices, gain_count)
    gain_whole = gain_whole.astype(jnp.float32)
    gains, low = [], 0
    for size in gain_sizes:
        gains.append(gain_whole[:, low : low + size].reshape(1, devices * size))
        low += size

    half = 3 * rows + cut
    ffn_low = 9 * rows - half
    attn_whole = assemble(orders, [(attn_ring, 0, 3 * rows, 0, 3 * rows)], 6 * rows)
    ffn_whole = assemble(orders, [(ffn_ring, 0, half, 0, ffn_low)], 9 * rows)
    both = range(batches)

    where = section[None].astype(jnp.int32)
    last = jnp.ones((1,), jnp.int32)
    carried, seen = [], []
    for batch in both:
        seen.append(attention(where, first[batch], first[batch], gains, tables[batch], attn_whole, False))
    for batch in both:
        (result,) = feed_forward(where, seen[batch][1], seen[batch][0], ffn_whole)
        carried.append(one_way(result, 0))

    kept = []
    for batch in both:
        mid, norm, norm_t, normalized_t, mix_t, qkv, pre, hidden = attention(
            where, first[batch], carried[batch], gains, tables[batch], attn_whole, True
        )
        result, gate, up, inner_t, pull, square = feed_forward(
            where, norm, mid, ffn_whole, (target[batch], keep_columns[batch])
        )
        kept.append(
            (hidden, normalized_t, qkv, pre, mix_t, mid, norm_t, result, gate, up, inner_t, pull, square)
        )
    (
        hidden, normalized_t, qkv, pre, mixed_t, middle, normed_t, result, gate, up, inner_t, pull,
        squares,
    ) = (list(column) for column in zip(*kept))

    incoming = []
    for batch in both:
        d_middle, d_attn = feed_forward_back(
            last, pull[batch], result[batch], middle[batch], gains, gate[batch], up[batch], ffn_whole
        )[:2]
        d_hidden = attention_back(
            where, d_attn, d_middle, hidden[batch], qkv[batch], pre[batch], gains, tables[batch],
            attn_whole,
        )[2]
        incoming.append(one_way(d_hidden, 1))

    d_middle, d_attn, d_gate, d_up, d_branch, gain_ffn = [], [], [], [], [], 0.0
    for batch in both:
        m, a, g, u, gain, low = feed_forward_back(
            where, pull[batch], incoming[batch], middle[batch], gains, gate[batch], up[batch],
            ffn_whole,
        )
        d_branch.append(low)
        d_middle.append(m)
        d_attn.append(a)
        d_gate.append(g)
        d_up.append(u)
        gain_ffn = gain_ffn + gain
    ffn_parts = [
        (normed_t, (d_gate, d_up), rows, 0, 0),
        (inner_t, (d_branch,), cut - moved, forward_rows - cut + moved, 0),
    ]
    their_orders = jnp.concatenate([other_order, order])
    d_query, d_pair, d_hidden = [], [], []
    gain_attn, gain_query, gain_key = 0.0, 0.0, 0.0
    for batch in both:
        if batch + 1 == batches:
            theirs, mine = weight_grads(their_orders, ffn_parts, model, tuple(d_query))
            ffn_ring = ScatterRing(mine, theirs)
        q, kv, x, gain_a, gain_q, gain_k = attention_back(
            where, d_attn[batch], d_middle[batch], hidden[batch], qkv[batch], pre[batch], gains,
            tables[batch], attn_whole, (mine,) if batch + 1 == batches else (),
        )
        d_query.append(q)
        d_pair.append(kv)
        d_hidden.append(x)
        gain_attn = gain_attn + gain_a
        gain_query = gain_query + gain_q
        gain_key = gain_key + gain_k
    gain_grads = (gain_attn, gain_query, gain_key, gain_ffn)
    attn_parts = [
        (normalized_t, (d_query, d_pair), rows, 0, 0),
        (mixed_t, (d_attn,), rows, rows, 0),
        (inner_t, (d_branch,), moved, forward_rows - 2 * cut + moved, cut - moved),
    ]
    theirs, mine = weight_grads(their_orders, attn_parts, model, (ffn_ring.value,))
    attn_ring = ScatterRing(mine, theirs)
    small = jnp.concatenate([*gain_grads, sum(squares), jnp.sum(keep).reshape(1, 1)], axis=1)
    small_rounds = cycles(small)
    got, _ = next(small_rounds)
    waits = []
    while ffn_ring.step < chips:
        ffn_ring.advance()
        attn_ring.advance(*waits)
        waits = []
        if ffn_ring.step % 2 == 1 and got is not None:
            small = sum(got)
            waits = [small]
            try:
                got, _ = small_rounds.send(small)
            except StopIteration:
                got = None
    while got is not None:
        small = sum(got)
        try:
            got, _ = small_rounds.send(small)
        except StopIteration:
            got = None

    ffn_first, ffn_second = ffn_ring.halves()
    attn_first, attn_second = attn_ring.halves()
    grad_gate = beside(ffn_first, 0, 3, rows)
    grad_up = beside(ffn_second, 0, 3, rows)
    grad_query = beside(attn_first, 0, 2, rows)
    grad_key, grad_value = attn_second[:rows], attn_second[rows : 2 * rows]
    grad_out = jnp.concatenate(
        [attn_first[2 * rows : 3 * rows], attn_second[2 * rows : 3 * rows]], axis=0
    )
    again = 3 * rows + max(0, 2 * cut - forward_rows)
    grad_down = jnp.concatenate(
        [ffn_first[3 * rows :], attn_first[3 * rows :], attn_second[again:], ffn_second[3 * rows :]],
        axis=0,
    )
    small_sum = small
    totals = small_sum[:, -2:]
    totals = jnp.where(section == 1, totals, one_way(totals, 1))[0]
    loss = totals[0] / (totals[1] * model)
    gain_grads, low = [], 0
    for size in gain_sizes:
        gain_grads.append(lax.dynamic_slice(small_sum, (0, low + index * size), (1, size)))
        low += devices * size
    grad_gain_attn, grad_gain_query, grad_gain_key, grad_gain_ffn = gain_grads

    half = batches // 2
    finals = jnp.stack(result)
    grads = jnp.stack(d_hidden)
    output = jnp.where(section == 0, one_way(finals[:half], 1), finals[half:])
    input_grad = jnp.where(section == 0, grads[:half], one_way(grads[half:], 0))
    return (
        output,
        loss,
        input_grad,
        grad_query[None],
        grad_key[None],
        grad_value[None],
        grad_out[None],
        grad_gate[None],
        grad_up[None],
        grad_down[None],
        grad_gain_attn,
        grad_gain_ffn,
        grad_gain_query,
        grad_gain_key,
    )


def solution(mesh):
    placed = (
        P(None, "dp", None),
        P(None, "dp", None),
        P(None, "dp", None),
        P("section", "dp", None),
        P("section", "dp", None),
        P("section", "dp", None),
        P("section", "dp", None),
        P("section", "dp", None),
        P("section", "dp", None),
        P("section", "dp", None),
        P("section", "dp"),
        P("section", "dp"),
        P("section", "dp"),
        P("section", "dp"),
    )
    return jax.shard_map(
        local,
        mesh=mesh,
        in_specs=placed,
        out_specs=(
            P("section", "dp", None),
            P(),
            P("section", "dp", None),
            P("section", "dp", None),
            P("section", "dp", None),
            P("section", "dp", None),
            P("section", "dp", None),
            P("section", "dp", None),
            P("section", "dp", None),
            P("section", "dp", None),
            P("section", "dp"),
            P("section", "dp"),
            P("section", "dp"),
            P("section", "dp"),
        ),
        check_vma=False,
    )
```

```python
import functools

import jax
import jax.numpy as jnp
from jax import lax
from jax.experimental import pallas as pl
from jax.experimental.pallas import tpu as pltpu
from jax.sharding import PartitionSpec as P

QUERY_HEADS = 16
KEY_VALUE_HEADS = 8
HEAD_SIZE = 128
TOKENS_PER_SHARD = 256


EPS = 1e-06
THETA = 1000000.0
NEGATIVE = -1e30
CONTRACT_ROWS = (((0,), (0,)), ((), ()))
CONTRACT_COLS = (((1,), (1,)), ((), ()))
GAIN_ROWS = 16
HOLD_FLOPS = 4400000000
SMALL_LAST = True
VMEM_GRANT = 9


def one_way(value, source):
    return lax.ppermute(value, "section", [(source, 1 - source)])


def chip_at(place, chips):
    place = lax.rem(place + 2 * chips, chips)
    return jnp.where(place < chips // 2, 2 * place, 2 * (chips - 1 - place) + 1)


def ring_place(chip, chips):
    return jnp.where(chip % 2 == 0, chip // 2, chips - 1 - chip // 2)


def ring_routes(devices):
    chips = devices // 2
    order = list(range(0, chips, 2)) + list(range(chips - 1, 0, -2))
    around = []
    for place in range(chips):
        here, there = order[place], order[(place + 1) % chips]
        around += [(2 * here, 2 * there), (2 * there + 1, 2 * here + 1)]
    return around, [(device, device ^ 1) for device in range(devices)]


def cycles(value):
    devices = lax.axis_size("dp")
    index = lax.axis_index("dp")
    width = 1
    while width < devices:
        base = min(4, devices // width)
        got = [value]
        for turn in range(1, base):
            route = []
            for low in range(devices):
                digit = low // width % base
                route.append((low, low + ((digit + turn) % base - digit) * width))
            got.append(lax.ppermute(value, "dp", route))
        value = yield got, index // width % base
        width *= base


class GatherRing:
    def __init__(self, packed, paced=False):
        self.paced = paced
        devices = lax.axis_size("dp")
        self.chips = devices // 2
        self.route, self.pair = ring_routes(devices)
        self.packed = packed
        self.other = lax.ppermute(packed, "dp", self.pair)
        core = lax.axis_index("dp") % 2
        self.pieces = [self.stack(core)]
        self.others = [self.stack(1 - core)]
        self.step = 1

    def stack(self, which):
        core = lax.axis_index("dp") % 2
        first = lax.dynamic_slice_in_dim(self.packed, which, 1, 0)
        second = lax.dynamic_slice_in_dim(self.other, which, 1, 0)
        return jnp.where(
            core == 0,
            jnp.concatenate([first, second], axis=0),
            jnp.concatenate([second, first], axis=0),
        )

    def advance(self, *before):
        value = self.pieces[-1]
        if before or self.paced and self.step > 1:
            value = self.pieces[-1] = hold(value, *before)
        self.pieces.append(lax.ppermute(value, "dp", self.route))
        self.swap(value)
        self.step += 1
        if self.step == self.chips:
            self.swap(self.pieces[-1])
        return self.pieces[-1]

    def swap(self, value):
        if len(self.pieces) > 2 or self.step == self.chips:
            self.others.append(lax.ppermute(value, "dp", self.pair))


class ScatterRing:
    def __init__(self, mine, theirs):
        devices = lax.axis_size("dp")
        self.chips = devices // 2
        self.route, self.pair = ring_routes(devices)
        self.mine = mine
        self.got = lax.ppermute(theirs, "dp", self.pair)
        value = mine[1].astype(jnp.float32) + self.got[1].astype(jnp.float32)
        self.value = value.astype(jnp.bfloat16)
        self.step = 1

    def advance(self, *before):
        if before:
            self.value = hold(self.value, *before)
        self.step += 1
        place = self.step % self.chips
        value = lax.ppermute(self.value, "dp", self.route).astype(jnp.float32)
        value = value + self.mine[place].astype(jnp.float32)
        value = value + self.got[place].astype(jnp.float32)
        self.value = value.astype(jnp.bfloat16) if self.step < self.chips else value
        return self.value

    def halves(self):
        core = lax.axis_index("dp") % 2
        own = lax.dynamic_index_in_dim(self.value, core, 0, keepdims=False)
        other = lax.dynamic_index_in_dim(self.value, 1 - core, 0, keepdims=False)
        other = lax.ppermute(other, "dp", self.pair)
        return jnp.where(core == 0, own, other), jnp.where(core == 0, other, own)


def beside(grad, low, pieces, rows):
    return jnp.concatenate(
        [grad[low + rows * i : low + rows * (i + 1)] for i in range(pieces)], axis=1
    )


def layout(lengths_row):
    ends = jnp.cumsum(lengths_row)
    places = jnp.arange(TOKENS_PER_SHARD, dtype=jnp.int32)
    passed = (ends[None, :] <= places[:, None]).astype(jnp.int32)
    segment_index = jnp.sum(passed, axis=1)
    start = jnp.sum(passed * lengths_row[None, :], axis=1)
    return (segment_index, places - start)


def rotary_tables(place):
    half = HEAD_SIZE // 2
    freqs = THETA ** (-(jnp.arange(half, dtype=jnp.float32) * 2.0 / HEAD_SIZE))
    angles = place.astype(jnp.float32)[:, None] * freqs[None, :]
    return (jnp.cos(angles), jnp.sin(angles))


LOCAL = pl.BlockSpec(memory_space=pltpu.VMEM)
SCALARS = pl.BlockSpec(memory_space=pltpu.SMEM)
ANYWHERE = pl.BlockSpec(memory_space=pl.ANY)


def hold(value, *after):
    return pl.pallas_call(
        lambda *refs: None,
        in_specs=[ANYWHERE] * (1 + len(after)),
        out_specs=ANYWHERE,
        out_shape=jax.ShapeDtypeStruct(value.shape, value.dtype),
        input_output_aliases={0: 0},
        cost_estimate=pl.CostEstimate(flops=HOLD_FLOPS, bytes_accessed=0, transcendentals=0),
    )(value, *after)


def flat_call(body, arguments, out_shape, scratch=(), flops=0, moved=0, vmem=VMEM_GRANT, after=()):
    specs = [SCALARS] + [LOCAL] * (len(arguments) - 1) + [ANYWHERE] * len(after)
    count = len(arguments)

    def run(*refs):
        body(*refs[:count], *refs[count + len(after) :])

    return pl.pallas_call(
        run,
        in_specs=specs,
        out_specs=[LOCAL] * len(out_shape),
        out_shape=out_shape,
        scratch_shapes=list(scratch),
        compiler_params=pltpu.CompilerParams(vmem_limit_bytes=vmem << 20),
        cost_estimate=pl.CostEstimate(
            flops=int(flops), bytes_accessed=int(moved), transcendentals=0
        ),
    )(*arguments, *after)


def low_shape(*shape):
    return jax.ShapeDtypeStruct(shape, jnp.bfloat16)


def full_shape(*shape):
    return jax.ShapeDtypeStruct(shape, jnp.float32)


def dot_plain(left, right):
    return jnp.dot(left, right, preferred_element_type=jnp.float32)


def dot_columns(left, right):
    return lax.dot_general(left, right, CONTRACT_COLS, preferred_element_type=jnp.float32)


def dot_rows(left, right):
    return lax.dot_general(left, right, CONTRACT_ROWS, preferred_element_type=jnp.float32)


def unit_rows(values):
    factor = lax.rsqrt(jnp.mean(values * values, axis=-1, keepdims=True) + EPS)
    return values * factor, factor


def norm_pull(grad, scaled, factor, gain):
    pulled = grad * gain
    return factor * (pulled - scaled * jnp.mean(pulled * scaled, axis=-1, keepdims=True))


def head_mean(values):
    average = jnp.full((HEAD_SIZE, HEAD_SIZE), 1.0 / HEAD_SIZE, jnp.bfloat16)
    return dot_plain(values.astype(jnp.bfloat16), average)


def slab(ref, low, rows):
    value = ref[:, low : low + rows, :]
    return value.reshape(value.shape[0] * rows, value.shape[2])


def part_of(index, width=HEAD_SIZE):
    return slice(index * width, (index + 1) * width)


def attention_kernel(
    keep, section_ref, h_ref, came_ref, gain_ref, gain_q_ref, gain_k_ref, gain_ffn_ref, cos_ref,
    sin_ref, row_ref, column_ref, w_ref, hm_ref, xf_ref, *rest,
):
    if keep:
        xf_t_ref, xa_t_ref, o_t_ref, qkv_ref, pre_ref, hidden_ref, o_ref = rest
    else:
        qkv_ref, o_ref = rest
    tokens, model = h_ref.shape
    rows = w_ref.shape[1] // 6
    hidden = h_ref[...]
    if keep:
        hidden = jnp.where(section_ref[0] == 0, hidden, came_ref[...])
        hidden_ref[...] = hidden
    hidden = hidden.astype(jnp.float32)
    scaled, _ = unit_rows(hidden)
    xa = (scaled * gain_ref[...]).astype(jnp.bfloat16)
    cosine, sine = cos_ref[...], sin_ref[...]
    for block, low in enumerate((0, rows, 4 * rows, 5 * rows)):
        pre = dot_plain(xa, slab(w_ref, low, rows))
        if block == 3:
            qkv_ref[:, part_of(block, model)] = pre.astype(jnp.bfloat16)
            continue
        if keep:
            pre_ref[:, part_of(block, model)] = pre.astype(jnp.bfloat16)
        gain = gain_q_ref[...] if block < 2 else gain_k_ref[...]
        for head in range(model // HEAD_SIZE):
            value = pre[:, part_of(head)]
            value = value * lax.rsqrt(head_mean(value * value) + EPS) * gain
            value = value * cosine + pltpu.roll(value, HEAD_SIZE // 2, 1) * sine
            qkv_ref[:, part_of(block * (model // HEAD_SIZE) + head)] = value.astype(jnp.bfloat16)
    causal = lax.broadcasted_iota(jnp.int32, (tokens, tokens), 0) >= lax.broadcasted_iota(
        jnp.int32, (tokens, tokens), 1
    )
    allowed = (row_ref[...] == column_ref[0]) & causal
    ones = jnp.ones((tokens, HEAD_SIZE), jnp.bfloat16)
    for shared in range(KEY_VALUE_HEADS):
        key = qkv_ref[:, part_of(QUERY_HEADS + shared)]
        value = qkv_ref[:, part_of(QUERY_HEADS + KEY_VALUE_HEADS + shared)]
        value = jnp.concatenate([value, ones], axis=1)
        for head in range(2 * shared, 2 * shared + 2):
            scores = dot_columns(qkv_ref[:, part_of(head)], key) * HEAD_SIZE ** (-0.5)
            raised = jnp.where(allowed, jnp.exp(scores), 0.0).astype(jnp.bfloat16)
            mixed = dot_plain(raised, value)
            mixed = mixed[:, :HEAD_SIZE] / mixed[:, HEAD_SIZE:]
            o_ref[:, part_of(head)] = mixed.astype(jnp.bfloat16)
    middle = hidden + dot_plain(o_ref[...], slab(w_ref, 2 * rows, 2 * rows))
    hm_ref[...] = middle
    scaled, _ = unit_rows(middle)
    xf = (scaled * gain_ffn_ref[...]).astype(jnp.bfloat16)
    xf_ref[...] = xf
    if keep:
        xf_t_ref[...] = jnp.transpose(xf)
        xa_t_ref[...] = jnp.transpose(xa)
        o_t_ref[...] = jnp.transpose(o_ref[...])


def attention(section, hidden, came, gains, tables, whole, keep):
    tokens, model = hidden.shape
    wide = QUERY_HEADS * HEAD_SIZE
    shapes = [full_shape(tokens, model), low_shape(tokens, model)]
    scratch = [pltpu.VMEM((tokens, wide), jnp.bfloat16)]
    if keep:
        shapes += [
            low_shape(model, tokens),
            low_shape(model, tokens),
            low_shape(wide, tokens),
            low_shape(tokens, 4 * model),
            low_shape(tokens, 3 * model),
            low_shape(tokens, model),
        ]
    else:
        scratch = [pltpu.VMEM((tokens, 4 * model), jnp.bfloat16)] + scratch
    return flat_call(
        functools.partial(attention_kernel, keep),
        (section, hidden, came, *gains, *tables, whole),
        shapes,
        scratch=scratch,
        flops=2 * tokens * model * 6 * model + 8 * tokens * tokens * wide,
        moved=12 * model * model + 20 * tokens * model,
    )


def ffn_kernel(keep, _, xf_ref, hm_ref, w_ref, *rest):
    if keep:
        teacher_ref, keep_ref, y_ref, g_ref, u_ref, z_t_ref, pull_ref, square_ref, inner = rest
    else:
        y_ref, inner = rest
    tokens, model = xf_ref.shape
    rows = w_ref.shape[1] // 9
    xf = xf_ref[...]
    for block in range(3):
        gate = dot_plain(xf, slab(w_ref, block * rows, rows))
        up = dot_plain(xf, slab(w_ref, (6 + block) * rows, rows))
        mixed = (gate * jax.nn.sigmoid(gate) * up).astype(jnp.bfloat16)
        inner[:, part_of(block, model)] = mixed
        if keep:
            g_ref[:, part_of(block, model)] = gate.astype(jnp.bfloat16)
            u_ref[:, part_of(block, model)] = up.astype(jnp.bfloat16)
            z_t_ref[part_of(block, model), :] = jnp.transpose(mixed)
    total = hm_ref[...] + dot_plain(inner[...], slab(w_ref, 3 * rows, 3 * rows))
    low = total.astype(jnp.bfloat16)
    y_ref[...] = low
    if keep:
        error = low.astype(jnp.float32) - teacher_ref[...]
        pull = keep_ref[...] * error
        pull_ref[...] = pull
        square_ref[...] = jnp.sum(jnp.sum(pull * error, axis=0, keepdims=True), axis=1, keepdims=True)


def feed_forward(section, normed, middle, whole, target=()):
    tokens, model = normed.shape
    width = 3 * model
    shapes = [low_shape(tokens, model)]
    if target:
        shapes += [low_shape(tokens, width), low_shape(tokens, width), low_shape(width, tokens)]
        shapes += [full_shape(tokens, model), full_shape(1, 1)]
    return flat_call(
        functools.partial(ffn_kernel, bool(target)),
        (section, normed, middle, whole, *target),
        shapes,
        scratch=[pltpu.VMEM((tokens, width), jnp.bfloat16)],
        flops=6 * tokens * width * model,
        moved=6 * width * model + 8 * tokens * model,
    )


def ffn_back_kernel(
    section_ref, dy_ref, came_ref, hm_ref, gain_ref, g_ref, u_ref, w_ref, dh_ref, low_ref, dg_ref,
    du_ref, dgain_ref, low_dy_ref,
):
    devices, rows, model = w_ref.shape
    rows = rows // 9
    d_result = jnp.where(section_ref[0] == 1, dy_ref[...], came_ref[...].astype(jnp.float32))
    low_dy = d_result.astype(jnp.bfloat16)
    low_dy_ref[...] = low_dy
    chunks = 4
    owners = devices // chunks
    chunk = 3 * model // chunks
    for block in range(chunks):
        part = part_of(block, chunk)
        down = w_ref[block * owners : (block + 1) * owners, 3 * rows : 6 * rows, :]
        d_inner = dot_columns(low_dy, down.reshape(chunk, model))
        gate = g_ref[:, part].astype(jnp.float32)
        sigma = jax.nn.sigmoid(gate)
        silu = gate * sigma
        d_gate = d_inner * u_ref[:, part].astype(jnp.float32) * (sigma + silu * (1.0 - sigma))
        dg_ref[:, part] = d_gate.astype(jnp.bfloat16)
        du_ref[:, part] = (d_inner * silu).astype(jnp.bfloat16)
    grad = None
    for block in range(3):
        part = part_of(block, model)
        term = dot_columns(dg_ref[:, part], slab(w_ref, block * rows, rows))
        term = term + dot_columns(du_ref[:, part], slab(w_ref, (6 + block) * rows, rows))
        grad = term if grad is None else grad + term
    scaled, factor = unit_rows(hm_ref[...])
    dgain_ref[...] = jnp.sum(grad * scaled, axis=0, keepdims=True)
    d_result = jnp.where(section_ref[0] == 1, dy_ref[...], came_ref[...].astype(jnp.float32))
    d_hidden = d_result + norm_pull(grad, scaled, factor, gain_ref[...])
    dh_ref[...] = d_hidden
    low_ref[...] = d_hidden.astype(jnp.bfloat16)


def feed_forward_back(section, pull, came, middle, gains, gate, up, whole):
    tokens, model = middle.shape
    width = 3 * model
    return flat_call(
        ffn_back_kernel,
        (section, pull, came, middle, gains[3], gate, up, whole),
        [
            full_shape(tokens, model),
            low_shape(tokens, model),
            low_shape(tokens, width),
            low_shape(tokens, width),
            full_shape(1, model),
            low_shape(tokens, model),
        ],
        flops=6 * tokens * width * model,
        moved=6 * width * model + 14 * tokens * model + 8 * tokens * width,
    )


def attention_back_kernel(
    _, low_ref, dh_ref, h_ref, qkv_ref, pre_ref, gain_ref, gain_q_ref, gain_k_ref, cos_ref, sin_ref,
    row_ref, column_ref, w_ref, dq_ref, dkv_ref, dx_ref, dgain_ref, dgain_q_ref,
    dgain_k_ref, do_ref,
):
    tokens, model = h_ref.shape
    rows = w_ref.shape[1] // 6
    do_ref[...] = dot_columns(low_ref[...], slab(w_ref, 2 * rows, 2 * rows)).astype(jnp.bfloat16)
    causal = lax.broadcasted_iota(jnp.int32, (tokens, tokens), 0) <= lax.broadcasted_iota(
        jnp.int32, (tokens, tokens), 1
    )
    allowed = (row_ref[...] == column_ref[0]) & causal
    cosine, sine = cos_ref[...], sin_ref[...]
    scale = HEAD_SIZE ** (-0.5)
    gain_grads = [jnp.zeros((1, HEAD_SIZE), jnp.float32)] * 2

    def through_norm(grad, pre, gain_ref, which):
        gain = gain_ref[...]
        grad = grad * cosine - pltpu.roll(grad, HEAD_SIZE // 2, 1) * sine
        pre = pre.astype(jnp.float32)
        factor = lax.rsqrt(head_mean(pre * pre) + EPS)
        scaled = pre * factor
        gain_grads[which] = gain_grads[which] + jnp.sum(grad * scaled, axis=0, keepdims=True)
        pulled = grad * gain
        return (factor * (pulled - scaled * head_mean(pulled * scaled))).astype(jnp.bfloat16)

    for shared in range(KEY_VALUE_HEADS):
        lone = part_of(shared)
        key = qkv_ref[:, part_of(QUERY_HEADS + shared)]
        value = qkv_ref[:, part_of(QUERY_HEADS + KEY_VALUE_HEADS + shared)]
        d_key = d_value = None
        for head in range(2 * shared, 2 * shared + 2):
            part = part_of(head)
            query, d_mixed = qkv_ref[:, part], do_ref[:, part]
            scores = dot_columns(key, query) * scale
            raised = jnp.where(allowed, jnp.exp(scores), 0.0)
            weights = raised * (1.0 / jnp.sum(raised, axis=0, keepdims=True))
            value_term = dot_plain(weights.astype(jnp.bfloat16), d_mixed)
            d_weights = dot_columns(value, d_mixed)
            pulled = jnp.sum(d_weights * weights, axis=0, keepdims=True)
            d_scores = (weights * (d_weights - pulled)).astype(jnp.bfloat16)
            d_query = dot_rows(d_scores, key) * scale
            key_term = dot_plain(d_scores, query)
            d_key = key_term if d_key is None else d_key + key_term
            d_value = value_term if d_value is None else d_value + value_term
            dq_ref[:, part] = through_norm(d_query, pre_ref[:, part], gain_q_ref, 0)
        dkv_ref[:, lone] = through_norm(
            d_key * scale, pre_ref[:, part_of(QUERY_HEADS + shared)], gain_k_ref, 1
        )
        dkv_ref[:, part_of(KEY_VALUE_HEADS + shared)] = d_value.astype(jnp.bfloat16)
    dgain_q_ref[...], dgain_k_ref[...] = gain_grads
    grad = dot_columns(dq_ref[:, part_of(0, model)], slab(w_ref, 0, rows))
    grad = grad + dot_columns(dq_ref[:, part_of(1, model)], slab(w_ref, rows, rows))
    grad = grad + dot_columns(dkv_ref[:, part_of(0, model)], slab(w_ref, 4 * rows, rows))
    grad = grad + dot_columns(dkv_ref[:, part_of(1, model)], slab(w_ref, 5 * rows, rows))
    scaled, factor = unit_rows(h_ref[...].astype(jnp.float32))
    dgain_ref[...] = jnp.sum(grad * scaled, axis=0, keepdims=True)
    d_hidden = dh_ref[...] + norm_pull(grad, scaled, factor, gain_ref[...])
    dx_ref[...] = d_hidden.astype(jnp.bfloat16)


def attention_back(section, low, d_middle, hidden, qkv, pre, gains, tables, whole, after=()):
    tokens, model = hidden.shape
    wide = QUERY_HEADS * HEAD_SIZE
    return flat_call(
        attention_back_kernel,
        (section, low, d_middle, hidden, qkv, pre, *gains[:3], *tables, whole),
        [
            low_shape(tokens, wide),
            low_shape(tokens, 2 * model),
            low_shape(tokens, model),
            full_shape(1, model),
            full_shape(1, HEAD_SIZE),
            full_shape(1, HEAD_SIZE),
        ],
        scratch=[pltpu.VMEM((tokens, wide), jnp.bfloat16)],
        flops=2 * tokens * model * 6 * model + 20 * tokens * tokens * wide,
        moved=12 * model * model + 40 * tokens * model,
        after=after,
    )


def grad_kernel(plan, chips, batches, order_ref, *refs):
    count = sum(1 + len(entry[5]) for entry in plan) * batches
    targets, stores = refs[count : count + 2], refs[count + 2 :]
    model = targets[0].shape[3]
    for target, base in ((targets[0], 0), (targets[1], chips + 1)):
        side = order_ref[base + chips]
        taken, start = 0, 0
        for (rows, size, low, least, blocks, choices), store in zip(plan, stores):
            left = refs[taken : taken + batches]
            taken += batches
            rights = []
            for _ in choices:
                rights.append(refs[taken : taken + batches])
                taken += batches
            first = least + side * low
            for t in range(chips):
                owner = 2 * order_ref[base + t]
                for core in range(2):
                    place = pl.multiple_of((owner + core) * rows + first, 16)
                    to = slice((2 * t + core) * size, (2 * t + core + 1) * size)
                    for batch in range(batches):
                        store[batch, to, :] = left[batch][pl.ds(place, size), :]
            for block in range(blocks):
                part = part_of(block, model)
                right = []
                for batch in range(batches):
                    value = rights[0][batch][:, part]
                    if len(rights) > 1:
                        value = jnp.where(side == 0, value, rights[1][batch][:, part])
                    right.append(value)
                for half in range(2):
                    value = None
                    span = slice(half * chips * size, (half + 1) * chips * size)
                    for batch in range(batches):
                        term = dot_plain(store[batch, span, :], right[batch])
                        value = term if value is None else value + term
                    value = value.astype(jnp.bfloat16).reshape(chips // 2, 2, size, model)
                    into = slice(start + block * size, start + (block + 1) * size)
                    target[half * chips // 2 : (half + 1) * chips // 2, :, into, :] = value
            start += blocks * size


def weight_grads(orders, parts, model, after=()):
    batches = len(parts[0][0])
    tokens = parts[0][0][0].shape[1]
    chips = orders.shape[0] // 2 - 1
    plan, scratch, operands, total = [], [], [], 0
    for left, rights, size, low, least in parts:
        rows = left[0].shape[0] // (2 * chips)
        blocks = rights[0][0].shape[1] // model
        plan.append((rows, size, low, least, blocks, tuple(range(len(rights)))))
        scratch.append(pltpu.VMEM((batches, 2 * chips * size, tokens), jnp.bfloat16))
        operands += list(left) + [array for right in rights for array in right]
        total += size * blocks
    shape = low_shape(chips, 2, total, model)
    return flat_call(
        functools.partial(grad_kernel, tuple(plan), chips, batches),
        (orders, *operands),
        [shape, shape],
        scratch=scratch,
        flops=8 * chips * total * model * tokens * batches,
        moved=8 * chips * total * model + 8 * tokens * batches * model,
        vmem=14,
        after=after,
    )


def pack_kernel(plan, *refs):
    target, sem = refs[-2:]
    model = target.shape[2]
    copies = []
    for half, entries in enumerate(plan):
        low = 0
        for source, start, rows, block in entries:
            copies.append(
                pltpu.make_async_copy(
                    refs[source].at[start : start + rows, part_of(block, model)],
                    target.at[half, low : low + rows, :],
                    sem.at[len(copies)],
                )
            )
            low += rows
    for copy in copies:
        copy.start()
    for copy in copies:
        copy.wait()


def pack(shards, plan, model, after=()):
    rows = sum(entry[2] for entry in plan[0])
    return pl.pallas_call(
        functools.partial(pack_kernel, plan),
        in_specs=[ANYWHERE] * (len(shards) + len(after)),
        out_specs=LOCAL,
        out_shape=low_shape(2, rows, model),
        scratch_shapes=[pltpu.SemaphoreType.DMA((len(plan[0]) + len(plan[1]),))],
        compiler_params=pltpu.CompilerParams(vmem_limit_bytes=VMEM_GRANT << 20),
    )(*shards, *after)


def assemble_kernel(chips, plan, order_ref, *refs):
    target, sem = refs[-2:]
    copies = []
    for group, (low, rows, start, further) in enumerate(plan):
        for turn in range(2):
            base = turn * (chips + 1)
            place = pl.multiple_of(start + order_ref[base + chips] * further, 16)
            for t in range(chips):
                piece = refs[(2 * group + turn) * chips + t]
                copies.append(
                    pltpu.make_async_copy(
                        piece.at[:, low : low + rows, :],
                        target.at[pl.ds(2 * order_ref[base + t], 2), pl.ds(place, rows), :],
                        sem.at[len(copies)],
                    )
                )
    for copy in copies:
        copy.start()
    for copy in copies:
        copy.wait()


def assemble(orders, sources, rows):
    chips = sources[0][0].chips
    pieces = [piece for source in sources for piece in source[0].pieces + source[0].others]
    model = pieces[0].shape[2]
    return pl.pallas_call(
        functools.partial(assemble_kernel, chips, tuple(source[1:] for source in sources)),
        in_specs=[SCALARS] + [ANYWHERE] * len(pieces),
        out_specs=LOCAL,
        out_shape=low_shape(2 * chips, rows, model),
        scratch_shapes=[pltpu.SemaphoreType.DMA((len(pieces),))],
        compiler_params=pltpu.CompilerParams(vmem_limit_bytes=VMEM_GRANT << 20),
        cost_estimate=pl.CostEstimate(
            flops=0, bytes_accessed=8 * chips * rows * model, transcendentals=0
        ),
    )(orders, *pieces)


def local(
    inputs,
    teacher,
    lengths,
    attn_query,
    attn_key,
    attn_value,
    attn_out,
    ffn_gate,
    ffn_up,
    ffn_down,
    norm_attn,
    norm_ffn,
    norm_query,
    norm_key,
):
    section = lax.axis_index("section")
    index = lax.axis_index("dp")
    devices = lax.axis_size("dp")
    chips = devices // 2
    batches, _, model = inputs.shape
    slots = lengths.shape[2]
    rows = attn_query.shape[1]
    forward_rows = ffn_down.shape[1]

    cut = forward_rows // 2 if forward_rows % 32 == 0 else 2 * rows
    core = index % 2
    place = ring_place(index // 2, chips)
    away = jnp.arange(chips, dtype=jnp.int32) * (2 * core - 1)
    order = jnp.concatenate([chip_at(place + away, chips), core[None]]).astype(jnp.int32)
    other_order = jnp.concatenate([chip_at(place - away, chips), 1 - core[None]]).astype(jnp.int32)
    orders = jnp.concatenate([order, other_order])
    gain_sizes = (norm_attn.shape[1], norm_query.shape[1], norm_key.shape[1], norm_ffn.shape[1])
    gain_shard = jnp.concatenate([norm_attn, norm_query, norm_key, norm_ffn], axis=1)
    gain_count = gain_shard.shape[1]
    gain_shard = jnp.pad(gain_shard, ((0, GAIN_ROWS - 1), (0, model - gain_count)))
    moved = cut // 2
    attn_packed = pack(
        (attn_query[0], attn_out[0], attn_key[0], attn_value[0], gain_shard),
        (
            ((0, 0, rows, 0), (0, 0, rows, 1), (1, 0, rows, 0), (4, 0, GAIN_ROWS, 0)),
            ((1, rows, rows, 0), (2, 0, rows, 0), (3, 0, rows, 0), (4, 0, GAIN_ROWS, 0)),
        ),
        model,
    )
    ffn_packed = pack(
        (ffn_gate[0], ffn_down[0], ffn_up[0]),
        (
            ((0, 0, rows, 0), (0, 0, rows, 1), (0, 0, rows, 2), (1, 0, cut, 0)),
            (
                (1, forward_rows - cut, cut, 0),
                (2, 0, rows, 0),
                (2, 0, rows, 1),
                (2, 0, rows, 2),
            ),
        ),
        model,
    )
    segments, places = jax.vmap(layout)(lengths[:, 0, :])
    keep = (segments < slots - 1).astype(jnp.float32)
    tables = []
    for batch in range(batches):
        cosine_table, sine_table = rotary_tables(places[batch])
        tables.append(
            (
                jnp.concatenate([cosine_table, cosine_table], axis=1),
                jnp.concatenate([-sine_table, sine_table], axis=1),
                segments[batch].reshape(TOKENS_PER_SHARD, 1),
                segments[batch].reshape(1, 1, TOKENS_PER_SHARD),
            )
        )
    keep_columns = [keep[batch][:, None] for batch in range(batches)]
    first = [inputs[batch] for batch in range(batches)]
    target = [teacher[batch] for batch in range(batches)]
    early = [array for table in tables for array in table] + keep_columns + first + target + [orders]
    attn_ring = GatherRing(attn_packed, True)
    ffn_ring = GatherRing(ffn_packed)
    attn_ring.advance()
    ffn_ring.advance()
    attn_ring.advance(*early)
    ffn_ring.advance(attn_ring.others[0], ffn_ring.others[0])
    while ffn_ring.step < chips:
        attn_ring.advance()
        ffn_ring.advance()
    carried_gains = jnp.stack([piece[:, 3 * rows, :gain_count] for piece in attn_ring.pieces])
    chip = jnp.arange(chips, dtype=jnp.int32)
    found = lax.rem((2 * core - 1) * (ring_place(chip, chips) - place) + chips, chips)
    gain_whole = jnp.take(carried_gains, found, axis=0).reshape(devices, gain_count)
    gain_whole = gain_whole.astype(jnp.float32)
    gains, low = [], 0
    for size in gain_sizes:
        gains.append(gain_whole[:, low : low + size].reshape(1, devices * size))
        low += size

    half = 3 * rows + cut
    ffn_low = 9 * rows - half
    attn_whole = assemble(orders, [(attn_ring, 0, 3 * rows, 0, 3 * rows)], 6 * rows)
    ffn_whole = assemble(orders, [(ffn_ring, 0, half, 0, ffn_low)], 9 * rows)
    both = range(batches)

    where = section[None].astype(jnp.int32)
    last = jnp.ones((1,), jnp.int32)
    carried, seen = [], []
    for batch in both:
        seen.append(attention(where, first[batch], first[batch], gains, tables[batch], attn_whole, False))
    for batch in both:
        (result,) = feed_forward(where, seen[batch][1], seen[batch][0], ffn_whole)
        carried.append(one_way(result, 0))

    kept = []
    for batch in both:
        mid, norm, norm_t, normalized_t, mix_t, qkv, pre, hidden = attention(
            where, first[batch], carried[batch], gains, tables[batch], attn_whole, True
        )
        result, gate, up, inner_t, pull, square = feed_forward(
            where, norm, mid, ffn_whole, (target[batch], keep_columns[batch])
        )
        kept.append(
            (hidden, normalized_t, qkv, pre, mix_t, mid, norm_t, result, gate, up, inner_t, pull, square)
        )
    (
        hidden, normalized_t, qkv, pre, mixed_t, middle, normed_t, result, gate, up, inner_t, pull,
        squares,
    ) = (list(column) for column in zip(*kept))

    incoming = []
    for batch in both:
        d_middle, d_attn = feed_forward_back(
            last, pull[batch], result[batch], middle[batch], gains, gate[batch], up[batch], ffn_whole
        )[:2]
        d_hidden = attention_back(
            where, d_attn, d_middle, hidden[batch], qkv[batch], pre[batch], gains, tables[batch],
            attn_whole,
        )[2]
        incoming.append(one_way(d_hidden, 1))

    d_middle, d_attn, d_gate, d_up, d_branch, gain_ffn = [], [], [], [], [], 0.0
    for batch in both:
        m, a, g, u, gain, low = feed_forward_back(
            where, pull[batch], incoming[batch], middle[batch], gains, gate[batch], up[batch],
            ffn_whole,
        )
        d_branch.append(low)
        d_middle.append(m)
        d_attn.append(a)
        d_gate.append(g)
        d_up.append(u)
        gain_ffn = gain_ffn + gain
    ffn_parts = [
        (normed_t, (d_gate, d_up), rows, 0, 0),
        (inner_t, (d_branch,), cut - moved, forward_rows - cut + moved, 0),
    ]
    their_orders = jnp.concatenate([other_order, order])
    d_query, d_pair, d_hidden = [], [], []
    gain_attn, gain_query, gain_key = 0.0, 0.0, 0.0
    for batch in both:
        if batch + 1 == batches:
            theirs, mine = weight_grads(their_orders, ffn_parts, model, tuple(d_query))
            ffn_ring = ScatterRing(mine, theirs)
        q, kv, x, gain_a, gain_q, gain_k = attention_back(
            where, d_attn[batch], d_middle[batch], hidden[batch], qkv[batch], pre[batch], gains,
            tables[batch], attn_whole, (mine,) if batch + 1 == batches else (),
        )
        d_query.append(q)
        d_pair.append(kv)
        d_hidden.append(x)
        gain_attn = gain_attn + gain_a
        gain_query = gain_query + gain_q
        gain_key = gain_key + gain_k
    gain_grads = (gain_attn, gain_query, gain_key, gain_ffn)
    attn_parts = [
        (normalized_t, (d_query, d_pair), rows, 0, 0),
        (mixed_t, (d_attn,), rows, rows, 0),
        (inner_t, (d_branch,), moved, forward_rows - 2 * cut + moved, cut - moved),
    ]
    theirs, mine = weight_grads(their_orders, attn_parts, model, (ffn_ring.value,))
    attn_ring = ScatterRing(mine, theirs)
    small = jnp.concatenate([*gain_grads, sum(squares), jnp.sum(keep).reshape(1, 1)], axis=1)
    small_rounds = cycles(small)
    got, _ = next(small_rounds)
    waits = []
    while ffn_ring.step < chips:
        ffn_ring.advance()
        attn_ring.advance(*waits)
        waits = []
        if ffn_ring.step % 2 == 1 and got is not None:
            small = sum(got)
            waits = [small]
            try:
                got, _ = small_rounds.send(small)
            except StopIteration:
                got = None
    while got is not None:
        small = sum(got)
        try:
            got, _ = small_rounds.send(small)
        except StopIteration:
            got = None

    ffn_first, ffn_second = ffn_ring.halves()
    attn_first, attn_second = attn_ring.halves()
    grad_gate = beside(ffn_first, 0, 3, rows)
    grad_up = beside(ffn_second, 0, 3, rows)
    grad_query = beside(attn_first, 0, 2, rows)
    grad_key, grad_value = attn_second[:rows], attn_second[rows : 2 * rows]
    grad_out = jnp.concatenate(
        [attn_first[2 * rows : 3 * rows], attn_second[2 * rows : 3 * rows]], axis=0
    )
    again = 3 * rows + max(0, 2 * cut - forward_rows)
    grad_down = jnp.concatenate(
        [ffn_first[3 * rows :], attn_first[3 * rows :], attn_second[again:], ffn_second[3 * rows :]],
        axis=0,
    )
    small_sum = small
    totals = small_sum[:, -2:]
    totals = jnp.where(section == 1, totals, one_way(totals, 1))[0]
    loss = totals[0] / (totals[1] * model)
    gain_grads, low = [], 0
    for size in gain_sizes:
        gain_grads.append(lax.dynamic_slice(small_sum, (0, low + index * size), (1, size)))
        low += devices * size
    grad_gain_attn, grad_gain_query, grad_gain_key, grad_gain_ffn = gain_grads

    half = batches // 2
    finals = jnp.stack(result)
    grads = jnp.stack(d_hidden)
    output = jnp.where(section == 0, one_way(finals[:half], 1), finals[half:])
    input_grad = jnp.where(section == 0, grads[:half], one_way(grads[half:], 0))
    return (
        output,
        loss,
        input_grad,
        grad_query[None],
        grad_key[None],
        grad_value[None],
        grad_out[None],
        grad_gate[None],
        grad_up[None],
        grad_down[None],
        grad_gain_attn,
        grad_gain_ffn,
        grad_gain_query,
        grad_gain_key,
    )


def solution(mesh):
    placed = (
        P(None, "dp", None),
        P(None, "dp", None),
        P(None, "dp", None),
        P("section", "dp", None),
        P("section", "dp", None),
        P("section", "dp", None),
        P("section", "dp", None),
        P("section", "dp", None),
        P("section", "dp", None),
        P("section", "dp", None),
        P("section", "dp"),
        P("section", "dp"),
        P("section", "dp"),
        P("section", "dp"),
    )
    return jax.shard_map(
        local,
        mesh=mesh,
        in_specs=placed,
        out_specs=(
            P("section", "dp", None),
            P(),
            P("section", "dp", None),
            P("section", "dp", None),
            P("section", "dp", None),
            P("section", "dp", None),
            P("section", "dp", None),
            P("section", "dp", None),
            P("section", "dp", None),
            P("section", "dp", None),
            P("section", "dp"),
            P("section", "dp"),
            P("section", "dp"),
            P("section", "dp"),
        ),
        check_vma=False,
    )
```
